512 devices in a mesh: tm: 64 (over z_lo, y, core), col: 8 (over z_hi, x).
Axes of the slice: x: 4, y: 4, z: 16 (z_hi: 2, z_lo: 8; z = z_hi * 8 + z_lo), core: 2. Of those that a mesh axis runs over, the one named last changes fastest.
Arguments:
- u_vel: float32 [4, 1024, 8, 1024], P(None, 'tm', None, 'col'), may hold values from -48 to 48
- v_vel: float32 [4, 1024, 8, 1024], P(None, 'tm', None, 'col'), may hold values from -48 to 48
- density: float32 [4, 1024, 8, 1024], P(None, 'tm', None, 'col'), may hold values from -48 to 48
- land_mask: int32 [8, 1024], P(None, 'col'), may hold values 0 or 1
- start_hour: int32 [8, 1024], P(None, 'col'), may hold values from 0 to 255
- levels: int32 [4], replicated, may hold values from 0 to 89, as said below
Outputs:
- pressure: float32 [4, 1024, 8, 1024], P(None, 'tm', None, 'col')
- flux_div: float32 [4, 1024, 8, 1024], P(None, 'tm', None, 'col')
The draws below stay inside these ranges and needn't reach their ends.
Inputs may be any that keep to these rules, and one draw needn't show every extreme that they name: `levels`: strictly increasing; the first is 0 and the last is 89.
All inputs are finite; a program needn't handle non-finite values. No bound on the sum of `land_mask` on one device may be relied on, other than what follows from the above.
Results may differ from the reference program's by a relative error of at most 0.0003.
Values sent between devices are 32-bit elements; how exact they have to be, the bound alone decides.
No kernel may reach another device: no remote copies, remote signals or barrier semaphores. Data moves between devices by JAX's collectives and lax.ppermute only.
A program may use at most 64 MiB of HBM per device.

```python
import math
import jax
import jax.numpy as jnp
import numpy as np
from jax import lax

LEV = 4
NY = 8
TIME = 1024
NX = 1024


def draw_levels(key, part):
    key = jax.random.fold_in(key, 7)
    inner = jax.random.permutation(key, 88)[:LEV - 2] + 1
    inner = jnp.sort(inner).astype(jnp.int32)
    return jnp.concatenate([jnp.zeros((1,), jnp.int32), inner, jnp.full((1,), 89, jnp.int32)])


def set_ends(drawn, own_key, least, top_value):
    longest = drawn.shape.index(max(drawn.shape))
    spots = []
    for shift in (0, 1):
        where = [jax.random.randint(jax.random.fold_in(own_key, axis), (), 0, length) for axis, length in enumerate(drawn.shape)]
        where[longest] = (where[longest] + shift) % drawn.shape[longest]
        spots.append(tuple(where))
    return drawn.at[spots[0]].set(least).at[spots[1]].set(top_value)


def steps_of(key, dims, split, least, high):
    level = 1.0
    for axis_at, shards_of in split:
        draws = jax.random.uniform(jax.random.fold_in(jax.random.fold_in(key, 6), axis_at), (shards_of,), jnp.float32, least / len(split), high / len(split))
        level = level * jnp.repeat(jnp.exp(draws), dims[axis_at] // shards_of).reshape((-1,) + (1,) * (len(dims) - 1 - axis_at))
    return level


def noise(own_key, shape, scale, reach, cuts=(), kind=jnp.bfloat16):
    array = jax.random.normal(own_key, shape, jnp.float32) * scale
    if len(cuts) > 0:
        array = steps_of(own_key, shape, cuts, -0.22, 0.18) * array
    return jnp.clip(array, min=-reach, max=reach).astype(kind)


def setup_inputs(seed: int = 0) -> dict:
    arg_keys = jax.random.split(jax.random.key(seed), 7)
    u_vel = noise(arg_keys[0], (LEV, TIME, NY, NX), 8.0, 48.0, ((1, 64), (3, 8)), jnp.float32)
    v_vel = noise(arg_keys[1], (LEV, TIME, NY, NX), 8.0, 48.0, ((1, 64), (3, 8)), jnp.float32)
    density = noise(arg_keys[2], (LEV, TIME, NY, NX), 8.0, 48.0, ((1, 64), (3, 8)), jnp.float32)
    land_mask = set_ends((jax.random.randint(arg_keys[3], (NY, NX), 0, 4) < 3).astype(jnp.int32), jax.random.fold_in(arg_keys[3], 1), 0, 1)
    start_hour = set_ends(jax.random.randint(arg_keys[4], (NY, NX), 0, TIME // 4), jax.random.fold_in(arg_keys[4], 1), 0, (TIME // 4) - 1).astype(jnp.int32)
    levels = draw_levels(jax.random.fold_in(arg_keys[6], 71), 0)
    return {"u_vel": u_vel, "v_vel": v_vel, "density": density, "land_mask": land_mask, "start_hour": start_hour, "levels": levels}


def expand_roots(roots):
    coefficients = [complex(1.0, 0.0)]
    for root in roots:
        widened = coefficients + [complex(0.0, 0.0)]
        for position in range(1, len(widened)):
            widened[position] = widened[position] - root * coefficients[position - 1]
        coefficients = widened
    return [coefficient.real for coefficient in coefficients]

def horner_value(coefficients, point):
    running = complex(0.0, 0.0)
    for coefficient in coefficients:
        running = running * point + coefficient
    return running

def derive_coeffs(coefficients):
    degree = len(coefficients) - 1
    return [coefficients[position] * (degree - position) for position in range(degree)]

def filter_design():
    low_edge = 1.0 / 12.9
    high_edge = 1.0 / 12.0
    warped_low = 2.0 * math.tan(math.pi * low_edge)
    warped_high = 2.0 * math.tan(math.pi * high_edge)
    centre = math.sqrt(warped_low * warped_high)
    spread = warped_high - warped_low
    digital = []
    for octant in (3, 5):
        proto = complex(math.cos(octant * math.pi / 4.0), math.sin(octant * math.pi / 4.0)) * spread
        radical = (proto * proto - 4.0 * centre * centre) ** 0.5
        for analog in ((proto + radical) / 2.0, (proto - radical) / 2.0):
            digital.append((2.0 + analog) / (2.0 - analog))
    denom = expand_roots(digital)
    numer = [1.0, 0.0, -2.0, 0.0, 1.0]
    omega = 2.0 * math.atan(centre / 2.0)
    zcentre = complex(math.cos(omega), math.sin(omega))
    respond = horner_value(numer, zcentre) / horner_value(denom, zcentre)
    numer = [coefficient / abs(respond) for coefficient in numer]
    remain = [numer[position] - numer[0] * denom[position] for position in range(1, 5)]
    slope = derive_coeffs(denom)
    amat = np.zeros((4, 4))
    bvec = np.zeros(4)
    cvec = np.zeros(4)
    upper = [pole for pole in digital if pole.imag > 0]
    for index, pole in enumerate(upper):
        resid = horner_value(remain, pole) / horner_value(slope, pole)
        first = 2 * index
        amat[first, first] = pole.real
        amat[first, first + 1] = -pole.imag
        amat[first + 1, first] = pole.imag
        amat[first + 1, first + 1] = pole.real
        bvec[first] = 1.0
        cvec[first] = 2.0 * resid.real
        cvec[first + 1] = -2.0 * resid.imag
    return (amat, bvec, cvec, float(numer[0]))

def run_filter(series):
    amat, bvec, cvec, direct = filter_design()
    amat = jnp.asarray(amat, jnp.float32)
    bvec = jnp.asarray(bvec, jnp.float32)
    cvec = jnp.asarray(cvec, jnp.float32)

    def advance(state, sample):
        output = jnp.einsum('j,j...->...', cvec, state, precision=lax.Precision.HIGHEST) + direct * sample
        shaped = bvec.reshape((4,) + (1,) * sample.ndim)
        state = jnp.einsum('ij,j...->i...', amat, state, precision=lax.Precision.HIGHEST) + shaped * sample[None]
        return (state, output)
    start = jnp.zeros((4,) + series.shape[1:], jnp.float32)
    return lax.scan(advance, start, series)[1]

def baroclinic(banded, levels):
    level_float = levels.astype(jnp.float32)
    depth = (level_float + level_float * level_float / 90.0) / 90.0
    rho = banded[2]
    press = [rho[0] * depth[0]]
    for level in range(1, rho.shape[0]):
        press.append(press[-1] + 0.5 * (rho[level - 1] + rho[level]) * (depth[level] - depth[level - 1]))
    press = jnp.stack(press)
    press = press - lax.optimization_barrier(jnp.mean(press, axis=0, keepdims=True))
    east = banded[0] - lax.optimization_barrier(jnp.mean(banded[0], axis=0, keepdims=True))
    north = banded[1] - lax.optimization_barrier(jnp.mean(banded[1], axis=0, keepdims=True))
    return jnp.stack([east, north, press])

def reference(u_vel, v_vel, density, land_mask, start_hour, levels):
    hours = jnp.arange(TIME, dtype=jnp.int32)[:, None, None]
    live = ((hours >= start_hour[None]) & (land_mask[None] == 1)).astype(jnp.float32)
    fields = jnp.stack([u_vel, v_vel, density]) * live[None, None]
    series = jnp.moveaxis(fields, 2, 0)
    forward = run_filter(series)
    banded = run_filter(forward[::-1])[::-1]
    banded = jnp.moveaxis(banded, 0, 2)
    derived = baroclinic(banded, levels)
    pressure = derived[2]
    east_flux = derived[0] * pressure
    north_flux = derived[1] * pressure
    padded_x = jnp.pad(east_flux, ((0, 0), (0, 0), (0, 0), (1, 1)))
    padded_y = jnp.pad(north_flux, ((0, 0), (0, 0), (1, 1), (0, 0)))
    spread = 0.5 * (padded_x[..., 2:] - padded_x[..., :-2]) + 0.5 * (padded_y[:, :, 2:, :] - padded_y[:, :, :-2, :])
    flux_div = spread * land_mask.astype(jnp.float32)[None, None]
    return (pressure, flux_div)
```

```python
import functools
import math

import jax
import jax.numpy as jnp
import numpy as np
from jax import lax
from jax.experimental import pallas as pl
from jax.experimental.pallas import tpu as pltpu
from jax.sharding import PartitionSpec as P

HOURS = 16
GROUP = 8
RUNS = 8
SERIES = 9
PAIRS = 5
ROWS = 8
LANES = 128
HIGH = lax.Precision.HIGHEST


def expand_roots(roots):
    coefficients = [complex(1.0, 0.0)]
    for root in roots:
        widened = coefficients + [complex(0.0, 0.0)]
        for position in range(1, len(widened)):
            widened[position] = widened[position] - root * coefficients[position - 1]
        coefficients = widened
    return [coefficient.real for coefficient in coefficients]


def horner_value(coefficients, point):
    running = complex(0.0, 0.0)
    for coefficient in coefficients:
        running = running * point + coefficient
    return running


def derive_coeffs(coefficients):
    degree = len(coefficients) - 1
    return [coefficients[position] * (degree - position) for position in range(degree)]


def filter_design():
    low_edge = 1.0 / 12.9
    high_edge = 1.0 / 12.0
    warped_low = 2.0 * math.tan(math.pi * low_edge)
    warped_high = 2.0 * math.tan(math.pi * high_edge)
    centre = math.sqrt(warped_low * warped_high)
    spread = warped_high - warped_low
    digital = []
    for octant in (3, 5):
        proto = complex(math.cos(octant * math.pi / 4.0), math.sin(octant * math.pi / 4.0)) * spread
        radical = (proto * proto - 4.0 * centre * centre) ** 0.5
        for analog in ((proto + radical) / 2.0, (proto - radical) / 2.0):
            digital.append((2.0 + analog) / (2.0 - analog))
    denom = expand_roots(digital)
    numer = [1.0, 0.0, -2.0, 0.0, 1.0]
    omega = 2.0 * math.atan(centre / 2.0)
    zcentre = complex(math.cos(omega), math.sin(omega))
    respond = horner_value(numer, zcentre) / horner_value(denom, zcentre)
    numer = [coefficient / abs(respond) for coefficient in numer]
    remain = [numer[position] - numer[0] * denom[position] for position in range(1, 5)]
    slope = derive_coeffs(denom)
    amat = np.zeros((4, 4))
    bvec = np.zeros(4)
    cvec = np.zeros(4)
    upper = [pole for pole in digital if pole.imag > 0]
    for index, pole in enumerate(upper):
        resid = horner_value(remain, pole) / horner_value(slope, pole)
        first = 2 * index
        amat[first, first] = pole.real
        amat[first, first + 1] = -pole.imag
        amat[first + 1, first] = pole.imag
        amat[first + 1, first + 1] = pole.real
        bvec[first] = 1.0
        cvec[first] = 2.0 * resid.real
        cvec[first + 1] = -2.0 * resid.imag
    return (amat, bvec, cvec, float(numer[0]))


def power(matrix, exponent):
    return np.linalg.matrix_power(matrix, exponent)


@functools.lru_cache(maxsize=None)
def plan():
    amat, bvec, cvec, direct = filter_design()
    n = HOURS
    impulse = [direct] + [float(cvec @ power(amat, step - 1) @ bvec) for step in range(1, n)]
    toeplitz = np.array([[impulse[row - col] if col <= row else 0.0 for col in range(n)] for row in range(n)])
    left = np.stack([power(amat, n - 1 - hour) @ bvec for hour in range(n)], axis=1)
    entering = np.stack([cvec @ power(amat, hour) for hour in range(n)], axis=0)
    back = np.stack([power(amat, hour) @ bvec for hour in range(n)], axis=1)
    summary = np.concatenate([left, back @ toeplitz], axis=0)
    coupling = back @ entering
    step = power(amat, n)
    width = GROUP * 8 + 8
    forward = np.zeros((GROUP + 1, 4, width))
    forward[0][:, GROUP * 8 : GROUP * 8 + 4] = np.eye(4)
    for j in range(GROUP):
        forward[j + 1] = step @ forward[j]
        forward[j + 1][:, j * 8 : j * 8 + 4] += np.eye(4)
    backward = np.zeros((GROUP + 1, 4, width))
    backward[GROUP][:, GROUP * 8 + 4 :] = np.eye(4)
    for j in reversed(range(GROUP)):
        backward[j] = step @ backward[j + 1] + coupling @ forward[j]
        backward[j][:, j * 8 + 4 : j * 8 + 8] += np.eye(4)
    own = GROUP * 8
    inner = np.zeros((GROUP * 8, width))
    for j in range(GROUP):
        inner[j * 8 : j * 8 + 4] = forward[j]
        inner[j * 8 + 4 : j * 8 + 8] = backward[j + 1]
    run_left = forward[GROUP][:, :own]
    run_right = backward[0][:, :own]
    run_coupling = backward[0][:, own : own + 4]
    run_step = power(step, GROUP)
    suffix = [np.zeros((4, 4))]
    for m in range(RUNS):
        suffix.append(suffix[-1] + power(run_step, m) @ run_coupling @ power(run_step, m))
    pair = 2 * own
    send = np.zeros((RUNS, 16, pair))
    gather = np.zeros((RUNS, 16, RUNS * 8))
    local = np.zeros((RUNS, 16, pair))
    for z in range(RUNS):
        after = suffix[RUNS - 1 - z]
        right = run_right + run_step @ after @ run_left
        for m in range(2):
            send[z, 4 * m : 4 * m + 4, m * own : (m + 1) * own] = run_left
            send[z, 8 + 4 * m : 12 + 4 * m, m * own : (m + 1) * own] = right
            local[z, 8 + 4 * m : 12 + 4 * m, m * own : (m + 1) * own] = after @ run_left
            for other in range(RUNS):
                here = slice(other * 8 + 4 * m, other * 8 + 4 * m + 4)
                if other < z:
                    came = power(run_step, z - 1 - other)
                    gather[z, 4 * m : 4 * m + 4, here] = came
                    gather[z, 8 + 4 * m : 12 + 4 * m, here] = after @ run_step @ came
                if other > z:
                    gather[z, 8 + 4 * m : 12 + 4 * m, here] = power(run_step, other - z - 1)
    spread = np.zeros((pair, pair))
    inject = np.zeros((pair, 16))
    for m in range(2):
        rows = slice(m * own, (m + 1) * own)
        spread[rows, rows] = inner[:, :own]
        inject[rows, 4 * m : 4 * m + 4] = inner[:, own : own + 4]
        inject[rows, 8 + 4 * m : 12 + 4 * m] = inner[:, own + 4 :]
    single = np.float32
    return {
        "amat": amat,
        "cvec": cvec,
        "direct": direct,
        "summary": summary,
        "send": send.astype(single),
        "gather": gather.astype(single),
        "local": local.astype(single),
        "spread": spread.astype(single),
        "inject": inject.astype(single),
    }


def live_hours(mask, start):
    first = lax.axis_index("tm") * HOURS
    ocean = mask == 1
    return [jnp.where(ocean & (start <= first + hour), 1.0, 0.0) for hour in range(HOURS)]


def depths(levels_ref):
    out = []
    for level in range(4):
        number = jnp.full((ROWS, LANES), levels_ref[level], jnp.int32).astype(jnp.float32)
        out.append((number + number * number / 90.0) / 90.0)
    return out


def anomalies(field, live):
    mean = 0.25 * ((field[0] + field[1]) + (field[2] + field[3]))
    return [(field[level] - mean) * live for level in range(3)]


def pressures(rho, depth):
    press = [rho[0] * depth[0]]
    for level in range(1, 4):
        press.append(press[-1] + 0.5 * (rho[level - 1] + rho[level]) * (depth[level] - depth[level - 1]))
    return press


def summary_kernel(levels_ref, u_ref, v_ref, rho_ref, mask_ref, start_ref, out_ref):
    summary = plan()["summary"]
    live = live_hours(mask_ref[...], start_ref[...])
    depth = depths(levels_ref)
    for which, ref in enumerate((u_ref, v_ref, rho_ref)):
        sums = [[None] * 8 for _ in range(3)]
        for hour in range(HOURS):
            field = [ref[level, hour] for level in range(4)]
            if which == 2:
                field = pressures(field, depth)
            for level, value in enumerate(anomalies(field, live[hour])):
                for k in range(8):
                    term = float(summary[k, hour]) * value
                    sums[level][k] = term if hour == 0 else sums[level][k] + term
        for level in range(3):
            for k in range(8):
                row = (which * 3 + level) * 8 + k
                out_ref[pl.ds(row, ROWS, stride=SERIES * 8), :] = sums[level][k]


def paired(ref):
    empty = jnp.zeros((8, LANES), jnp.float32)
    columns = []
    for q in range(PAIRS):
        parts = []
        for m in range(2):
            s = 2 * q + m
            for j in range(GROUP):
                parts.append(ref[j, pl.ds(s * 8, 8), :] if s < SERIES else empty)
        columns.append(jnp.concatenate(parts, axis=0))
    return jnp.concatenate(columns, axis=1)


def dot(lhs, rhs):
    return jnp.dot(lhs, rhs, precision=HIGH, preferred_element_type=jnp.float32)


def run_kernel(in_ref, send_ref, out_ref):
    z = lax.axis_index("tm") // GROUP
    totals = dot(send_ref[z], paired(in_ref))
    for other in range(RUNS):
        later = other > z
        for q in range(PAIRS):
            lanes = slice(q * LANES, (q + 1) * LANES)
            out_ref[other, pl.ds(q * 8, 8), :] = jnp.where(later, totals[0:8, lanes], totals[8:16, lanes])


def border_kernel(in_ref, runs_ref, gather_ref, local_ref, spread_ref, inject_ref, out_ref):
    z = lax.axis_index("tm") // GROUP
    blocks = paired(in_ref)
    runs = jnp.concatenate(
        [
            jnp.concatenate([runs_ref[other, pl.ds(q * 8, 8), :] for other in range(RUNS)], axis=0)
            for q in range(PAIRS)
        ],
        axis=1,
    )
    states = dot(gather_ref[z], runs) + dot(local_ref[z], blocks)
    borders = dot(spread_ref[...], blocks) + dot(inject_ref[...], states)
    for s in range(SERIES):
        q, m = s // 2, s % 2
        for j in range(GROUP):
            row = m * GROUP * 8 + j * 8
            out_ref[j, pl.ds(s * 8, 8), :] = borders[row : row + 8, q * LANES : (q + 1) * LANES]


def filter_steps(state, samples):
    amat, cvec, direct = plan()["amat"], plan()["cvec"], plan()["direct"]
    out = []
    for sample in samples:
        value = direct * sample
        for k in range(4):
            value = value + float(cvec[k]) * state[k]
        out.append(value)
        fresh = []
        for first in (0, 2):
            real, imag = float(amat[first, first]), float(amat[first + 1, first])
            fresh.append((real * state[first] - imag * state[first + 1]) + sample)
            fresh.append(imag * state[first] + real * state[first + 1])
        state = fresh
    return out


def band_kernel(
    levels_ref, u_ref, v_ref, rho_ref, mask_ref, start_ref, borders_ref, press_ref, flux_ref, edge_ref, held, east, north
):
    mask = mask_ref[...]
    start = start_ref[...]
    live = live_hours(mask, start)
    depth = depths(levels_ref)
    for which, ref in ((2, rho_ref), (0, u_ref), (1, v_ref)):
        for hour in range(HOURS):
            field = [ref[level, hour] for level in range(4)]
            if which == 2:
                field = pressures(field, depth)
            for level, value in enumerate(anomalies(field, live[hour])):
                held[level, hour] = value
        target = (east, north, press_ref)[which]
        for level in range(3):
            states = [
                borders_ref[pl.ds((which * 3 + level) * 8 + k, ROWS, stride=SERIES * 8), :] for k in range(8)
            ]
            samples = filter_steps(states[:4], [held[level, hour] for hour in range(HOURS)])
            samples = filter_steps(states[4:], samples[::-1])[::-1]
            for hour in range(HOURS):
                target[level, hour] = samples[hour]
    lane = lax.broadcasted_iota(jnp.int32, (ROWS, LANES), 1)
    row = lax.broadcasted_iota(jnp.int32, (ROWS, LANES), 0)
    half = 0.5 * mask.astype(jnp.float32)
    last = lane == LANES - 1
    edges = jnp.zeros((ROWS, LANES), jnp.float32)
    for hour in range(HOURS):
        u_all = [east[level, hour] for level in range(3)]
        v_all = [north[level, hour] for level in range(3)]
        p_all = [press_ref[level, hour] for level in range(3)]
        for values in (u_all, v_all, p_all):
            values.append(-((values[0] + values[1]) + values[2]))
        press_ref[3, hour] = p_all[3]
        for level in range(4):
            fx = u_all[level] * p_all[level]
            fy = v_all[level] * p_all[level]
            position = 2 * (level * HOURS + hour)
            turned = pltpu.roll(fx, (position + 1) % LANES, 1)
            edges = jnp.where((lane == position) | (lane == position + 1), turned, edges)
            along_x = jnp.where(last, 0.0, pltpu.roll(fx, LANES - 1, 1)) - jnp.where(
                lane == 0, 0.0, pltpu.roll(fx, 1, 1)
            )
            along_y = jnp.where(row == ROWS - 1, 0.0, pltpu.roll(fy, ROWS - 1, 0)) - jnp.where(
                row == 0, 0.0, pltpu.roll(fy, 1, 0)
            )
            flux_ref[level, hour] = half * (along_x + along_y)
    edge_ref[...] = edges


def seam_kernel(flux_ref, mask_ref, west_ref, east_ref, out_ref):
    lane = lax.broadcasted_iota(jnp.int32, (ROWS, LANES), 1)
    half = 0.5 * mask_ref[...].astype(jnp.float32)
    weight = jnp.where(lane == LANES - 1, half, jnp.where(lane == 0, -half, 0.0))
    halo = jnp.where(
        lane % 2 == 0, pltpu.roll(east_ref[...], LANES - 1, 1), pltpu.roll(west_ref[...], 1, 1)
    )
    for level in range(4):
        for hour in range(HOURS):
            position = 2 * (level * HOURS + hour)
            turned = pltpu.roll(halo, LANES - 1 - position, 1)
            out_ref[level, hour] = flux_ref[level, hour] + weight * turned


def swap(array):
    groups = [[z * GROUP + i for i in range(GROUP)] for z in range(RUNS)]
    return lax.all_to_all(array, "tm", 0, 0, tiled=True, axis_index_groups=groups)


def swap_runs(array):
    groups = [[z * GROUP + i for z in range(RUNS)] for i in range(GROUP)]
    return lax.all_to_all(array, "tm", 0, 0, tiled=True, axis_index_groups=groups)


VMEM = pl.BlockSpec(memory_space=pltpu.VMEM)
SMEM = pl.BlockSpec(memory_space=pltpu.SMEM)


def call(kernel, shapes, n_in, scalars=0, scratch=()):
    shapes = [jax.ShapeDtypeStruct(shape, jnp.float32) for shape in shapes]
    single = len(shapes) == 1
    return pl.pallas_call(
        kernel,
        out_shape=shapes[0] if single else shapes,
        in_specs=[SMEM] * scalars + [VMEM] * (n_in - scalars),
        out_specs=VMEM if single else [VMEM] * len(shapes),
        scratch_shapes=[pltpu.VMEM(shape, jnp.float32) for shape in scratch],
        compiler_params=pltpu.CompilerParams(vmem_limit_bytes=32 * 1024 * 1024),
    )


def on_device(u_vel, v_vel, density, land_mask, start_hour, levels):
    tables = plan()
    whole = (4, HOURS, ROWS, LANES)
    part = (3, HOURS, ROWS, LANES)
    slots = (ROWS, SERIES * 8, LANES)
    flat = (ROWS * SERIES * 8, LANES)
    fields = (levels, u_vel, v_vel, density, land_mask, start_hour)
    own = call(summary_kernel, [flat], 6, 1)(*fields)
    blocks = swap(own.reshape(slots))
    runs = call(run_kernel, [(RUNS, PAIRS * 8, LANES)], 2)(blocks, tables["send"])
    runs = swap_runs(runs)
    borders = call(border_kernel, [slots], 6)(
        blocks, runs, tables["gather"], tables["local"], tables["spread"], tables["inject"]
    )
    borders = swap(borders).reshape(flat)
    pressure, flux, edges = call(band_kernel, [whole, whole, (ROWS, LANES)], 7, 1, [part, part, part])(
        *fields, borders
    )
    count = lax.axis_size("col")
    west = lax.ppermute(edges, "col", [(i, i + 1) for i in range(count - 1)])
    east = lax.ppermute(edges, "col", [(i + 1, i) for i in range(count - 1)])
    flux = call(seam_kernel, [whole], 4)(flux, land_mask, west, east)
    return (pressure, flux)


def solution(mesh):
    return jax.shard_map(
        on_device,
        mesh=mesh,
        in_specs=(
            P(None, "tm", None, "col"),
            P(None, "tm", None, "col"),
            P(None, "tm", None, "col"),
            P(None, "col"),
            P(None, "col"),
            P(),
        ),
        out_specs=(P(None, "tm", None, "col"), P(None, "tm", None, "col")),
        check_vma=False,
    )
```

```python
import functools
import math

import jax
import jax.numpy as jnp
import numpy as np
from jax import lax
from jax.experimental import pallas as pl
from jax.experimental.pallas import tpu as pltpu
from jax.sharding import PartitionSpec as P

HOURS = 16
GROUP = 16
RUNS = 4
OWNERS = 2 * GROUP
SERIES = 9
ROWS = 8
LANES = 128
QUARTER = 32
SLOT = 24
SPAN = GROUP * HOURS
QUARTERS = (0, 3, 1, 2)
PAIRS = ((0, 1), (2, 3), (4, 5), (6, 7))
FAR = ((1, 2), (3, 4), (5, 6), (7, 0))
HIGH = lax.Precision.HIGHEST


def expand_roots(roots):
    coefficients = [complex(1.0, 0.0)]
    for root in roots:
        widened = coefficients + [complex(0.0, 0.0)]
        for position in range(1, len(widened)):
            widened[position] = widened[position] - root * coefficients[position - 1]
        coefficients = widened
    return [coefficient.real for coefficient in coefficients]


def horner_value(coefficients, point):
    running = complex(0.0, 0.0)
    for coefficient in coefficients:
        running = running * point + coefficient
    return running


def derive_coeffs(coefficients):
    degree = len(coefficients) - 1
    return [coefficients[position] * (degree - position) for position in range(degree)]


def filter_design():
    low_edge = 1.0 / 12.9
    high_edge = 1.0 / 12.0
    warped_low = 2.0 * math.tan(math.pi * low_edge)
    warped_high = 2.0 * math.tan(math.pi * high_edge)
    centre = math.sqrt(warped_low * warped_high)
    spread = warped_high - warped_low
    digital = []
    for octant in (3, 5):
        proto = complex(math.cos(octant * math.pi / 4.0), math.sin(octant * math.pi / 4.0)) * spread
        radical = (proto * proto - 4.0 * centre * centre) ** 0.5
        for analog in ((proto + radical) / 2.0, (proto - radical) / 2.0):
            digital.append((2.0 + analog) / (2.0 - analog))
    denom = expand_roots(digital)
    numer = [1.0, 0.0, -2.0, 0.0, 1.0]
    omega = 2.0 * math.atan(centre / 2.0)
    zcentre = complex(math.cos(omega), math.sin(omega))
    respond = horner_value(numer, zcentre) / horner_value(denom, zcentre)
    numer = [coefficient / abs(respond) for coefficient in numer]
    remain = [numer[position] - numer[0] * denom[position] for position in range(1, 5)]
    slope = derive_coeffs(denom)
    amat = np.zeros((4, 4))
    bvec = np.zeros(4)
    cvec = np.zeros(4)
    upper = [pole for pole in digital if pole.imag > 0]
    for index, pole in enumerate(upper):
        resid = horner_value(remain, pole) / horner_value(slope, pole)
        first = 2 * index
        amat[first, first] = pole.real
        amat[first, first + 1] = -pole.imag
        amat[first + 1, first] = pole.imag
        amat[first + 1, first + 1] = pole.real
        bvec[first] = 1.0
        cvec[first] = 2.0 * resid.real
        cvec[first + 1] = -2.0 * resid.imag
    return (amat, bvec, cvec, float(numer[0]))


def power(matrix, exponent):
    return np.linalg.matrix_power(matrix, exponent)


def power(matrix, exponent):
    return np.linalg.matrix_power(matrix, exponent)


def block_maps(hours):
    amat, bvec, cvec, direct = filter_design()
    impulse = [direct] + [float(cvec @ power(amat, step - 1) @ bvec) for step in range(1, hours)]
    toeplitz = np.zeros((hours, hours))
    for row in range(hours):
        for column in range(row + 1):
            toeplitz[row, column] = impulse[row - column]
    powers = [np.eye(4)]
    for hour in range(hours):
        powers.append(powers[-1] @ amat)
    left = np.stack([powers[hours - 1 - hour] @ bvec for hour in range(hours)], axis=1)
    entering = np.stack([cvec @ powers[hour] for hour in range(hours)], axis=0)
    back = np.stack([powers[hour] @ bvec for hour in range(hours)], axis=1)
    summary = np.concatenate([left, back @ toeplitz], axis=0)
    response = toeplitz.T @ toeplitz
    injected = np.concatenate([toeplitz.T @ entering, entering[::-1]], axis=1)
    return summary, back @ entering, powers[hours], response, injected


@functools.lru_cache(maxsize=None)
def plan():
    amat, bvec, cvec, direct = filter_design()
    summary, coupling, step, _, _ = block_maps(HOURS)
    own = GROUP * 8
    forward = np.zeros((GROUP + 1, 4, own + 8))
    forward[0][:, own : own + 4] = np.eye(4)
    for j in range(GROUP):
        forward[j + 1] = step @ forward[j]
        forward[j + 1][:, j * 8 : j * 8 + 4] += np.eye(4)
    backward = np.zeros((GROUP + 1, 4, own + 8))
    backward[GROUP][:, own + 4 :] = np.eye(4)
    for j in reversed(range(GROUP)):
        backward[j] = step @ backward[j + 1] + coupling @ forward[j]
        backward[j][:, j * 8 + 4 : j * 8 + 8] += np.eye(4)
    inner = np.zeros((own, own + 8))
    for j in range(GROUP):
        inner[j * 8 : j * 8 + 4] = forward[j]
        inner[j * 8 + 4 : j * 8 + 8] = backward[j + 1]
    run_left = forward[GROUP][:, :own]
    run_right = backward[0][:, :own]
    run_summary, run_coupling, run_step, response, injected = block_maps(SPAN)
    suffix = [np.zeros((4, 4))]
    for m in range(RUNS):
        suffix.append(suffix[-1] + power(run_step, m) @ run_coupling @ power(run_step, m))
    send = np.zeros((RUNS, 16, 2 * own))
    local = np.zeros((RUNS, 16, 2 * own))
    gather = np.zeros((RUNS, 16, RUNS * 8))
    edge_gather = np.zeros((RUNS, LANES, LANES))
    for z in range(RUNS):
        after = suffix[RUNS - 1 - z]
        for tile in range(2):
            columns = slice(tile * own, (tile + 1) * own)
            ahead = slice(4 * tile, 4 * tile + 4)
            behind = slice(8 + 4 * tile, 12 + 4 * tile)
            send[z, ahead, columns] = run_left
            send[z, behind, columns] = run_right + run_step @ after @ run_left
            local[z, behind, columns] = after @ run_left
            for other in range(RUNS):
                here = slice(other * 8 + 4 * tile, other * 8 + 4 * tile + 4)
                if other < z:
                    came = power(run_step, z - 1 - other)
                    gather[z, ahead, here] = came
                    gather[z, behind, here] = after @ run_step @ came
                if other > z:
                    gather[z, behind, here] = power(run_step, other - z - 1)
        for other in range(RUNS):
            from_left = slice(other * 8, other * 8 + 4)
            from_right = slice(other * 8 + 4, other * 8 + 8)
            if other < z:
                came = power(run_step, z - 1 - other)
                edge_gather[z, from_left, 0:4] = came.T
                edge_gather[z, from_left, 4:8] = (after @ run_step @ came).T
            if other == z:
                edge_gather[z, from_left, 4:8] = after.T
            if other > z:
                came = power(run_step, other - z - 1)
                edge_gather[z, from_right, 4:8] = came.T
                edge_gather[z, from_left, 4:8] = (came @ run_step @ suffix[RUNS - 1 - other]).T
    spread = inner[:, :own]
    inject = np.zeros((2, own, 16))
    for tile in range(2):
        inject[tile, :, 4 * tile : 4 * tile + 4] = inner[:, own : own + 4]
        inject[tile, :, 8 + 4 * tile : 12 + 4 * tile] = inner[:, own + 4 :]
    edge_sum = np.zeros((SPAN, LANES))
    edge_sum[:, QUARTER : QUARTER + 8] = run_summary.T
    edge_out = np.zeros((SPAN + LANES, SPAN))
    edge_out[:SPAN] = response.T
    edge_out[SPAN : SPAN + 8] = injected.T
    tables = dict(
        send=send,
        local=local,
        gather=gather,
        spread=spread,
        inject=inject,
        edge_sum=edge_sum,
        edge_gather=edge_gather,
        edge_out=edge_out,
    )
    tables = {name: table.astype(np.float32) for name, table in tables.items()}
    return dict(tables, amat=amat, cvec=cvec, direct=direct, summary=summary)


def place():
    tile = lax.axis_index("col") % 2
    return lax.axis_index("tm") // GROUP, tile, 1 - tile


def lanes_of(shape=(ROWS, LANES)):
    return lax.broadcasted_iota(jnp.int32, shape, 1)


def live_hours(mask, start):
    first = lax.axis_index("tm") * HOURS
    ocean = mask == 1
    return [jnp.where(ocean & (start <= first + hour), 1.0, 0.0) for hour in range(HOURS)]


def depths(levels_ref):
    out = []
    for level in range(4):
        number = jnp.full((ROWS, LANES), levels_ref[level], jnp.int32).astype(jnp.float32)
        out.append((number + number * number / 90.0) / 90.0)
    return out


def anomalies(field, live):
    mean = 0.25 * ((field[0] + field[1]) + (field[2] + field[3]))
    return [(field[level] - mean) * live for level in range(3)]


def pressures(rho, depth):
    press = [rho[0] * depth[0]]
    for level in range(1, 4):
        press.append(press[-1] + 0.5 * (rho[level - 1] + rho[level]) * (depth[level] - depth[level - 1]))
    return press


def last_level(values):
    return -((values[0] + values[1]) + values[2])


def turn(value, shift):
    shift = shift % LANES
    return value if shift == 0 else pltpu.roll(value, shift, 1)


def transposed(parts, lane):
    low = lane < 2 * QUARTER
    even = (lane // QUARTER) % 2 == 0
    halves = [None] * 4
    for i in range(2):
        first, second = parts[i], parts[i + 2]
        halves[i] = jnp.where(low, first, turn(second, 64))
        halves[i + 2] = jnp.where(low, turn(first, 64), second)
    out = [None] * 4
    for i in (0, 2):
        first, second = halves[i], halves[i + 1]
        out[i] = jnp.where(even, first, turn(second, QUARTER))
        out[i + 1] = jnp.where(even, turn(first, -QUARTER), second)
    return out


def summary_kernel(
    levels_hbm, u_hbm, v_hbm, rho_hbm, mask_hbm, start_hbm, out_ref, levels_ref, u_ref, v_ref, rho_ref, mask_ref, start_ref, sums_ref, sems
):
    summary = plan()["summary"]
    copies = [
        pltpu.make_async_copy(source, target, sems.at[index])
        for index, (source, target) in enumerate(
            (
                (mask_hbm, mask_ref),
                (start_hbm, start_ref),
                (levels_hbm, levels_ref),
                (u_hbm, u_ref),
                (rho_hbm, rho_ref),
                (v_hbm, v_ref),
            )
        )
    ]
    for copy in copies:
        copy.start()
    for copy in copies[:3]:
        copy.wait()
    live = live_hours(mask_ref[...], start_ref[...])
    depth = depths(levels_ref)
    lane = lanes_of()
    west = [jnp.zeros((ROWS, LANES), jnp.float32) for _ in range(8)]
    east = list(west)
    for which, ref in enumerate((u_ref, rho_ref, v_ref)):
        copies[3 + which].wait()
        sums = [[None] * 8 for _ in range(3)]
        for hour in range(HOURS):
            field = [ref[level, hour] for level in range(4)]
            if which == 1:
                field = pressures(field, depth)
            values = anomalies(field, live[hour])
            for level, value in enumerate(values):
                for k in range(8):
                    term = float(summary[k, hour]) * value
                    sums[level][k] = term if hour == 0 else sums[level][k] + term
            if which < 2:
                for level, value in enumerate(values + [last_level(values)]):
                    turned = turn(value, QUARTER + hour)
                    at = which * 4 + level
                    west[at] = jnp.where(lane == QUARTER + hour, turned, west[at])
                    east[at] = jnp.where(lane == QUARTER - 1 + hour, turned, east[at])
        for level in range(3):
            for k in range(8):
                sums_ref[(which * 3 + level) * 8 + k] = sums[level][k]
    first = lane < QUARTER
    for k in range(8):
        for v in range(2):
            parts = transposed([sums_ref[(4 * v + a) * 8 + k] for a in range(4)], lane)
            for index, quarter in enumerate(QUARTERS):
                out_ref[pl.ds(index * SLOT + v * 8 + k, ROWS, stride=4 * SLOT), :] = parts[quarter]
        single = sums_ref[64 + k]
        others = {0: west[k], 3: turn(east[k], 1)}
        for index, quarter in enumerate(QUARTERS):
            part = jnp.where(first, turn(single, -QUARTER * quarter), others.get(quarter, 0.0))
            out_ref[pl.ds(index * SLOT + 16 + k, ROWS, stride=4 * SLOT), :] = part


def blocks_of(in_ref, tile):
    return jnp.concatenate(
        [
            jnp.concatenate([in_ref[2 * j + tile, pl.ds(v * 8, 8), :] for j in range(GROUP)], axis=0)
            for v in range(3)
        ],
        axis=1,
    )


def edge_hours(in_ref, tile):
    lane = lanes_of()
    halves = []
    for half in range(2):
        total = jnp.zeros((ROWS, LANES), jnp.float32)
        for i in range(8):
            turned = turn(in_ref[2 * (half * 8 + i) + tile, pl.ds(16, 8), :], i * HOURS - QUARTER)
            total = jnp.where(lane // HOURS == i, turned, total)
        halves.append(total)
    return jnp.concatenate(halves, axis=1)


def dot(lhs, rhs):
    return jnp.dot(lhs, rhs, precision=HIGH, preferred_element_type=jnp.float32)


def run_kernel(in_ref, send_ref, edge_sum_ref, out_ref):
    run, tile, side = place()
    blocks = jnp.concatenate([blocks_of(in_ref, 0), blocks_of(in_ref, 1)], axis=0)
    totals = dot(send_ref[run], blocks)
    near = edge_hours(in_ref, 1 - tile)
    far = edge_hours(in_ref, tile)
    sums = dot(jnp.concatenate([near, far], axis=0), edge_sum_ref[...])
    first = lanes_of() < QUARTER
    for other in range(RUNS):
        for v in range(3):
            lanes = slice(v * LANES, (v + 1) * LANES)
            mine = jnp.where(other > run, totals[0:8, lanes], totals[8:16, lanes])
            if v == 2:
                mine = jnp.where(first, mine, sums[0:8])
                across = sums[8:16]
            else:
                across = far[:, lanes]
            for slot_side in range(2):
                out_ref[2 * other + slot_side, pl.ds(v * 8, 8), :] = jnp.where(side == slot_side, mine, across)


def edge_flux(in_ref, runs_ref, run, tile, side, edge_gather, edge_out):
    lane = lanes_of()
    own = [runs_ref[2 * other + side, pl.ds(16, 8), :] for other in range(RUNS)]
    across = [runs_ref[2 * other + 1 - side, pl.ds(16, 8), :] for other in range(RUNS)]
    sums = []
    for parts in (own, across):
        total = jnp.zeros((ROWS, LANES), jnp.float32)
        for other in range(RUNS):
            total = jnp.where(lane // 8 == other, turn(parts[other], other * 8 - QUARTER), total)
        sums.append(total)
    states = dot(jnp.concatenate(sums, axis=0), edge_gather)
    near = edge_hours(in_ref, 1 - tile)
    far = jnp.concatenate([runs_ref[2 * run + 1 - side, pl.ds(v * 8, 8), :] for v in range(2)], axis=1)
    hours = jnp.concatenate([near, far], axis=0)
    banded = dot(jnp.concatenate([hours, states], axis=1), edge_out)
    row = lax.broadcasted_iota(jnp.int32, (ROWS, SPAN), 0)
    products = [part * pltpu.roll(part, 4, 0) for part in (banded[0:8], banded[8:16])]
    return jnp.where(row < 4, products[0], products[1])


def border_kernel(
    in_ref, runs_ref, gather_ref, local_ref, spread_ref, inject_ref, edge_gather_ref, edge_out_ref, out_ref
):
    run, tile, side = place()
    flux = edge_flux(in_ref, runs_ref, run, tile, side, edge_gather_ref[run], edge_out_ref[...])
    tiles = [blocks_of(in_ref, 0), blocks_of(in_ref, 1)]
    runs = jnp.concatenate([runs_ref[2 * other + side].reshape(3, 8, LANES) for other in range(RUNS)], axis=1)
    runs = jnp.concatenate([runs[v] for v in range(3)], axis=1)
    states = dot(gather_ref[run], runs) + dot(local_ref[run], jnp.concatenate(tiles, axis=0))
    first = lanes_of() < QUARTER
    for which in range(2):
        borders = dot(spread_ref[...], tiles[which]) + dot(inject_ref[which], states)
        for j in range(GROUP):
            for v in range(3):
                value = borders[j * 8 : j * 8 + 8, v * LANES : (v + 1) * LANES]
                if v == 2:
                    half = flux[:, (j // 8) * LANES : (j // 8 + 1) * LANES]
                    value = jnp.where(first, value, turn(half, QUARTER - (j % 8) * HOURS))
                out_ref[2 * j + which, pl.ds(v * 8, 8), :] = value


def filter_steps(state, samples):
    amat, cvec, direct = plan()["amat"], plan()["cvec"], plan()["direct"]
    out = []
    for sample in samples:
        value = direct * sample
        for k in range(4):
            value = value + float(cvec[k]) * state[k]
        out.append(value)
        fresh = []
        for first in (0, 2):
            real, imag = float(amat[first, first]), float(amat[first + 1, first])
            fresh.append((real * state[first] - imag * state[first + 1]) + sample)
            fresh.append(imag * state[first] + real * state[first + 1])
        state = fresh
    return out


def band_kernel(
    levels_ref, u_ref, v_ref, rho_ref, mask_ref, start_ref, borders_ref, press_ref, flux_ref, held, east, north, states_ref
):
    _, tile, _ = place()
    column = lax.axis_index("col")
    mask = mask_ref[...]
    live = live_hours(mask, start_ref[...])
    depth = depths(levels_ref)
    lane = lanes_of()
    for k in range(8):
        for v in range(3):
            parts = [None] * 4
            for index, quarter in enumerate(QUARTERS):
                parts[quarter] = borders_ref[pl.ds(index * SLOT + v * 8 + k, ROWS, stride=4 * SLOT), :]
            if v < 2:
                for a, part in enumerate(transposed(parts, lane)):
                    states_ref[(4 * v + a) * 8 + k] = part
            else:
                total = parts[0]
                for quarter in range(1, 4):
                    total = jnp.where(lane // QUARTER == quarter, turn(parts[quarter], QUARTER * quarter), total)
                states_ref[64 + k] = total
    for which, ref in ((1, rho_ref), (0, u_ref), (2, v_ref)):
        for hour in range(HOURS):
            field = [ref[level, hour] for level in range(4)]
            if which == 1:
                field = pressures(field, depth)
            for level, value in enumerate(anomalies(field, live[hour])):
                held[level, hour] = value
        target = (east, press_ref, north)[which]
        for level in range(3):
            states = [states_ref[(which * 3 + level) * 8 + k] for k in range(8)]
            samples = filter_steps(states[:4], [held[level, hour] for hour in range(HOURS)])
            samples = filter_steps(states[4:], samples[::-1])[::-1]
            for hour in range(HOURS):
                target[level, hour] = samples[hour]
    row = lax.broadcasted_iota(jnp.int32, (ROWS, LANES), 0)
    half = 0.5 * mask.astype(jnp.float32)
    last = lane == LANES - 1
    halos = []
    for level in range(4):
        near = borders_ref[pl.ds(tile * SLOT + 16 + level, ROWS, stride=4 * SLOT), :]
        far = borders_ref[pl.ds(tile * SLOT + 20 + level, ROWS, stride=4 * SLOT), :]
        from_west = jnp.where(column == 0, 0.0, jnp.where(tile == 0, far, near))
        from_east = jnp.where(column == 2 * len(PAIRS) - 1, 0.0, jnp.where(tile == 0, near, far))
        halos.append((from_west, from_east))
    for hour in range(HOURS):
        u_all = [east[level, hour] for level in range(3)]
        v_all = [north[level, hour] for level in range(3)]
        p_all = [press_ref[level, hour] for level in range(3)]
        for values in (u_all, v_all, p_all):
            values.append(last_level(values))
        press_ref[3, hour] = p_all[3]
        for level in range(4):
            fx = u_all[level] * p_all[level]
            fy = v_all[level] * p_all[level]
            from_west, from_east = halos[level]
            next_x = jnp.where(last, turn(from_east, LANES - 1 - QUARTER - hour), turn(fx, -1))
            prev_x = jnp.where(lane == 0, turn(from_west, -QUARTER - hour), turn(fx, 1))
            next_y = jnp.where(row == ROWS - 1, 0.0, pltpu.roll(fy, ROWS - 1, 0))
            prev_y = jnp.where(row == 0, 0.0, pltpu.roll(fy, 1, 0))
            flux_ref[level, hour] = half * ((next_x - prev_x) + (next_y - prev_y))


def swap(array, devices, columns):
    groups = [[tm * 8 + col for tm in some for col in pair] for some in devices for pair in columns]
    return lax.all_to_all(array, ("tm", "col"), 0, 0, tiled=True, axis_index_groups=groups)


VMEM = pl.BlockSpec(memory_space=pltpu.VMEM)
SMEM = pl.BlockSpec(memory_space=pltpu.SMEM)
ANY = pl.BlockSpec(memory_space=pl.ANY)


def call(kernel, shapes, in_specs, scratch=()):
    shapes = [jax.ShapeDtypeStruct(shape, jnp.float32) for shape in shapes]
    single = len(shapes) == 1
    return pl.pallas_call(
        kernel,
        out_shape=shapes[0] if single else shapes,
        in_specs=in_specs,
        out_specs=VMEM if single else [VMEM] * len(shapes),
        scratch_shapes=scratch,
        compiler_params=pltpu.CompilerParams(vmem_limit_bytes=32 * 1024 * 1024),
    )


def on_device(u_vel, v_vel, density, land_mask, start_hour, levels):
    tables = plan()
    whole = (4, HOURS, ROWS, LANES)
    slots = (OWNERS, SLOT, LANES)
    flat = (OWNERS * SLOT, LANES)
    runs = [[z * GROUP + j for j in range(GROUP)] for z in range(RUNS)]
    across = [[z * GROUP + j for z in range(RUNS)] for j in range(GROUP)]
    fields = (levels, u_vel, v_vel, density, land_mask, start_hour)
    state_scratch = pltpu.VMEM((SERIES * 8, ROWS, LANES), jnp.float32)
    part_scratch = pltpu.VMEM((3, HOURS, ROWS, LANES), jnp.float32)
    own = call(
        summary_kernel,
        [flat],
        [ANY] * 6,
        [
            pltpu.SMEM((4,), jnp.int32),
            pltpu.VMEM(whole, jnp.float32),
            pltpu.VMEM(whole, jnp.float32),
            pltpu.VMEM(whole, jnp.float32),
            pltpu.VMEM((ROWS, LANES), jnp.int32),
            pltpu.VMEM((ROWS, LANES), jnp.int32),
            state_scratch,
            pltpu.SemaphoreType.DMA((6,)),
        ],
    )(*fields)
    blocks = swap(own.reshape(slots), runs, PAIRS)
    totals = call(run_kernel, [(2 * RUNS, SLOT, LANES)], [VMEM] * 3)(blocks, tables["send"], tables["edge_sum"])
    totals = swap(totals, across, FAR)
    borders = call(border_kernel, [slots], [VMEM] * 8)(
        blocks,
        totals,
        tables["gather"],
        tables["local"],
        tables["spread"],
        tables["inject"],
        tables["edge_gather"],
        tables["edge_out"],
    )
    borders = swap(borders, runs, PAIRS).reshape(flat)
    pressure, flux = call(
        band_kernel, [whole, whole], [SMEM] + [VMEM] * 6, [part_scratch, part_scratch, part_scratch, state_scratch]
    )(*fields, borders)
    return (pressure, flux)


def solution(mesh):
    return jax.shard_map(
        on_device,
        mesh=mesh,
        in_specs=(
            P(None, "tm", None, "col"),
            P(None, "tm", None, "col"),
            P(None, "tm", None, "col"),
            P(None, "col"),
            P(None, "col"),
            P(),
        ),
        out_specs=(P(None, "tm", None, "col"), P(None, "tm", None, "col")),
        check_vma=False,
    )
```

```python
import functools
import math

import jax
import jax.numpy as jnp
import numpy as np
from jax import lax
from jax.experimental import pallas as pl
from jax.experimental.pallas import tpu as pltpu
from jax.sharding import PartitionSpec as P

HOURS = 16
GROUP = 16
RUNS = 4
OWNERS = 2 * GROUP
SERIES = 9
ROWS = 8
LANES = 128
QUARTER = 32
SLOT = 24
SPAN = GROUP * HOURS
QUARTERS = (0, 3, 1, 2)
PAIRS = ((0, 1), (2, 3), (4, 5), (6, 7))
FAR = ((1, 2), (3, 4), (5, 6), (7, 0))
HIGH = lax.Precision.HIGHEST


def expand_roots(roots):
    coefficients = [complex(1.0, 0.0)]
    for root in roots:
        widened = coefficients + [complex(0.0, 0.0)]
        for position in range(1, len(widened)):
            widened[position] = widened[position] - root * coefficients[position - 1]
        coefficients = widened
    return [coefficient.real for coefficient in coefficients]


def horner_value(coefficients, point):
    running = complex(0.0, 0.0)
    for coefficient in coefficients:
        running = running * point + coefficient
    return running


def derive_coeffs(coefficients):
    degree = len(coefficients) - 1
    return [coefficients[position] * (degree - position) for position in range(degree)]


def filter_design():
    low_edge = 1.0 / 12.9
    high_edge = 1.0 / 12.0
    warped_low = 2.0 * math.tan(math.pi * low_edge)
    warped_high = 2.0 * math.tan(math.pi * high_edge)
    centre = math.sqrt(warped_low * warped_high)
    spread = warped_high - warped_low
    digital = []
    for octant in (3, 5):
        proto = complex(math.cos(octant * math.pi / 4.0), math.sin(octant * math.pi / 4.0)) * spread
        radical = (proto * proto - 4.0 * centre * centre) ** 0.5
        for analog in ((proto + radical) / 2.0, (proto - radical) / 2.0):
            digital.append((2.0 + analog) / (2.0 - analog))
    denom = expand_roots(digital)
    numer = [1.0, 0.0, -2.0, 0.0, 1.0]
    omega = 2.0 * math.atan(centre / 2.0)
    zcentre = complex(math.cos(omega), math.sin(omega))
    respond = horner_value(numer, zcentre) / horner_value(denom, zcentre)
    numer = [coefficient / abs(respond) for coefficient in numer]
    remain = [numer[position] - numer[0] * denom[position] for position in range(1, 5)]
    slope = derive_coeffs(denom)
    amat = np.zeros((4, 4))
    bvec = np.zeros(4)
    cvec = np.zeros(4)
    upper = [pole for pole in digital if pole.imag > 0]
    for index, pole in enumerate(upper):
        resid = horner_value(remain, pole) / horner_value(slope, pole)
        first = 2 * index
        amat[first, first] = pole.real
        amat[first, first + 1] = -pole.imag
        amat[first + 1, first] = pole.imag
        amat[first + 1, first + 1] = pole.real
        bvec[first] = 1.0
        cvec[first] = 2.0 * resid.real
        cvec[first + 1] = -2.0 * resid.imag
    return (amat, bvec, cvec, float(numer[0]))


def power(matrix, exponent):
    return np.linalg.matrix_power(matrix, exponent)


def power(matrix, exponent):
    return np.linalg.matrix_power(matrix, exponent)


def block_maps(hours):
    amat, bvec, cvec, direct = filter_design()
    impulse = [direct] + [float(cvec @ power(amat, step - 1) @ bvec) for step in range(1, hours)]
    toeplitz = np.zeros((hours, hours))
    for row in range(hours):
        for column in range(row + 1):
            toeplitz[row, column] = impulse[row - column]
    powers = [np.eye(4)]
    for hour in range(hours):
        powers.append(powers[-1] @ amat)
    left = np.stack([powers[hours - 1 - hour] @ bvec for hour in range(hours)], axis=1)
    entering = np.stack([cvec @ powers[hour] for hour in range(hours)], axis=0)
    back = np.stack([powers[hour] @ bvec for hour in range(hours)], axis=1)
    summary = np.concatenate([left, back @ toeplitz], axis=0)
    response = toeplitz.T @ toeplitz
    injected = np.concatenate([toeplitz.T @ entering, entering[::-1]], axis=1)
    return summary, back @ entering, powers[hours], response, injected


@functools.lru_cache(maxsize=None)
def plan():
    amat, bvec, cvec, direct = filter_design()
    summary, coupling, step, _, entering = block_maps(HOURS)
    basis = []
    for sign in (1.0, -1.0):
        part = np.linalg.svd(entering + sign * entering[::-1])[0][:, :4]
        basis.append(part)
    coordinates = np.concatenate(basis, axis=1).T @ entering
    own = GROUP * 8
    forward = np.zeros((GROUP + 1, 4, own + 8))
    forward[0][:, own : own + 4] = np.eye(4)
    for j in range(GROUP):
        forward[j + 1] = step @ forward[j]
        forward[j + 1][:, j * 8 : j * 8 + 4] += np.eye(4)
    backward = np.zeros((GROUP + 1, 4, own + 8))
    backward[GROUP][:, own + 4 :] = np.eye(4)
    for j in reversed(range(GROUP)):
        backward[j] = step @ backward[j + 1] + coupling @ forward[j]
        backward[j][:, j * 8 + 4 : j * 8 + 8] += np.eye(4)
    inner = np.zeros((own, own + 8))
    for j in range(GROUP):
        inner[j * 8 : j * 8 + 4] = forward[j]
        inner[j * 8 + 4 : j * 8 + 8] = backward[j + 1]
    run_left = forward[GROUP][:, :own]
    run_right = backward[0][:, :own]
    run_summary, run_coupling, run_step, response, injected = block_maps(SPAN)
    suffix = [np.zeros((4, 4))]
    for m in range(RUNS):
        suffix.append(suffix[-1] + power(run_step, m) @ run_coupling @ power(run_step, m))
    send = np.zeros((RUNS, 16, 2 * own))
    local = np.zeros((RUNS, 16, 2 * own))
    gather = np.zeros((RUNS, 16, RUNS * 8))
    edge_gather = np.zeros((RUNS, LANES, LANES))
    for z in range(RUNS):
        after = suffix[RUNS - 1 - z]
        for tile in range(2):
            columns = slice(tile * own, (tile + 1) * own)
            ahead = slice(4 * tile, 4 * tile + 4)
            behind = slice(8 + 4 * tile, 12 + 4 * tile)
            send[z, ahead, columns] = run_left
            send[z, behind, columns] = run_right + run_step @ after @ run_left
            local[z, behind, columns] = after @ run_left
            for other in range(RUNS):
                here = slice(other * 8 + 4 * tile, other * 8 + 4 * tile + 4)
                if other < z:
                    came = power(run_step, z - 1 - other)
                    gather[z, ahead, here] = came
                    gather[z, behind, here] = after @ run_step @ came
                if other > z:
                    gather[z, behind, here] = power(run_step, other - z - 1)
        for other in range(RUNS):
            from_left = slice(other * 8, other * 8 + 4)
            from_right = slice(other * 8 + 4, other * 8 + 8)
            if other < z:
                came = power(run_step, z - 1 - other)
                edge_gather[z, from_left, 0:4] = came.T
                edge_gather[z, from_left, 4:8] = (after @ run_step @ came).T
            if other == z:
                edge_gather[z, from_left, 4:8] = after.T
            if other > z:
                came = power(run_step, other - z - 1)
                edge_gather[z, from_right, 4:8] = came.T
                edge_gather[z, from_left, 4:8] = (came @ run_step @ suffix[RUNS - 1 - other]).T
    for j in range(GROUP):
        inner[j * 8 : j * 8 + 8] = coordinates @ inner[j * 8 : j * 8 + 8]
    spread = inner[:, :own]
    inject = np.zeros((2, own, 16))
    for tile in range(2):
        inject[tile, :, 4 * tile : 4 * tile + 4] = inner[:, own : own + 4]
        inject[tile, :, 8 + 4 * tile : 12 + 4 * tile] = inner[:, own + 4 :]
    edge_sum = np.zeros((SPAN, LANES))
    edge_sum[:, QUARTER : QUARTER + 8] = run_summary.T
    edge_response = response.T
    edge_inject = np.zeros((LANES, SPAN))
    edge_inject[:8] = injected.T
    tables = dict(
        send=send,
        local=local,
        gather=gather,
        spread=spread,
        inject=inject,
        edge_sum=edge_sum,
        edge_gather=edge_gather,
        edge_response=edge_response,
        edge_inject=edge_inject,
    )
    tables = {name: table.astype(np.float32) for name, table in tables.items()}
    return dict(tables, amat=amat, cvec=cvec, direct=direct, summary=summary, even=basis[0], odd=basis[1])


def place():
    tile = lax.axis_index("col") % 2
    return lax.axis_index("tm") // GROUP, tile, 1 - tile


def lanes_of(shape=(ROWS, LANES)):
    return lax.broadcasted_iota(jnp.int32, shape, 1)


def live_hours(mask, start):
    first = lax.axis_index("tm") * HOURS
    ocean = mask == 1
    return [jnp.where(ocean & (start <= first + hour), 1.0, 0.0) for hour in range(HOURS)]


def depths(levels_ref):
    out = []
    for level in range(4):
        number = jnp.full((ROWS, LANES), levels_ref[level], jnp.int32).astype(jnp.float32)
        out.append((number + number * number / 90.0) / 90.0)
    return out


def anomalies(field, live):
    mean = 0.25 * ((field[0] + field[1]) + (field[2] + field[3]))
    return [(field[level] - mean) * live for level in range(3)]


def pressures(rho, depth):
    press = [rho[0] * depth[0]]
    for level in range(1, 4):
        press.append(press[-1] + 0.5 * (rho[level - 1] + rho[level]) * (depth[level] - depth[level - 1]))
    return press


def last_level(values):
    return -((values[0] + values[1]) + values[2])


def turn(value, shift):
    shift = shift % LANES
    return value if shift == 0 else pltpu.roll(value, shift, 1)


def transposed(parts, lane):
    low = lane < 2 * QUARTER
    even = (lane // QUARTER) % 2 == 0
    halves = [None] * 4
    for i in range(2):
        first, second = parts[i], parts[i + 2]
        halves[i] = jnp.where(low, first, turn(second, 64))
        halves[i + 2] = jnp.where(low, turn(first, 64), second)
    out = [None] * 4
    for i in (0, 2):
        first, second = halves[i], halves[i + 1]
        out[i] = jnp.where(even, first, turn(second, QUARTER))
        out[i + 1] = jnp.where(even, turn(first, -QUARTER), second)
    return out


def summary_kernel(
    levels_hbm, u_hbm, v_hbm, rho_hbm, mask_hbm, start_hbm, out_ref, kept_ref, levels_ref, u_ref, v_ref, rho_ref, mask_ref, start_ref, sums_ref, sems
):
    summary = plan()["summary"]
    copies = [
        pltpu.make_async_copy(source, target, sems.at[index])
        for index, (source, target) in enumerate(
            (
                (mask_hbm, mask_ref),
                (start_hbm, start_ref),
                (levels_hbm, levels_ref),
                (u_hbm, u_ref),
                (rho_hbm, rho_ref),
                (v_hbm, v_ref),
            )
        )
    ]
    for copy in copies:
        copy.start()
    for copy in copies[:3]:
        copy.wait()
    live = live_hours(mask_ref[...], start_ref[...])
    depth = depths(levels_ref)
    lane = lanes_of()
    west = [jnp.zeros((ROWS, LANES), jnp.float32) for _ in range(8)]
    east = list(west)
    for which, ref in enumerate((u_ref, rho_ref, v_ref)):
        copies[3 + which].wait()
        sums = [[None] * 8 for _ in range(3)]
        for hour in range(HOURS):
            field = [ref[level, hour] for level in range(4)]
            if which == 1:
                field = pressures(field, depth)
            values = anomalies(field, live[hour])
            for level, value in enumerate(values):
                kept_ref[which * 3 + level, hour] = value
                for k in range(8):
                    term = float(summary[k, hour]) * value
                    sums[level][k] = term if hour == 0 else sums[level][k] + term
                if which < 2:
                    turned = turn(value, QUARTER + hour)
                    at = which * 4 + level
                    west[at] = jnp.where(lane == QUARTER + hour, turned, west[at])
                    east[at] = jnp.where(lane == QUARTER - 1 + hour, turned, east[at])
        for level in range(3):
            for k in range(8):
                sums_ref[(which * 3 + level) * 8 + k] = sums[level][k]
    for ends in (west, east):
        for at in (0, 4):
            ends[at + 3] = last_level(ends[at : at + 3])
    first = lane < QUARTER
    for k in range(8):
        for v in range(2):
            parts = transposed([sums_ref[(4 * v + a) * 8 + k] for a in range(4)], lane)
            for index, quarter in enumerate(QUARTERS):
                out_ref[pl.ds(index * SLOT + v * 8 + k, ROWS, stride=4 * SLOT), :] = parts[quarter]
        single = sums_ref[64 + k]
        others = {0: west[k], 3: turn(east[k], 1)}
        for index, quarter in enumerate(QUARTERS):
            part = jnp.where(first, turn(single, -QUARTER * quarter), others.get(quarter, 0.0))
            out_ref[pl.ds(index * SLOT + 16 + k, ROWS, stride=4 * SLOT), :] = part


def filter_steps(samples):
    amat, cvec, direct = plan()["amat"], plan()["cvec"], plan()["direct"]
    out = [direct * samples[0]]
    state = [samples[0], None, samples[0], None]
    for sample in samples[1:]:
        value = direct * sample
        for k in range(4):
            if state[k] is not None:
                value = value + float(cvec[k]) * state[k]
        out.append(value)
        fresh = []
        for first in (0, 2):
            real, imag = float(amat[first, first]), float(amat[first + 1, first])
            if state[first + 1] is None:
                fresh.append(real * state[first] + sample)
                fresh.append(imag * state[first])
            else:
                fresh.append((real * state[first] - imag * state[first + 1]) + sample)
                fresh.append(imag * state[first] + real * state[first + 1])
        state = fresh
    return out


def response_kernel(kept_ref, out_ref):
    def one(s, carry):
        samples = filter_steps([kept_ref[s, hour] for hour in range(HOURS)])
        samples = filter_steps(samples[::-1])[::-1]
        for hour in range(HOURS):
            out_ref[s, hour] = samples[hour]
        return carry

    lax.fori_loop(0, SERIES, one, 0)


def blocks_of(in_ref, tile):
    return jnp.concatenate(
        [
            jnp.concatenate([in_ref[2 * j + tile, pl.ds(v * 8, 8), :] for j in range(GROUP)], axis=0)
            for v in range(3)
        ],
        axis=1,
    )


def edge_hours(in_ref, tile):
    lane = lanes_of()
    halves = []
    for half in range(2):
        total = jnp.zeros((ROWS, LANES), jnp.float32)
        for i in range(8):
            turned = turn(in_ref[2 * (half * 8 + i) + tile, pl.ds(16, 8), :], i * HOURS - QUARTER)
            total = jnp.where(lane // HOURS == i, turned, total)
        halves.append(total)
    return jnp.concatenate(halves, axis=1)


def dot(lhs, rhs):
    return jnp.dot(lhs, rhs, precision=HIGH, preferred_element_type=jnp.float32)


def run_kernel(in_ref, send_ref, edge_sum_ref, out_ref):
    run, tile, side = place()
    blocks = jnp.concatenate([blocks_of(in_ref, 0), blocks_of(in_ref, 1)], axis=0)
    totals = dot(send_ref[run], blocks)
    near = edge_hours(in_ref, 1 - tile)
    far = edge_hours(in_ref, tile)
    sums = dot(jnp.concatenate([near, far], axis=0), edge_sum_ref[...])
    first = lanes_of() < QUARTER
    for other in range(RUNS):
        for v in range(3):
            lanes = slice(v * LANES, (v + 1) * LANES)
            mine = jnp.where(other > run, totals[0:8, lanes], totals[8:16, lanes])
            if v == 2:
                mine = jnp.where(first, mine, sums[0:8])
                across = sums[8:16]
            else:
                across = far[:, lanes]
            for slot_side in range(2):
                out_ref[2 * other + slot_side, pl.ds(v * 8, 8), :] = jnp.where(side == slot_side, mine, across)


def inner_kernel(in_ref, local_ref, spread_ref, edge_response_ref, base_ref, states_ref, near_ref):
    run, tile, _ = place()
    tiles = [blocks_of(in_ref, 0), blocks_of(in_ref, 1)]
    for which in range(2):
        base_ref[which] = dot(spread_ref[...], tiles[which])
    states_ref[...] = dot(local_ref[run], jnp.concatenate(tiles, axis=0))
    near_ref[...] = dot(edge_hours(in_ref, 1 - tile), edge_response_ref[...])


def edge_flux(runs_ref, near, run, side, edge_gather, edge_response, edge_inject):
    lane = lanes_of()
    own = [runs_ref[2 * other + side, pl.ds(16, 8), :] for other in range(RUNS)]
    across = [runs_ref[2 * other + 1 - side, pl.ds(16, 8), :] for other in range(RUNS)]
    sums = []
    for parts in (own, across):
        total = jnp.zeros((ROWS, LANES), jnp.float32)
        for other in range(RUNS):
            total = jnp.where(lane // 8 == other, turn(parts[other], other * 8 - QUARTER), total)
        sums.append(total)
    far = jnp.concatenate([runs_ref[2 * run + 1 - side, pl.ds(v * 8, 8), :] for v in range(2)], axis=1)
    far = dot(far, edge_response)
    states = dot(jnp.concatenate(sums, axis=0), edge_gather)
    added = dot(states, edge_inject)
    row = lax.broadcasted_iota(jnp.int32, (ROWS, SPAN), 0)
    products = [part * pltpu.roll(part, 4, 0) for part in (near + added[0:8], far + added[8:16])]
    return jnp.where(row < 4, products[0], products[1])


def border_kernel(
    base_ref, states_ref, near_ref, runs_ref, gather_ref, inject_ref, edge_gather_ref, edge_response_ref, edge_inject_ref, out_ref
):
    run, tile, side = place()
    flux = edge_flux(
        runs_ref, near_ref[...], run, side, edge_gather_ref[run], edge_response_ref[...], edge_inject_ref[...]
    )
    runs = jnp.concatenate(
        [
            jnp.concatenate([runs_ref[2 * other + side, pl.ds(v * 8, 8), :] for other in range(RUNS)], axis=0)
            for v in range(3)
        ],
        axis=1,
    )
    states = dot(gather_ref[run], runs) + states_ref[...]
    first = lanes_of() < QUARTER
    for which in range(2):
        borders = base_ref[which] + dot(inject_ref[which], states)
        for j in range(GROUP):
            for v in range(3):
                value = borders[j * 8 : j * 8 + 8, v * LANES : (v + 1) * LANES]
                if v == 2:
                    half = flux[:, (j // 8) * LANES : (j // 8 + 1) * LANES]
                    value = jnp.where(first, value, turn(half, QUARTER - (j % 8) * HOURS))
                out_ref[2 * j + which, pl.ds(v * 8, 8), :] = value


def band_kernel(response_ref, mask_ref, borders_ref, press_hbm, flux_hbm, press_ref, flux_ref, states_ref, sems):
    _, tile, _ = place()
    column = lax.axis_index("col")
    even, odd = plan()["even"], plan()["odd"]
    lane = lanes_of()
    for k in range(8):
        for v in range(3):
            parts = [None] * 4
            for index, quarter in enumerate(QUARTERS):
                parts[quarter] = borders_ref[pl.ds(index * SLOT + v * 8 + k, ROWS, stride=4 * SLOT), :]
            if v < 2:
                for a, part in enumerate(transposed(parts, lane)):
                    states_ref[(4 * v + a) * 8 + k] = part
            else:
                total = parts[0]
                for quarter in range(1, 4):
                    total = jnp.where(lane // QUARTER == quarter, turn(parts[quarter], QUARTER * quarter), total)
                states_ref[64 + k] = total
    row = lax.broadcasted_iota(jnp.int32, (ROWS, LANES), 0)
    half = 0.5 * mask_ref[...].astype(jnp.float32)
    last = lane == LANES - 1
    halos = []
    for level in range(4):
        near = borders_ref[pl.ds(tile * SLOT + 16 + level, ROWS, stride=4 * SLOT), :]
        far = borders_ref[pl.ds(tile * SLOT + 20 + level, ROWS, stride=4 * SLOT), :]
        from_west = jnp.where(column == 0, 0.0, jnp.where(tile == 0, far, near))
        from_east = jnp.where(column == 2 * len(PAIRS) - 1, 0.0, jnp.where(tile == 0, near, far))
        halos.append((from_west, from_east))
    copies = []
    for early in range(HOURS // 2):
        late = HOURS - 1 - early
        banded = {early: [], late: []}
        for s in range(SERIES):
            states = [states_ref[s * 8 + k] for k in range(8)]
            sums = []
            for table, first in ((even, 0), (odd, 4)):
                total = float(table[early, 0]) * states[first]
                for k in range(1, 4):
                    total = total + float(table[early, k]) * states[first + k]
                sums.append(total)
            banded[early].append(response_ref[s, early] + (sums[0] + sums[1]))
            banded[late].append(response_ref[s, late] + (sums[0] - sums[1]))
        for hour in (early, late):
            u_all, p_all, v_all = (banded[hour][at : at + 3] for at in (0, 3, 6))
            for values in (u_all, v_all, p_all):
                values.append(last_level(values))
            for level in range(4):
                press_ref[level, hour] = p_all[level]
                fx = u_all[level] * p_all[level]
                fy = v_all[level] * p_all[level]
                from_west, from_east = halos[level]
                next_x = jnp.where(last, turn(from_east, LANES - 1 - QUARTER - hour), turn(fx, -1))
                prev_x = jnp.where(lane == 0, turn(from_west, -QUARTER - hour), turn(fx, 1))
                next_y = jnp.where(row == ROWS - 1, 0.0, pltpu.roll(fy, ROWS - 1, 0))
                prev_y = jnp.where(row == 0, 0.0, pltpu.roll(fy, 1, 0))
                flux_ref[level, hour] = half * ((next_x - prev_x) + (next_y - prev_y))
        if early % 2 == 1:
            for begin in (early - 1, late):
                for source, target in ((press_ref, press_hbm), (flux_ref, flux_hbm)):
                    copies.append(
                        pltpu.make_async_copy(
                            source.at[:, pl.ds(begin, 2)], target.at[:, pl.ds(begin, 2)], sems.at[len(copies)]
                        )
                    )
                    copies[-1].start()
    for copy in copies:
        copy.wait()


def swap(array, devices, columns):
    groups = [[tm * 8 + col for tm in some for col in pair] for some in devices for pair in columns]
    return lax.all_to_all(array, ("tm", "col"), 0, 0, tiled=True, axis_index_groups=groups)


VMEM = pl.BlockSpec(memory_space=pltpu.VMEM)
HBM = pl.BlockSpec(memory_space=pltpu.HBM)


def call(kernel, shapes, in_specs, scratch=(), out_spec=None, flops=10**6, moved=10**6):
    out_spec = VMEM if out_spec is None else out_spec
    return pl.pallas_call(
        kernel,
        out_shape=[jax.ShapeDtypeStruct(shape, jnp.float32) for shape in shapes],
        in_specs=in_specs,
        out_specs=[out_spec] * len(shapes),
        scratch_shapes=scratch,
        cost_estimate=pl.CostEstimate(flops=flops, bytes_accessed=moved, transcendentals=0),
        compiler_params=pltpu.CompilerParams(vmem_limit_bytes=32 * 1024 * 1024),
    )


def on_device(u_vel, v_vel, density, land_mask, start_hour, levels):
    tables = plan()
    whole = (4, HOURS, ROWS, LANES)
    series = (SERIES, HOURS, ROWS, LANES)
    slots = (OWNERS, SLOT, LANES)
    flat = (OWNERS * SLOT, LANES)
    runs = [[z * GROUP + j for j in range(GROUP)] for z in range(RUNS)]
    across = [[z * GROUP + j for z in range(RUNS)] for j in range(GROUP)]
    state_scratch = pltpu.VMEM((SERIES * 8, ROWS, LANES), jnp.float32)
    own, kept = call(
        summary_kernel,
        [flat, series],
        [HBM] * 6,
        [
            pltpu.SMEM((4,), jnp.int32),
            pltpu.VMEM(whole, jnp.float32),
            pltpu.VMEM(whole, jnp.float32),
            pltpu.VMEM(whole, jnp.float32),
            pltpu.VMEM((ROWS, LANES), jnp.int32),
            pltpu.VMEM((ROWS, LANES), jnp.int32),
            state_scratch,
            pltpu.SemaphoreType.DMA((6,)),
        ],
    )(levels, u_vel, v_vel, density, land_mask, start_hour)
    blocks = swap(own.reshape(slots), runs, PAIRS)
    (response,) = call(response_kernel, [series], [VMEM], flops=7 * 10**6)(kept)
    (totals,) = call(run_kernel, [(2 * RUNS, SLOT, LANES)], [VMEM] * 3)(blocks, tables["send"], tables["edge_sum"])
    totals = swap(totals, across, FAR)
    base, states, near = call(
        inner_kernel, [(2, GROUP * 8, 3 * LANES), (16, 3 * LANES), (ROWS, SPAN)], [VMEM] * 4, flops=3 * 10**7
    )(blocks, tables["local"], tables["spread"], tables["edge_response"])
    (borders,) = call(border_kernel, [slots], [VMEM] * 9)(
        base,
        states,
        near,
        totals,
        tables["gather"],
        tables["inject"],
        tables["edge_gather"],
        tables["edge_response"],
        tables["edge_inject"],
    )
    borders = swap(borders, runs, PAIRS).reshape(flat)
    pressure, flux = call(
        band_kernel,
        [whole, whole],
        [VMEM] * 3,
        [
            pltpu.VMEM(whole, jnp.float32),
            pltpu.VMEM(whole, jnp.float32),
            state_scratch,
            pltpu.SemaphoreType.DMA((HOURS,)),
        ],
        out_spec=HBM,
    )(response, land_mask, borders)
    return (pressure, flux)


def solution(mesh):
    return jax.shard_map(
        on_device,
        mesh=mesh,
        in_specs=(
            P(None, "tm", None, "col"),
            P(None, "tm", None, "col"),
            P(None, "tm", None, "col"),
            P(None, "col"),
            P(None, "col"),
            P(),
        ),
        out_specs=(P(None, "tm", None, "col"), P(None, "tm", None, "col")),
        check_vma=False,
    )
```

```python
import functools
import math

import jax
import jax.numpy as jnp
import numpy as np
from jax import lax
from jax.experimental import pallas as pl
from jax.experimental.pallas import tpu as pltpu
from jax.sharding import PartitionSpec as P

HOURS = 16
GROUP = 16
RUNS = 4
OWNERS = 2 * GROUP
SERIES = 9
ROWS = 8
LANES = 128
QUARTER = 32
SLOT = 24
SPAN = GROUP * HOURS
QUARTERS = (0, 3, 1, 2)
PAIRS = ((0, 1), (2, 3), (4, 5), (6, 7))
FAR = ((1, 2), (3, 4), (5, 6), (7, 0))
HIGH = lax.Precision.HIGHEST


def expand_roots(roots):
    coefficients = [complex(1.0, 0.0)]
    for root in roots:
        widened = coefficients + [complex(0.0, 0.0)]
        for position in range(1, len(widened)):
            widened[position] = widened[position] - root * coefficients[position - 1]
        coefficients = widened
    return [coefficient.real for coefficient in coefficients]


def horner_value(coefficients, point):
    running = complex(0.0, 0.0)
    for coefficient in coefficients:
        running = running * point + coefficient
    return running


def derive_coeffs(coefficients):
    degree = len(coefficients) - 1
    return [coefficients[position] * (degree - position) for position in range(degree)]


def filter_design():
    low_edge = 1.0 / 12.9
    high_edge = 1.0 / 12.0
    warped_low = 2.0 * math.tan(math.pi * low_edge)
    warped_high = 2.0 * math.tan(math.pi * high_edge)
    centre = math.sqrt(warped_low * warped_high)
    spread = warped_high - warped_low
    digital = []
    for octant in (3, 5):
        proto = complex(math.cos(octant * math.pi / 4.0), math.sin(octant * math.pi / 4.0)) * spread
        radical = (proto * proto - 4.0 * centre * centre) ** 0.5
        for analog in ((proto + radical) / 2.0, (proto - radical) / 2.0):
            digital.append((2.0 + analog) / (2.0 - analog))
    denom = expand_roots(digital)
    numer = [1.0, 0.0, -2.0, 0.0, 1.0]
    omega = 2.0 * math.atan(centre / 2.0)
    zcentre = complex(math.cos(omega), math.sin(omega))
    respond = horner_value(numer, zcentre) / horner_value(denom, zcentre)
    numer = [coefficient / abs(respond) for coefficient in numer]
    remain = [numer[position] - numer[0] * denom[position] for position in range(1, 5)]
    slope = derive_coeffs(denom)
    amat = np.zeros((4, 4))
    bvec = np.zeros(4)
    cvec = np.zeros(4)
    upper = [pole for pole in digital if pole.imag > 0]
    for index, pole in enumerate(upper):
        resid = horner_value(remain, pole) / horner_value(slope, pole)
        first = 2 * index
        amat[first, first] = pole.real
        amat[first, first + 1] = -pole.imag
        amat[first + 1, first] = pole.imag
        amat[first + 1, first + 1] = pole.real
        bvec[first] = 1.0
        cvec[first] = 2.0 * resid.real
        cvec[first + 1] = -2.0 * resid.imag
    return (amat, bvec, cvec, float(numer[0]))


def power(matrix, exponent):
    return np.linalg.matrix_power(matrix, exponent)


def power(matrix, exponent):
    return np.linalg.matrix_power(matrix, exponent)


def block_maps(hours):
    amat, bvec, cvec, direct = filter_design()
    impulse = [direct] + [float(cvec @ power(amat, step - 1) @ bvec) for step in range(1, hours)]
    toeplitz = np.zeros((hours, hours))
    for row in range(hours):
        for column in range(row + 1):
            toeplitz[row, column] = impulse[row - column]
    powers = [np.eye(4)]
    for hour in range(hours):
        powers.append(powers[-1] @ amat)
    left = np.stack([powers[hours - 1 - hour] @ bvec for hour in range(hours)], axis=1)
    entering = np.stack([cvec @ powers[hour] for hour in range(hours)], axis=0)
    back = np.stack([powers[hour] @ bvec for hour in range(hours)], axis=1)
    summary = np.concatenate([left, back @ toeplitz], axis=0)
    response = toeplitz.T @ toeplitz
    injected = np.concatenate([toeplitz.T @ entering, entering[::-1]], axis=1)
    return summary, back @ entering, powers[hours], response, injected


@functools.lru_cache(maxsize=None)
def plan():
    amat, bvec, cvec, direct = filter_design()
    summary, coupling, step, _, entering = block_maps(HOURS)
    basis = []
    for sign in (1.0, -1.0):
        part = np.linalg.svd(entering + sign * entering[::-1])[0][:, :4]
        basis.append(part)
    coordinates = np.concatenate(basis, axis=1).T @ entering
    own = GROUP * 8
    forward = np.zeros((GROUP + 1, 4, own + 8))
    forward[0][:, own : own + 4] = np.eye(4)
    for j in range(GROUP):
        forward[j + 1] = step @ forward[j]
        forward[j + 1][:, j * 8 : j * 8 + 4] += np.eye(4)
    backward = np.zeros((GROUP + 1, 4, own + 8))
    backward[GROUP][:, own + 4 :] = np.eye(4)
    for j in reversed(range(GROUP)):
        backward[j] = step @ backward[j + 1] + coupling @ forward[j]
        backward[j][:, j * 8 + 4 : j * 8 + 8] += np.eye(4)
    inner = np.zeros((own, own + 8))
    for j in range(GROUP):
        inner[j * 8 : j * 8 + 4] = forward[j]
        inner[j * 8 + 4 : j * 8 + 8] = backward[j + 1]
    run_left = forward[GROUP][:, :own]
    run_right = backward[0][:, :own]
    run_summary, run_coupling, run_step, response, injected = block_maps(SPAN)
    suffix = [np.zeros((4, 4))]
    for m in range(RUNS):
        suffix.append(suffix[-1] + power(run_step, m) @ run_coupling @ power(run_step, m))
    send = np.zeros((RUNS, 16, 2 * own))
    local = np.zeros((RUNS, 16, 2 * own))
    gather = np.zeros((RUNS, 16, RUNS * 8))
    edge_gather = np.zeros((RUNS, LANES, LANES))
    for z in range(RUNS):
        after = suffix[RUNS - 1 - z]
        for tile in range(2):
            columns = slice(tile * own, (tile + 1) * own)
            ahead = slice(4 * tile, 4 * tile + 4)
            behind = slice(8 + 4 * tile, 12 + 4 * tile)
            send[z, ahead, columns] = run_left
            send[z, behind, columns] = run_right + run_step @ after @ run_left
            local[z, behind, columns] = after @ run_left
            for other in range(RUNS):
                here = slice(other * 8 + 4 * tile, other * 8 + 4 * tile + 4)
                if other < z:
                    came = power(run_step, z - 1 - other)
                    gather[z, ahead, here] = came
                    gather[z, behind, here] = after @ run_step @ came
                if other > z:
                    gather[z, behind, here] = power(run_step, other - z - 1)
        for other in range(RUNS):
            from_left = slice(other * 8, other * 8 + 4)
            from_right = slice(other * 8 + 4, other * 8 + 8)
            if other < z:
                came = power(run_step, z - 1 - other)
                edge_gather[z, from_left, 0:4] = came.T
                edge_gather[z, from_left, 4:8] = (after @ run_step @ came).T
            if other == z:
                edge_gather[z, from_left, 4:8] = after.T
            if other > z:
                came = power(run_step, other - z - 1)
                edge_gather[z, from_right, 4:8] = came.T
                edge_gather[z, from_left, 4:8] = (came @ run_step @ suffix[RUNS - 1 - other]).T
    for j in range(GROUP):
        inner[j * 8 : j * 8 + 8] = coordinates @ inner[j * 8 : j * 8 + 8]
    spread = inner[:, :own]
    inject = np.zeros((2, own, 16))
    for tile in range(2):
        inject[tile, :, 4 * tile : 4 * tile + 4] = inner[:, own : own + 4]
        inject[tile, :, 8 + 4 * tile : 12 + 4 * tile] = inner[:, own + 4 :]
    edge_sum = np.zeros((SPAN, LANES))
    edge_sum[:, QUARTER : QUARTER + 8] = run_summary.T
    edge_response = response.T
    edge_inject = np.zeros((LANES, SPAN))
    edge_inject[:8] = injected.T
    tables = dict(
        send=send,
        local=local,
        gather=gather,
        spread=spread,
        inject=inject,
        edge_sum=edge_sum,
        edge_gather=edge_gather,
        edge_response=edge_response,
        edge_inject=edge_inject,
    )
    tables = {name: table.astype(np.float32) for name, table in tables.items()}
    return dict(tables, amat=amat, cvec=cvec, direct=direct, summary=summary, even=basis[0], odd=basis[1])


def place():
    tile = lax.axis_index("col") % 2
    return lax.axis_index("tm") // GROUP, tile, 1 - tile


def lanes_of(shape=(ROWS, LANES)):
    return lax.broadcasted_iota(jnp.int32, shape, 1)


def live_hours(mask, start):
    first = lax.axis_index("tm") * HOURS
    ocean = mask == 1
    return [jnp.where(ocean & (start <= first + hour), 1.0, 0.0) for hour in range(HOURS)]


def depths(levels_ref):
    out = []
    for level in range(4):
        number = jnp.full((ROWS, LANES), levels_ref[level], jnp.int32).astype(jnp.float32)
        out.append((number + number * number / 90.0) / 90.0)
    return out


def anomalies(field, live):
    mean = 0.25 * ((field[0] + field[1]) + (field[2] + field[3]))
    return [(field[level] - mean) * live for level in range(3)]


def pressures(rho, depth):
    press = [rho[0] * depth[0]]
    for level in range(1, 4):
        press.append(press[-1] + 0.5 * (rho[level - 1] + rho[level]) * (depth[level] - depth[level - 1]))
    return press


def last_level(values):
    return -((values[0] + values[1]) + values[2])


def turn(value, shift):
    shift = shift % LANES
    return value if shift == 0 else pltpu.roll(value, shift, 1)


def transposed(parts, lane):
    low = lane < 2 * QUARTER
    even = (lane // QUARTER) % 2 == 0
    halves = [None] * 4
    for i in range(2):
        first, second = parts[i], parts[i + 2]
        halves[i] = jnp.where(low, first, turn(second, 64))
        halves[i + 2] = jnp.where(low, turn(first, 64), second)
    out = [None] * 4
    for i in (0, 2):
        first, second = halves[i], halves[i + 1]
        out[i] = jnp.where(even, first, turn(second, QUARTER))
        out[i + 1] = jnp.where(even, turn(first, -QUARTER), second)
    return out


def summary_kernel(
    levels_hbm, u_hbm, v_hbm, rho_hbm, mask_hbm, start_hbm, out_ref, kept_ref, levels_ref, u_ref, v_ref, rho_ref, mask_ref, start_ref, sums_ref, sems
):
    summary = plan()["summary"]
    copies = [
        pltpu.make_async_copy(source, target, sems.at[index])
        for index, (source, target) in enumerate(
            (
                (mask_hbm, mask_ref),
                (start_hbm, start_ref),
                (levels_hbm, levels_ref),
                (u_hbm, u_ref),
                (rho_hbm, rho_ref),
                (v_hbm, v_ref),
            )
        )
    ]
    for copy in copies:
        copy.start()
    for copy in copies[:3]:
        copy.wait()
    live = live_hours(mask_ref[...], start_ref[...])
    depth = depths(levels_ref)
    lane = lanes_of()
    west = [jnp.zeros((ROWS, LANES), jnp.float32) for _ in range(8)]
    east = list(west)
    for which, ref in enumerate((u_ref, rho_ref, v_ref)):
        copies[3 + which].wait()
        sums = [[None] * 8 for _ in range(3)]
        for hour in range(HOURS):
            field = [ref[level, hour] for level in range(4)]
            if which == 1:
                field = pressures(field, depth)
            values = anomalies(field, live[hour])
            for level, value in enumerate(values):
                kept_ref[which * 3 + level, hour] = value
                for k in range(8):
                    term = float(summary[k, hour]) * value
                    sums[level][k] = term if hour == 0 else sums[level][k] + term
                if which < 2:
                    turned = turn(value, QUARTER + hour)
                    at = which * 4 + level
                    west[at] = jnp.where(lane == QUARTER + hour, turned, west[at])
                    east[at] = jnp.where(lane == QUARTER - 1 + hour, turned, east[at])
        for level in range(3):
            for k in range(8):
                sums_ref[(which * 3 + level) * 8 + k] = sums[level][k]
    for ends in (west, east):
        for at in (0, 4):
            ends[at + 3] = last_level(ends[at : at + 3])
    first = lane < QUARTER
    for k in range(8):
        for v in range(2):
            parts = transposed([sums_ref[(4 * v + a) * 8 + k] for a in range(4)], lane)
            for index, quarter in enumerate(QUARTERS):
                out_ref[pl.ds(index * SLOT + v * 8 + k, ROWS, stride=4 * SLOT), :] = parts[quarter]
        single = sums_ref[64 + k]
        others = {0: west[k], 3: turn(east[k], 1)}
        for index, quarter in enumerate(QUARTERS):
            part = jnp.where(first, turn(single, -QUARTER * quarter), others.get(quarter, 0.0))
            out_ref[pl.ds(index * SLOT + 16 + k, ROWS, stride=4 * SLOT), :] = part


def filter_steps(samples):
    amat, cvec, direct = plan()["amat"], plan()["cvec"], plan()["direct"]
    out = [direct * samples[0]]
    state = [samples[0], None, samples[0], None]
    for sample in samples[1:]:
        value = direct * sample
        for k in range(4):
            if state[k] is not None:
                value = value + float(cvec[k]) * state[k]
        out.append(value)
        fresh = []
        for first in (0, 2):
            real, imag = float(amat[first, first]), float(amat[first + 1, first])
            if state[first + 1] is None:
                fresh.append(real * state[first] + sample)
                fresh.append(imag * state[first])
            else:
                fresh.append((real * state[first] - imag * state[first + 1]) + sample)
                fresh.append(imag * state[first] + real * state[first + 1])
        state = fresh
    return out


def response_kernel(kept_ref, out_ref):
    def one(s, carry):
        samples = filter_steps([kept_ref[s, hour] for hour in range(HOURS)])
        samples = filter_steps(samples[::-1])[::-1]
        for hour in range(HOURS):
            out_ref[s, hour] = samples[hour]
        return carry

    lax.fori_loop(0, SERIES, one, 0)


def blocks_of(in_ref, tile):
    return jnp.concatenate(
        [
            jnp.concatenate([in_ref[2 * j + tile, pl.ds(v * 8, 8), :] for j in range(GROUP)], axis=0)
            for v in range(3)
        ],
        axis=1,
    )


def edge_hours(in_ref, tile):
    lane = lanes_of()
    halves = []
    for half in range(2):
        total = jnp.zeros((ROWS, LANES), jnp.float32)
        for i in range(8):
            turned = turn(in_ref[2 * (half * 8 + i) + tile, pl.ds(16, 8), :], i * HOURS - QUARTER)
            total = jnp.where(lane // HOURS == i, turned, total)
        halves.append(total)
    return jnp.concatenate(halves, axis=1)


def dot(lhs, rhs):
    return jnp.dot(lhs, rhs, precision=HIGH, preferred_element_type=jnp.float32)


def run_kernel(in_ref, send_ref, edge_sum_ref, out_ref):
    run, tile, side = place()
    blocks = jnp.concatenate([blocks_of(in_ref, 0), blocks_of(in_ref, 1)], axis=0)
    totals = dot(send_ref[run], blocks)
    near = edge_hours(in_ref, 1 - tile)
    far = edge_hours(in_ref, tile)
    sums = dot(jnp.concatenate([near, far], axis=0), edge_sum_ref[...])
    first = lanes_of() < QUARTER
    for other in range(RUNS):
        for v in range(3):
            lanes = slice(v * LANES, (v + 1) * LANES)
            mine = jnp.where(other > run, totals[0:8, lanes], totals[8:16, lanes])
            if v == 2:
                mine = jnp.where(first, mine, sums[0:8])
                across = sums[8:16]
            else:
                across = far[:, lanes]
            for slot_side in range(2):
                out_ref[2 * other + slot_side, pl.ds(v * 8, 8), :] = jnp.where(side == slot_side, mine, across)


def inner_kernel(in_ref, local_ref, spread_ref, edge_response_ref, base_ref, states_ref, near_ref):
    run, tile, _ = place()
    tiles = [blocks_of(in_ref, 0), blocks_of(in_ref, 1)]
    for which in range(2):
        base_ref[which] = dot(spread_ref[...], tiles[which])
    states_ref[...] = dot(local_ref[run], jnp.concatenate(tiles, axis=0))
    near_ref[...] = dot(edge_hours(in_ref, 1 - tile), edge_response_ref[...])


def edge_flux(runs_ref, near, run, side, edge_gather, edge_response, edge_inject):
    lane = lanes_of()
    own = [runs_ref[2 * other + side, pl.ds(16, 8), :] for other in range(RUNS)]
    across = [runs_ref[2 * other + 1 - side, pl.ds(16, 8), :] for other in range(RUNS)]
    sums = []
    for parts in (own, across):
        total = jnp.zeros((ROWS, LANES), jnp.float32)
        for other in range(RUNS):
            total = jnp.where(lane // 8 == other, turn(parts[other], other * 8 - QUARTER), total)
        sums.append(total)
    far = jnp.concatenate([runs_ref[2 * run + 1 - side, pl.ds(v * 8, 8), :] for v in range(2)], axis=1)
    far = dot(far, edge_response)
    states = dot(jnp.concatenate(sums, axis=0), edge_gather)
    added = dot(states, edge_inject)
    row = lax.broadcasted_iota(jnp.int32, (ROWS, SPAN), 0)
    products = [part * pltpu.roll(part, 4, 0) for part in (near + added[0:8], far + added[8:16])]
    return jnp.where(row < 4, products[0], products[1])


def border_kernel(
    base_ref, states_ref, near_ref, runs_ref, gather_ref, inject_ref, edge_gather_ref, edge_response_ref, edge_inject_ref, out_ref
):
    run, tile, side = place()
    flux = edge_flux(
        runs_ref, near_ref[...], run, side, edge_gather_ref[run], edge_response_ref[...], edge_inject_ref[...]
    )
    runs = jnp.concatenate(
        [
            jnp.concatenate([runs_ref[2 * other + side, pl.ds(v * 8, 8), :] for other in range(RUNS)], axis=0)
            for v in range(3)
        ],
        axis=1,
    )
    states = dot(gather_ref[run], runs) + states_ref[...]
    first = lanes_of() < QUARTER
    for which in range(2):
        borders = base_ref[which] + dot(inject_ref[which], states)
        for j in range(GROUP):
            for v in range(3):
                value = borders[j * 8 : j * 8 + 8, v * LANES : (v + 1) * LANES]
                if v == 2:
                    half = flux[:, (j // 8) * LANES : (j // 8 + 1) * LANES]
                    value = jnp.where(first, value, turn(half, QUARTER - (j % 8) * HOURS))
                out_ref[2 * j + which, pl.ds(v * 8, 8), :] = value


def band_kernel(response_ref, mask_ref, borders_ref, press_hbm, flux_hbm, press_ref, flux_ref, states_ref, sems):
    _, tile, _ = place()
    column = lax.axis_index("col")
    even, odd = plan()["even"], plan()["odd"]
    lane = lanes_of()
    for k in range(8):
        for v in range(3):
            parts = [None] * 4
            for index, quarter in enumerate(QUARTERS):
                parts[quarter] = borders_ref[pl.ds(index * SLOT + v * 8 + k, ROWS, stride=4 * SLOT), :]
            if v < 2:
                for a, part in enumerate(transposed(parts, lane)):
                    states_ref[(4 * v + a) * 8 + k] = part
            else:
                total = parts[0]
                for quarter in range(1, 4):
                    total = jnp.where(lane // QUARTER == quarter, turn(parts[quarter], QUARTER * quarter), total)
                states_ref[64 + k] = total
    row = lax.broadcasted_iota(jnp.int32, (ROWS, LANES), 0)
    half = 0.5 * mask_ref[...].astype(jnp.float32)
    last = lane == LANES - 1
    halos = []
    for level in range(4):
        near = borders_ref[pl.ds(tile * SLOT + 16 + level, ROWS, stride=4 * SLOT), :]
        far = borders_ref[pl.ds(tile * SLOT + 20 + level, ROWS, stride=4 * SLOT), :]
        from_west = jnp.where(column == 0, 0.0, jnp.where(tile == 0, far, near))
        from_east = jnp.where(column == 2 * len(PAIRS) - 1, 0.0, jnp.where(tile == 0, near, far))
        halos.append((from_west, from_east))
    copies = []
    for early in range(HOURS // 2):
        late = HOURS - 1 - early
        banded = {early: [], late: []}
        for s in range(SERIES):
            states = [states_ref[s * 8 + k] for k in range(8)]
            sums = []
            for table, first in ((even, 0), (odd, 4)):
                total = float(table[early, 0]) * states[first]
                for k in range(1, 4):
                    total = total + float(table[early, k]) * states[first + k]
                sums.append(total)
            banded[early].append(response_ref[s, early] + (sums[0] + sums[1]))
            banded[late].append(response_ref[s, late] + (sums[0] - sums[1]))
        for hour in (early, late):
            u_all, p_all, v_all = (banded[hour][at : at + 3] for at in (0, 3, 6))
            for values in (u_all, v_all, p_all):
                values.append(last_level(values))
            for level in range(4):
                press_ref[level, hour] = p_all[level]
                fx = u_all[level] * p_all[level]
                fy = v_all[level] * p_all[level]
                from_west, from_east = halos[level]
                next_x = jnp.where(last, turn(from_east, LANES - 1 - QUARTER - hour), turn(fx, -1))
                prev_x = jnp.where(lane == 0, turn(from_west, -QUARTER - hour), turn(fx, 1))
                next_y = jnp.where(row == ROWS - 1, 0.0, pltpu.roll(fy, ROWS - 1, 0))
                prev_y = jnp.where(row == 0, 0.0, pltpu.roll(fy, 1, 0))
                flux_ref[level, hour] = half * ((next_x - prev_x) + (next_y - prev_y))
        if early % 2 == 1:
            for begin in (early - 1, late):
                for source, target in ((press_ref, press_hbm), (flux_ref, flux_hbm)):
                    copies.append(
                        pltpu.make_async_copy(
                            source.at[:, pl.ds(begin, 2)], target.at[:, pl.ds(begin, 2)], sems.at[len(copies)]
                        )
                    )
                    copies[-1].start()
    for copy in copies:
        copy.wait()


def swap(array, devices, columns):
    groups = [[tm * 8 + col for tm in some for col in pair] for some in devices for pair in columns]
    return lax.all_to_all(array, ("tm", "col"), 0, 0, tiled=True, axis_index_groups=groups)


VMEM = pl.BlockSpec(memory_space=pltpu.VMEM)
HBM = pl.BlockSpec(memory_space=pltpu.HBM)


def call(kernel, shapes, in_specs, scratch=(), out_spec=None, flops=10**6, moved=10**6):
    out_spec = VMEM if out_spec is None else out_spec
    return pl.pallas_call(
        kernel,
        out_shape=[
            jax.ShapeDtypeStruct(shape, jnp.float32) if out_spec is HBM else pltpu.VMEM(shape, jnp.float32)
            for shape in shapes
        ],
        in_specs=in_specs,
        out_specs=[out_spec] * len(shapes),
        scratch_shapes=scratch,
        cost_estimate=pl.CostEstimate(flops=flops, bytes_accessed=moved, transcendentals=0),
        compiler_params=pltpu.CompilerParams(vmem_limit_bytes=32 * 1024 * 1024),
    )


def on_device(u_vel, v_vel, density, land_mask, start_hour, levels):
    tables = plan()
    whole = (4, HOURS, ROWS, LANES)
    series = (SERIES, HOURS, ROWS, LANES)
    slots = (OWNERS, SLOT, LANES)
    flat = (OWNERS * SLOT, LANES)
    runs = [[z * GROUP + j for j in range(GROUP)] for z in range(RUNS)]
    across = [[z * GROUP + j for z in range(RUNS)] for j in range(GROUP)]
    state_scratch = pltpu.VMEM((SERIES * 8, ROWS, LANES), jnp.float32)
    arguments = (levels, u_vel, v_vel, density, land_mask, start_hour)
    own, kept = call(
        summary_kernel,
        [flat, series],
        [HBM] * 6,
        [
            pltpu.SMEM((4,), jnp.int32),
            pltpu.VMEM(whole, jnp.float32),
            pltpu.VMEM(whole, jnp.float32),
            pltpu.VMEM(whole, jnp.float32),
            pltpu.VMEM((ROWS, LANES), jnp.int32),
            pltpu.VMEM((ROWS, LANES), jnp.int32),
            state_scratch,
            pltpu.SemaphoreType.DMA((6,)),
        ],
    )(*[pltpu.with_memory_space_constraint(array, pltpu.HBM) for array in arguments])
    blocks = swap(own.reshape(slots), runs, PAIRS)
    (response,) = call(response_kernel, [series], [VMEM], flops=7 * 10**6)(kept)
    (totals,) = call(run_kernel, [(2 * RUNS, SLOT, LANES)], [VMEM] * 3)(blocks, tables["send"], tables["edge_sum"])
    totals = swap(totals, across, FAR)
    base, states, near = call(
        inner_kernel, [(2, GROUP * 8, 3 * LANES), (16, 3 * LANES), (ROWS, SPAN)], [VMEM] * 4, flops=3 * 10**7
    )(blocks, tables["local"], tables["spread"], tables["edge_response"])
    (borders,) = call(border_kernel, [slots], [VMEM] * 9)(
        base,
        states,
        near,
        totals,
        tables["gather"],
        tables["inject"],
        tables["edge_gather"],
        tables["edge_response"],
        tables["edge_inject"],
    )
    borders = swap(borders, runs, PAIRS).reshape(flat)
    pressure, flux = call(
        band_kernel,
        [whole, whole],
        [VMEM] * 3,
        [
            pltpu.VMEM(whole, jnp.float32),
            pltpu.VMEM(whole, jnp.float32),
            state_scratch,
            pltpu.SemaphoreType.DMA((HOURS,)),
        ],
        out_spec=HBM,
    )(response, land_mask, borders)
    return (pressure, flux)


def solution(mesh):
    return jax.shard_map(
        on_device,
        mesh=mesh,
        in_specs=(
            P(None, "tm", None, "col"),
            P(None, "tm", None, "col"),
            P(None, "tm", None, "col"),
            P(None, "col"),
            P(None, "col"),
            P(),
        ),
        out_specs=(P(None, "tm", None, "col"), P(None, "tm", None, "col")),
        check_vma=False,
    )
```

```python
import functools
import math

import jax
import jax.numpy as jnp
import numpy as np
from jax import lax
from jax.experimental import pallas as pl
from jax.experimental.pallas import tpu as pltpu
from jax.sharding import PartitionSpec as P

HOURS = 16
GROUP = 16
RUNS = 4
OWNERS = 2 * GROUP
SERIES = 9
ROWS = 8
LANES = 128
QUARTER = 32
SLOT = 19
SPAN = GROUP * HOURS
QUARTERS = (0, 3, 1, 2)
PAIRS = ((0, 1), (2, 3), (4, 5), (6, 7))
FAR = ((1, 2), (3, 4), (5, 6), (7, 0))
HIGH = lax.Precision.HIGHEST


def expand_roots(roots):
    coefficients = [complex(1.0, 0.0)]
    for root in roots:
        widened = coefficients + [complex(0.0, 0.0)]
        for position in range(1, len(widened)):
            widened[position] = widened[position] - root * coefficients[position - 1]
        coefficients = widened
    return [coefficient.real for coefficient in coefficients]


def horner_value(coefficients, point):
    running = complex(0.0, 0.0)
    for coefficient in coefficients:
        running = running * point + coefficient
    return running


def derive_coeffs(coefficients):
    degree = len(coefficients) - 1
    return [coefficients[position] * (degree - position) for position in range(degree)]


def filter_design():
    low_edge = 1.0 / 12.9
    high_edge = 1.0 / 12.0
    warped_low = 2.0 * math.tan(math.pi * low_edge)
    warped_high = 2.0 * math.tan(math.pi * high_edge)
    centre = math.sqrt(warped_low * warped_high)
    spread = warped_high - warped_low
    digital = []
    for octant in (3, 5):
        proto = complex(math.cos(octant * math.pi / 4.0), math.sin(octant * math.pi / 4.0)) * spread
        radical = (proto * proto - 4.0 * centre * centre) ** 0.5
        for analog in ((proto + radical) / 2.0, (proto - radical) / 2.0):
            digital.append((2.0 + analog) / (2.0 - analog))
    denom = expand_roots(digital)
    numer = [1.0, 0.0, -2.0, 0.0, 1.0]
    omega = 2.0 * math.atan(centre / 2.0)
    zcentre = complex(math.cos(omega), math.sin(omega))
    respond = horner_value(numer, zcentre) / horner_value(denom, zcentre)
    numer = [coefficient / abs(respond) for coefficient in numer]
    remain = [numer[position] - numer[0] * denom[position] for position in range(1, 5)]
    slope = derive_coeffs(denom)
    amat = np.zeros((4, 4))
    bvec = np.zeros(4)
    cvec = np.zeros(4)
    upper = [pole for pole in digital if pole.imag > 0]
    for index, pole in enumerate(upper):
        resid = horner_value(remain, pole) / horner_value(slope, pole)
        first = 2 * index
        amat[first, first] = pole.real
        amat[first, first + 1] = -pole.imag
        amat[first + 1, first] = pole.imag
        amat[first + 1, first + 1] = pole.real
        bvec[first] = 1.0
        cvec[first] = 2.0 * resid.real
        cvec[first + 1] = -2.0 * resid.imag
    return (amat, bvec, cvec, float(numer[0]))


def power(matrix, exponent):
    return np.linalg.matrix_power(matrix, exponent)


def power(matrix, exponent):
    return np.linalg.matrix_power(matrix, exponent)


def block_maps(hours):
    amat, bvec, cvec, direct = filter_design()
    impulse = [direct] + [float(cvec @ power(amat, step - 1) @ bvec) for step in range(1, hours)]
    toeplitz = np.zeros((hours, hours))
    for row in range(hours):
        for column in range(row + 1):
            toeplitz[row, column] = impulse[row - column]
    powers = [np.eye(4)]
    for hour in range(hours):
        powers.append(powers[-1] @ amat)
    left = np.stack([powers[hours - 1 - hour] @ bvec for hour in range(hours)], axis=1)
    entering = np.stack([cvec @ powers[hour] for hour in range(hours)], axis=0)
    back = np.stack([powers[hour] @ bvec for hour in range(hours)], axis=1)
    summary = np.concatenate([left, back @ toeplitz], axis=0)
    response = toeplitz.T @ toeplitz
    injected = np.concatenate([toeplitz.T @ entering, entering[::-1]], axis=1)
    return summary, back @ entering, powers[hours], response, injected


def direct_form():
    amat, _, cvec, _ = filter_design()
    denom = np.poly(amat)
    outputs = [cvec @ power(amat, hour) for hour in range(4)]
    rows = [sum(denom[lag] * outputs[row - lag] for lag in range(row + 1)) for row in range(4)]
    return denom, np.stack(rows)


@functools.lru_cache(maxsize=None)
def plan():
    gain = filter_design()[3]
    scale = gain * gain
    denom, to_direct = direct_form()
    summary, coupling, step, _, _ = block_maps(HOURS)
    own = GROUP * 8
    forward = np.zeros((GROUP + 1, 4, own + 8))
    forward[0][:, own : own + 4] = np.eye(4)
    for j in range(GROUP):
        forward[j + 1] = step @ forward[j]
        forward[j + 1][:, j * 8 : j * 8 + 4] += np.eye(4)
    backward = np.zeros((GROUP + 1, 4, own + 8))
    backward[GROUP][:, own + 4 :] = np.eye(4)
    for j in reversed(range(GROUP)):
        backward[j] = step @ backward[j + 1] + coupling @ forward[j]
        backward[j][:, j * 8 + 4 : j * 8 + 8] += np.eye(4)
    inner = np.zeros((own, own + 8))
    for j in range(GROUP):
        inner[j * 8 : j * 8 + 4] = gain * to_direct @ forward[j]
        inner[j * 8 + 4 : j * 8 + 8] = to_direct @ backward[j + 1]
    run_left = forward[GROUP][:, :own]
    run_right = backward[0][:, :own]
    run_summary, run_coupling, run_step, response, injected = block_maps(SPAN)
    swapped = [j * 8 + k for k in range(8) for j in range(GROUP)]
    suffix = [np.zeros((4, 4))]
    for m in range(RUNS):
        suffix.append(suffix[-1] + power(run_step, m) @ run_coupling @ power(run_step, m))
    send = np.zeros((RUNS, 16, 2 * own))
    local = np.zeros((RUNS, 16, 2 * own))
    gather = np.zeros((RUNS, 16, RUNS * 8))
    send_ninth = np.zeros((RUNS, 16, own))
    local_ninth = np.zeros((RUNS, 16, own))
    edge_gather = np.zeros((RUNS, LANES, LANES))
    for z in range(RUNS):
        after = suffix[RUNS - 1 - z]
        right = run_right + run_step @ after @ run_left
        send_ninth[z, 0:4] = run_left[:, swapped]
        send_ninth[z, 8:12] = right[:, swapped]
        local_ninth[z, 8:12] = (after @ run_left)[:, swapped]
        for tile in range(2):
            columns = slice(tile * own, (tile + 1) * own)
            ahead = slice(4 * tile, 4 * tile + 4)
            behind = slice(8 + 4 * tile, 12 + 4 * tile)
            send[z, ahead, columns] = run_left
            send[z, behind, columns] = right
            local[z, behind, columns] = after @ run_left
            for other in range(RUNS):
                here = slice(other * 8 + 4 * tile, other * 8 + 4 * tile + 4)
                if other < z:
                    came = power(run_step, z - 1 - other)
                    gather[z, ahead, here] = came
                    gather[z, behind, here] = after @ run_step @ came
                if other > z:
                    gather[z, behind, here] = power(run_step, other - z - 1)
        for other in range(RUNS):
            from_left = slice(other * 8, other * 8 + 4)
            from_right = slice(other * 8 + 4, other * 8 + 8)
            if other < z:
                came = power(run_step, z - 1 - other)
                edge_gather[z, from_left, 0:4] = came.T
                edge_gather[z, from_left, 4:8] = (after @ run_step @ came).T
            if other == z:
                edge_gather[z, from_left, 4:8] = after.T
            if other > z:
                came = power(run_step, other - z - 1)
                edge_gather[z, from_right, 4:8] = came.T
                edge_gather[z, from_left, 4:8] = (came @ run_step @ suffix[RUNS - 1 - other]).T
    spread = inner[:, :own]
    inject = np.zeros((2, own, 16))
    for tile in range(2):
        inject[tile, :, 4 * tile : 4 * tile + 4] = inner[:, own : own + 4]
        inject[tile, :, 8 + 4 * tile : 12 + 4 * tile] = inner[:, own + 4 :]
    edge_sum = np.zeros((SPAN, LANES))
    edge_sum[:, 2 * QUARTER : 2 * QUARTER + 8] = run_summary.T / scale
    order = [(j // 8) * 8 + (8 - j % 8) % 8 for j in range(GROUP)]
    places = [order[j] * HOURS + hour for j in range(GROUP) for hour in range(HOURS)]
    edge_out = np.zeros((SPAN + LANES, SPAN))
    edge_out[:SPAN, places] = response.T / scale
    edge_out[SPAN : SPAN + 8, places] = injected.T
    tables = dict(
        send=send,
        local=local,
        gather=gather,
        spread=spread,
        inject=inject,
        send_ninth=send_ninth,
        local_ninth=local_ninth,
        spread_ninth=spread[swapped][:, swapped],
        inject_ninth=inject[0][swapped],
        edge_sum=edge_sum,
        edge_gather=edge_gather,
        edge_out=edge_out,
    )
    tables = {name: table.astype(np.float32) for name, table in tables.items()}
    return dict(tables, denom=denom, scale=scale, summary=summary / scale)


def place():
    tile = lax.axis_index("col") % 2
    return lax.axis_index("tm") // GROUP, tile, 1 - tile


def lanes_of(shape=(ROWS, LANES)):
    return lax.broadcasted_iota(jnp.int32, shape, 1)


def live_hours(mask, start, scale):
    first = lax.axis_index("tm") * HOURS
    ocean = mask == 1
    return [jnp.where(ocean & (start <= first + hour), scale, 0.0) for hour in range(HOURS)]


def depths(levels_ref):
    out = []
    for level in range(4):
        number = jnp.full((ROWS, LANES), levels_ref[level], jnp.int32).astype(jnp.float32)
        out.append((number + number * number / 90.0) / 90.0)
    return out


def anomalies(field, live):
    mean = 0.25 * ((field[0] + field[1]) + (field[2] + field[3]))
    return [(field[level] - mean) * live for level in range(3)]


def pressures(rho, depth):
    press = [rho[0] * depth[0]]
    for level in range(1, 4):
        press.append(press[-1] + 0.5 * (rho[level - 1] + rho[level]) * (depth[level] - depth[level - 1]))
    return press


def last_level(values):
    return -((values[0] + values[1]) + values[2])


def turn(value, shift):
    shift = shift % LANES
    return value if shift == 0 else pltpu.roll(value, shift, 1)


def transposed(parts, lane):
    low = lane < 2 * QUARTER
    even = (lane // QUARTER) % 2 == 0
    halves = [None] * 4
    for i in range(2):
        first, second = parts[i], parts[i + 2]
        halves[i] = jnp.where(low, first, turn(second, 64))
        halves[i + 2] = jnp.where(low, turn(first, 64), second)
    out = [None] * 4
    for i in (0, 2):
        first, second = halves[i], halves[i + 1]
        out[i] = jnp.where(even, first, turn(second, QUARTER))
        out[i + 1] = jnp.where(even, turn(first, -QUARTER), second)
    return out


def block_transposed(value, lane):
    value = pltpu.roll(value, 0, 1, stride=HOURS, stride_axis=0)
    total = value
    for block in range(1, 8):
        total = jnp.where(lane // HOURS == block, pltpu.roll(value, 8 - block, 0), total)
    return pltpu.roll(total, 0, 1, stride=HOURS, stride_axis=0)


def summary_kernel(
    levels_hbm, u_hbm, v_hbm, rho_hbm, mask_hbm, start_hbm, out_ref, kept_ref, levels_ref, u_ref, v_ref, rho_ref, mask_ref, start_ref, sums_ref, sems
):
    summary, scale = plan()["summary"], float(plan()["scale"])
    copies = [
        pltpu.make_async_copy(source, target, sems.at[index])
        for index, (source, target) in enumerate(
            (
                (mask_hbm, mask_ref),
                (start_hbm, start_ref),
                (levels_hbm, levels_ref),
                (u_hbm, u_ref),
                (rho_hbm, rho_ref),
                (v_hbm, v_ref),
            )
        )
    ]
    for copy in copies:
        copy.start()
    for copy in copies[:3]:
        copy.wait()
    live = live_hours(mask_ref[...], start_ref[...], scale)
    depth = depths(levels_ref)
    lane = lanes_of()
    west = jnp.zeros((ROWS, LANES), jnp.float32)
    east = west
    for which, ref in enumerate((u_ref, rho_ref, v_ref)):
        copies[3 + which].wait()
        sums = [[None] * 8 for _ in range(3)]
        for hour in range(HOURS):
            field = [ref[level, hour] for level in range(4)]
            if which == 1:
                field = pressures(field, depth)
            values = anomalies(field, live[hour])
            for level, value in enumerate(values):
                kept_ref[which * 3 + level, hour] = value
                for k in range(8):
                    term = float(summary[k, hour]) * value
                    sums[level][k] = term if hour == 0 else sums[level][k] + term
                if which < 2:
                    position = (8 - which * 4 - level) % 8 * HOURS + hour
                    turned = turn(value, position)
                    west = jnp.where(lane == position, turned, west)
                    east = jnp.where(lane == (position - 1) % LANES, turned, east)
        for level in range(3):
            for k in range(8):
                sums_ref[(which * 3 + level) * 8 + k] = sums[level][k]
    edges = []
    for ends in (west, turn(east, 1)):
        three = -((turn(ends, -HOURS) + turn(ends, -2 * HOURS)) + turn(ends, -3 * HOURS))
        block = lane // HOURS
        edges.append(jnp.where((block == 5) | (block == 1), three, ends))
    spare = {0: edges[0], 3: edges[1]}
    for v in range(2):
        for k in range(8):
            parts = transposed([sums_ref[(4 * v + a) * 8 + k] for a in range(4)], lane)
            for index, quarter in enumerate(QUARTERS):
                out_ref[pl.ds(index * SLOT + v * 8 + k, ROWS, stride=4 * SLOT), :] = parts[quarter]
        parts = transposed([sums_ref[64 + 4 * v + a] for a in range(4)], lane)
        for index, quarter in enumerate(QUARTERS):
            out_ref[pl.ds(index * SLOT + 16 + v, ROWS, stride=4 * SLOT), :] = parts[quarter]
    for index, quarter in enumerate(QUARTERS):
        out_ref[pl.ds(index * SLOT + 18, ROWS, stride=4 * SLOT), :] = spare.get(
            quarter, jnp.zeros((ROWS, LANES), jnp.float32)
        )


def blocks_of(in_ref, tile):
    return jnp.concatenate(
        [
            jnp.concatenate([in_ref[pl.ds((2 * j + tile) * SLOT + v * 8, 8), :] for j in range(GROUP)], axis=0)
            for v in range(2)
        ],
        axis=1,
    )


def ninth_of(in_ref):
    first = lanes_of((GROUP, LANES)) < QUARTER
    parts = []
    for half in range(2):
        tiles = [in_ref[pl.ds(tile * SLOT + 16 + half, GROUP, stride=2 * SLOT), :] for tile in range(2)]
        for a in range(4):
            parts.append(jnp.where(first, turn(tiles[0], -QUARTER * a), turn(tiles[1], QUARTER - QUARTER * a)))
    return jnp.concatenate(parts, axis=0)


def edge_hours(in_ref, tile):
    lane = lanes_of()
    rows = in_ref[pl.ds(tile * SLOT + 18, GROUP, stride=2 * SLOT), :]
    return jnp.concatenate([block_transposed(rows[half * 8 : half * 8 + 8], lane) for half in range(2)], axis=1)


def dot(lhs, rhs):
    return jnp.dot(lhs, rhs, precision=HIGH, preferred_element_type=jnp.float32)


def run_kernel(in_ref, send_ref, send_ninth_ref, edge_sum_ref, out_ref):
    run, tile, side = place()
    blocks = jnp.concatenate([blocks_of(in_ref, 0), blocks_of(in_ref, 1)], axis=0)
    totals = dot(send_ref[run], blocks)
    ninth = dot(send_ninth_ref[run], ninth_of(in_ref))
    near = edge_hours(in_ref, 1 - tile)
    far = edge_hours(in_ref, tile)
    sums = dot(jnp.concatenate([near, far], axis=0), edge_sum_ref[...])
    first = lanes_of() < 2 * QUARTER
    for other in range(RUNS):
        for v in range(3):
            lanes = slice(v * LANES, (v + 1) * LANES)
            if v == 2:
                mine = jnp.where(first, jnp.where(other > run, ninth[0:8], ninth[8:16]), sums[0:8])
                across = sums[8:16]
            else:
                mine = jnp.where(other > run, totals[0:8, lanes], totals[8:16, lanes])
                across = far[:, lanes]
            for slot_side in range(2):
                out_ref[2 * other + slot_side, pl.ds(v * 8, 8), :] = jnp.where(side == slot_side, mine, across)


def edge_flux(in_ref, runs_ref, run, tile, side, edge_gather, edge_out):
    lane = lanes_of()
    own = [runs_ref[2 * other + side, pl.ds(16, 8), :] for other in range(RUNS)]
    across = [runs_ref[2 * other + 1 - side, pl.ds(16, 8), :] for other in range(RUNS)]
    sums = []
    for parts in (own, across):
        total = jnp.zeros((ROWS, LANES), jnp.float32)
        for other in range(RUNS):
            total = jnp.where(lane // 8 == other, turn(parts[other], other * 8 - 2 * QUARTER), total)
        sums.append(total)
    states = dot(jnp.concatenate(sums, axis=0), edge_gather)
    near = edge_hours(in_ref, 1 - tile)
    far = jnp.concatenate([runs_ref[2 * run + 1 - side, pl.ds(v * 8, 8), :] for v in range(2)], axis=1)
    hours = jnp.concatenate([near, far], axis=0)
    banded = dot(jnp.concatenate([hours, states], axis=1), edge_out)
    row = lax.broadcasted_iota(jnp.int32, (ROWS, SPAN), 0)
    products = [part * pltpu.roll(part, 4, 0) for part in (banded[0:8], banded[8:16])]
    flux = jnp.where(row < 4, products[0], products[1])
    return jnp.concatenate(
        [block_transposed(flux[:, half * LANES : (half + 1) * LANES], lane) for half in range(2)], axis=0
    )


def border_kernel(
    in_ref,
    runs_ref,
    gather_ref,
    local_ref,
    spread_ref,
    inject_ref,
    local_ninth_ref,
    spread_ninth_ref,
    inject_ninth_ref,
    edge_gather_ref,
    edge_out_ref,
    out_ref,
):
    run, tile, side = place()
    flux = edge_flux(in_ref, runs_ref, run, tile, side, edge_gather_ref[run], edge_out_ref[...])
    runs = [
        jnp.concatenate([runs_ref[2 * other + side, pl.ds(v * 8, 8), :] for other in range(RUNS)], axis=0)
        for v in range(3)
    ]
    gather = dot(gather_ref[run], jnp.concatenate(runs, axis=1))
    tiles = [blocks_of(in_ref, 0), blocks_of(in_ref, 1)]
    states = gather[:, : 2 * LANES] + dot(local_ref[run], jnp.concatenate(tiles, axis=0))
    for which in range(2):
        borders = dot(spread_ref[...], tiles[which]) + dot(inject_ref[which], states)
        for j in range(GROUP):
            for v in range(2):
                out_ref[pl.ds((2 * j + which) * SLOT + v * 8, 8), :] = borders[
                    j * 8 : j * 8 + 8, v * LANES : (v + 1) * LANES
                ]
        out_ref[pl.ds(which * SLOT + 18, GROUP, stride=2 * SLOT), :] = flux
    ninth = ninth_of(in_ref)
    states = gather[:, 2 * LANES :] + dot(local_ninth_ref[run], ninth)
    borders = dot(spread_ninth_ref[...], ninth) + dot(inject_ninth_ref[...], states)
    block = lanes_of((GROUP, LANES)) // QUARTER
    for which in range(2):
        for half in range(2):
            total = jnp.zeros((GROUP, LANES), jnp.float32)
            for a in range(4):
                row = (half * 4 + a) * GROUP
                total = jnp.where(block == a, turn(borders[row : row + GROUP], QUARTER * (a - which)), total)
            out_ref[pl.ds(which * SLOT + 16 + half, GROUP, stride=2 * SLOT), :] = total


def filter_steps(state, samples):
    _, one, two, three, four = (float(value) for value in plan()["denom"])
    first, second, third, fourth = state
    out = []
    for sample in samples:
        value = sample + first
        out.append(value)
        first = second - one * value
        second = (third - (sample + sample)) - two * value
        third = fourth - three * value
        fourth = sample - four * value
    return out


def band_kernel(
    kept_ref, mask_ref, borders_ref, press_hbm, flux_hbm, press_ref, flux_ref, east_ref, north_ref, states_ref, sems
):
    _, tile, _ = place()
    column = lax.axis_index("col")
    lane = lanes_of()
    for v in range(2):
        for k in range(8):
            parts = [None] * 4
            for index, quarter in enumerate(QUARTERS):
                parts[quarter] = borders_ref[pl.ds(index * SLOT + v * 8 + k, ROWS, stride=4 * SLOT), :]
            for a, part in enumerate(transposed(parts, lane)):
                states_ref[(4 * v + a) * 8 + k] = part
        for index, quarter in enumerate(QUARTERS):
            parts[quarter] = borders_ref[pl.ds(index * SLOT + 16 + v, ROWS, stride=4 * SLOT), :]
        for a, part in enumerate(transposed(parts, lane)):
            states_ref[64 + 4 * v + a] = part
    copies = []

    def send(source, target):
        copies.append(pltpu.make_async_copy(source, target, sems.at[len(copies)]))
        copies[-1].start()

    for which, target in ((1, press_ref), (0, east_ref), (2, north_ref)):
        for level in range(3):
            s = which * 3 + level
            states = [states_ref[s * 8 + k] for k in range(8)]
            samples = filter_steps(states[:4], [kept_ref[s, hour] for hour in range(HOURS)])
            samples = filter_steps(states[4:], samples[::-1])[::-1]
            for hour in range(HOURS):
                target[level, hour] = samples[hour]
        if which == 1:
            for hour in range(HOURS):
                press_ref[3, hour] = last_level([press_ref[level, hour] for level in range(3)])
            send(press_ref, press_hbm)
    row = lax.broadcasted_iota(jnp.int32, (ROWS, LANES), 0)
    half = 0.5 * mask_ref[...].astype(jnp.float32)
    last = lane == LANES - 1
    halos = borders_ref[pl.ds(tile * SLOT + 18, ROWS, stride=4 * SLOT), :]
    halos = jnp.where(tile == 0, turn(halos, 64), halos)
    outside = ((column == 0) & (lane < 64)) | ((column == 2 * len(PAIRS) - 1) & (lane >= 64))
    halos = jnp.where(outside, 0.0, halos)
    for hour in range(HOURS):
        u_all = [east_ref[level, hour] for level in range(3)]
        v_all = [north_ref[level, hour] for level in range(3)]
        p_all = [press_ref[level, hour] for level in range(4)]
        for values in (u_all, v_all):
            values.append(last_level(values))
        for level in range(4):
            fx = u_all[level] * p_all[level]
            fy = v_all[level] * p_all[level]
            position = level * HOURS + hour
            next_x = jnp.where(last, turn(halos, LANES - 1 - 64 - position), turn(fx, -1))
            prev_x = jnp.where(lane == 0, turn(halos, -position), turn(fx, 1))
            next_y = jnp.where(row == ROWS - 1, 0.0, pltpu.roll(fy, ROWS - 1, 0))
            prev_y = jnp.where(row == 0, 0.0, pltpu.roll(fy, 1, 0))
            flux_ref[level, hour] = half * ((next_x - prev_x) + (next_y - prev_y))
        if hour % 4 == 3:
            send(flux_ref.at[:, pl.ds(hour - 3, 4)], flux_hbm.at[:, pl.ds(hour - 3, 4)])
    for copy in copies:
        copy.wait()


def swap(array, devices, columns):
    groups = [[tm * 8 + col for tm in some for col in pair] for some in devices for pair in columns]
    return lax.all_to_all(array, ("tm", "col"), 0, 0, tiled=True, axis_index_groups=groups)


VMEM = pl.BlockSpec(memory_space=pltpu.VMEM)
HBM = pl.BlockSpec(memory_space=pltpu.HBM)


def call(kernel, shapes, in_specs, scratch=(), out_spec=VMEM):
    return pl.pallas_call(
        kernel,
        out_shape=[
            jax.ShapeDtypeStruct(shape, jnp.float32) if out_spec is HBM else pltpu.VMEM(shape, jnp.float32)
            for shape in shapes
        ],
        in_specs=in_specs,
        out_specs=[out_spec] * len(shapes),
        scratch_shapes=scratch,
        compiler_params=pltpu.CompilerParams(vmem_limit_bytes=32 * 1024 * 1024),
    )


def on_device(u_vel, v_vel, density, land_mask, start_hour, levels):
    tables = plan()
    whole = (4, HOURS, ROWS, LANES)
    part = (3, HOURS, ROWS, LANES)
    flat = (OWNERS * SLOT, LANES)
    slots = (OWNERS, 1, SLOT * LANES)
    runs = [[z * GROUP + j for j in range(GROUP)] for z in range(RUNS)]
    across = [[z * GROUP + j for z in range(RUNS)] for j in range(GROUP)]
    state_scratch = pltpu.VMEM((SERIES * 8, ROWS, LANES), jnp.float32)
    arguments = (levels, u_vel, v_vel, density, land_mask, start_hour)
    own, kept = call(
        summary_kernel,
        [flat, (SERIES, HOURS, ROWS, LANES)],
        [HBM] * 6,
        [
            pltpu.SMEM((4,), jnp.int32),
            pltpu.VMEM(whole, jnp.float32),
            pltpu.VMEM(whole, jnp.float32),
            pltpu.VMEM(whole, jnp.float32),
            pltpu.VMEM((ROWS, LANES), jnp.int32),
            pltpu.VMEM((ROWS, LANES), jnp.int32),
            state_scratch,
            pltpu.SemaphoreType.DMA((6,)),
        ],
    )(*[pltpu.with_memory_space_constraint(array, pltpu.HBM) for array in arguments])
    blocks = swap(own.reshape(slots), runs, PAIRS).reshape(flat)
    (totals,) = call(run_kernel, [(2 * RUNS, 24, LANES)], [VMEM] * 4)(
        blocks, tables["send"], tables["send_ninth"], tables["edge_sum"]
    )
    totals = swap(totals, across, FAR)
    names = (
        "gather",
        "local",
        "spread",
        "inject",
        "local_ninth",
        "spread_ninth",
        "inject_ninth",
        "edge_gather",
        "edge_out",
    )
    (borders,) = call(border_kernel, [flat], [VMEM] * (2 + len(names)))(
        blocks, totals, *[tables[name] for name in names]
    )
    borders = swap(borders.reshape(slots), runs, PAIRS).reshape(flat)
    pressure, flux = call(
        band_kernel,
        [whole, whole],
        [VMEM] * 3,
        [
            pltpu.VMEM(whole, jnp.float32),
            pltpu.VMEM(whole, jnp.float32),
            pltpu.VMEM(part, jnp.float32),
            pltpu.VMEM(part, jnp.float32),
            state_scratch,
            pltpu.SemaphoreType.DMA((5,)),
        ],
        out_spec=HBM,
    )(kept, land_mask, borders)
    return (pressure, flux)


def solution(mesh):
    return jax.shard_map(
        on_device,
        mesh=mesh,
        in_specs=(
            P(None, "tm", None, "col"),
            P(None, "tm", None, "col"),
            P(None, "tm", None, "col"),
            P(None, "col"),
            P(None, "col"),
            P(),
        ),
        out_specs=(P(None, "tm", None, "col"), P(None, "tm", None, "col")),
        check_vma=False,
    )
```

```python
import functools
import math

import jax
import jax.numpy as jnp
import ml_dtypes
import numpy as np
from jax import lax
from jax.experimental import pallas as pl
from jax.experimental.pallas import tpu as pltpu
from jax.sharding import PartitionSpec as P

HOURS = 16
GROUP = 16
RUNS = 4
OWNERS = 2 * GROUP
SERIES = 9
ROWS = 8
LANES = 128
QUARTER = 32
SLOT = 19
SPAN = GROUP * HOURS
QUARTERS = (0, 3, 1, 2)
PAIRS = ((0, 1), (2, 3), (4, 5), (6, 7))
FAR = ((1, 2), (3, 4), (5, 6), (7, 0))
HIGH = lax.Precision.HIGHEST


def expand_roots(roots):
    coefficients = [complex(1.0, 0.0)]
    for root in roots:
        widened = coefficients + [complex(0.0, 0.0)]
        for position in range(1, len(widened)):
            widened[position] = widened[position] - root * coefficients[position - 1]
        coefficients = widened
    return [coefficient.real for coefficient in coefficients]


def horner_value(coefficients, point):
    running = complex(0.0, 0.0)
    for coefficient in coefficients:
        running = running * point + coefficient
    return running


def derive_coeffs(coefficients):
    degree = len(coefficients) - 1
    return [coefficients[position] * (degree - position) for position in range(degree)]


def filter_design():
    low_edge = 1.0 / 12.9
    high_edge = 1.0 / 12.0
    warped_low = 2.0 * math.tan(math.pi * low_edge)
    warped_high = 2.0 * math.tan(math.pi * high_edge)
    centre = math.sqrt(warped_low * warped_high)
    spread = warped_high - warped_low
    digital = []
    for octant in (3, 5):
        proto = complex(math.cos(octant * math.pi / 4.0), math.sin(octant * math.pi / 4.0)) * spread
        radical = (proto * proto - 4.0 * centre * centre) ** 0.5
        for analog in ((proto + radical) / 2.0, (proto - radical) / 2.0):
            digital.append((2.0 + analog) / (2.0 - analog))
    denom = expand_roots(digital)
    numer = [1.0, 0.0, -2.0, 0.0, 1.0]
    omega = 2.0 * math.atan(centre / 2.0)
    zcentre = complex(math.cos(omega), math.sin(omega))
    respond = horner_value(numer, zcentre) / horner_value(denom, zcentre)
    numer = [coefficient / abs(respond) for coefficient in numer]
    remain = [numer[position] - numer[0] * denom[position] for position in range(1, 5)]
    slope = derive_coeffs(denom)
    amat = np.zeros((4, 4))
    bvec = np.zeros(4)
    cvec = np.zeros(4)
    upper = [pole for pole in digital if pole.imag > 0]
    for index, pole in enumerate(upper):
        resid = horner_value(remain, pole) / horner_value(slope, pole)
        first = 2 * index
        amat[first, first] = pole.real
        amat[first, first + 1] = -pole.imag
        amat[first + 1, first] = pole.imag
        amat[first + 1, first + 1] = pole.real
        bvec[first] = 1.0
        cvec[first] = 2.0 * resid.real
        cvec[first + 1] = -2.0 * resid.imag
    return (amat, bvec, cvec, float(numer[0]))


def power(matrix, exponent):
    return np.linalg.matrix_power(matrix, exponent)


def power(matrix, exponent):
    return np.linalg.matrix_power(matrix, exponent)


def block_maps(hours):
    amat, bvec, cvec, direct = filter_design()
    impulse = [direct] + [float(cvec @ power(amat, step - 1) @ bvec) for step in range(1, hours)]
    toeplitz = np.zeros((hours, hours))
    for row in range(hours):
        for column in range(row + 1):
            toeplitz[row, column] = impulse[row - column]
    powers = [np.eye(4)]
    for hour in range(hours):
        powers.append(powers[-1] @ amat)
    left = np.stack([powers[hours - 1 - hour] @ bvec for hour in range(hours)], axis=1)
    entering = np.stack([cvec @ powers[hour] for hour in range(hours)], axis=0)
    back = np.stack([powers[hour] @ bvec for hour in range(hours)], axis=1)
    summary = np.concatenate([left, back @ toeplitz], axis=0)
    response = toeplitz.T @ toeplitz
    injected = np.concatenate([toeplitz.T @ entering, entering[::-1]], axis=1)
    return summary, back @ entering, powers[hours], response, injected


def direct_form():
    amat, _, cvec, _ = filter_design()
    denom = np.poly(amat)
    outputs = [cvec @ power(amat, hour) for hour in range(4)]
    rows = [sum(denom[lag] * outputs[row - lag] for lag in range(row + 1)) for row in range(4)]
    return denom, np.stack(rows)


def thirds(table):
    rest = table.astype(np.float32)
    out = []
    for _ in range(3):
        part = rest.astype(ml_dtypes.bfloat16)
        out.append(part)
        rest = rest - part.astype(np.float32)
    return out


def along_rows(table):
    high, middle, low = thirds(table)
    first = np.concatenate([np.concatenate([high, high], axis=-1), np.concatenate([middle, middle], axis=-1)], axis=-2)
    return first, np.concatenate([high, low], axis=-1)


def along_depth(table, height):
    high, middle, low = thirds(table)
    parts = np.concatenate([high, high, middle, middle, high, low], axis=-1)
    pad = [(0, 0)] * (parts.ndim - 1) + [(0, height - parts.shape[-1])]
    return np.pad(parts, pad)


@functools.lru_cache(maxsize=None)
def plan():
    gain = filter_design()[3]
    scale = gain * gain
    denom, to_direct = direct_form()
    summary, coupling, step, _, _ = block_maps(HOURS)
    own = GROUP * 8
    forward = np.zeros((GROUP + 1, 4, own + 8))
    forward[0][:, own : own + 4] = np.eye(4)
    for j in range(GROUP):
        forward[j + 1] = step @ forward[j]
        forward[j + 1][:, j * 8 : j * 8 + 4] += np.eye(4)
    backward = np.zeros((GROUP + 1, 4, own + 8))
    backward[GROUP][:, own + 4 :] = np.eye(4)
    for j in reversed(range(GROUP)):
        backward[j] = step @ backward[j + 1] + coupling @ forward[j]
        backward[j][:, j * 8 + 4 : j * 8 + 8] += np.eye(4)
    inner = np.zeros((own, own + 8))
    for j in range(GROUP):
        inner[j * 8 : j * 8 + 4] = gain * to_direct @ forward[j]
        inner[j * 8 + 4 : j * 8 + 8] = to_direct @ backward[j + 1]
    run_left = forward[GROUP][:, :own]
    run_right = backward[0][:, :own]
    run_summary, run_coupling, run_step, response, injected = block_maps(SPAN)
    swapped = [j * 8 + k for k in range(8) for j in range(GROUP)]
    suffix = [np.zeros((4, 4))]
    for m in range(RUNS):
        suffix.append(suffix[-1] + power(run_step, m) @ run_coupling @ power(run_step, m))
    send = np.zeros((RUNS, 16, 2 * own))
    local = np.zeros((RUNS, 16, 2 * own))
    gather = np.zeros((RUNS, 16, RUNS * 8))
    send_ninth = np.zeros((RUNS, 16, own))
    local_ninth = np.zeros((RUNS, 16, own))
    edge_gather = np.zeros((RUNS, QUARTER, LANES))
    for z in range(RUNS):
        after = suffix[RUNS - 1 - z]
        right = run_right + run_step @ after @ run_left
        send_ninth[z, 0:4] = run_left[:, swapped]
        send_ninth[z, 8:12] = right[:, swapped]
        local_ninth[z, 8:12] = (after @ run_left)[:, swapped]
        for tile in range(2):
            columns = slice(tile * own, (tile + 1) * own)
            ahead = slice(4 * tile, 4 * tile + 4)
            behind = slice(8 + 4 * tile, 12 + 4 * tile)
            send[z, ahead, columns] = run_left
            send[z, behind, columns] = right
            local[z, behind, columns] = after @ run_left
            for other in range(RUNS):
                here = slice(other * 8 + 4 * tile, other * 8 + 4 * tile + 4)
                if other < z:
                    came = power(run_step, z - 1 - other)
                    gather[z, ahead, here] = came
                    gather[z, behind, here] = after @ run_step @ came
                if other > z:
                    gather[z, behind, here] = power(run_step, other - z - 1)
        for other in range(RUNS):
            from_left = slice(other * 8, other * 8 + 4)
            from_right = slice(other * 8 + 4, other * 8 + 8)
            if other < z:
                came = power(run_step, z - 1 - other)
                edge_gather[z, from_left, 0:4] = came.T
                edge_gather[z, from_left, 4:8] = (after @ run_step @ came).T
            if other == z:
                edge_gather[z, from_left, 4:8] = after.T
            if other > z:
                came = power(run_step, other - z - 1)
                edge_gather[z, from_right, 4:8] = came.T
                edge_gather[z, from_left, 4:8] = (came @ run_step @ suffix[RUNS - 1 - other]).T
    spread = inner[:, :own]
    inject = np.zeros((2, own, 16))
    for tile in range(2):
        inject[tile, :, 4 * tile : 4 * tile + 4] = inner[:, own : own + 4]
        inject[tile, :, 8 + 4 * tile : 12 + 4 * tile] = inner[:, own + 4 :]
    edge_sum = np.zeros((SPAN, LANES))
    edge_sum[:, 2 * QUARTER : 2 * QUARTER + 8] = run_summary.T / scale
    order = [(j // 8) * 8 + (8 - j % 8) % 8 for j in range(GROUP)]
    places = [order[j] * HOURS + hour for j in range(GROUP) for hour in range(HOURS)]
    edge_response = np.zeros((SPAN, SPAN))
    edge_response[:, places] = response.T / scale
    edge_inject = np.zeros((8, SPAN))
    edge_inject[:, places] = injected.T
    spread_first, spread_second = along_rows(spread)
    local_tiles = [along_rows(local[:, :, tile * own : (tile + 1) * own]) for tile in range(2)]
    ninth_first, ninth_second = along_rows(spread[swapped][:, swapped])
    local_ninth_first, local_ninth_second = along_rows(local_ninth)
    tables = dict(
        send=send.astype(np.float32),
        send_ninth=send_ninth.astype(np.float32),
        edge_sum=edge_sum.astype(np.float32),
        gather=along_depth(gather, 256),
        local_first=np.stack([tile[0] for tile in local_tiles], axis=1),
        local_second=np.stack([tile[1] for tile in local_tiles], axis=1),
        spread_first=spread_first,
        spread_second=spread_second,
        inject=along_depth(np.concatenate([inject[0], inject[1]]), LANES),
        local_ninth_first=local_ninth_first,
        local_ninth_second=local_ninth_second,
        ninth_first=ninth_first,
        ninth_second=ninth_second,
        inject_ninth=along_depth(inject[0][swapped], LANES),
        edge_gather=along_depth(np.swapaxes(edge_gather, 1, 2), 256).swapaxes(1, 2),
        edge_response=np.stack(thirds(edge_response)),
        edge_inject=along_depth(edge_inject.T, LANES).T,
    )
    return dict(tables, denom=denom, scale=scale, summary=summary / scale)


def place():
    tile = lax.axis_index("col") % 2
    return lax.axis_index("tm") // GROUP, tile, 1 - tile


def lanes_of(shape=(ROWS, LANES)):
    return lax.broadcasted_iota(jnp.int32, shape, 1)


def live_hours(mask, start, scale):
    first = lax.axis_index("tm") * HOURS
    ocean = mask == 1
    return [jnp.where(ocean & (start <= first + hour), scale, 0.0) for hour in range(HOURS)]


def depths(levels_ref):
    out = []
    for level in range(4):
        number = jnp.full((ROWS, LANES), levels_ref[level], jnp.int32).astype(jnp.float32)
        out.append((number + number * number / 90.0) / 90.0)
    return out


def anomalies(field, live):
    mean = 0.25 * ((field[0] + field[1]) + (field[2] + field[3]))
    return [(field[level] - mean) * live for level in range(3)]


def pressures(rho, depth):
    press = [rho[0] * depth[0]]
    for level in range(1, 4):
        press.append(press[-1] + 0.5 * (rho[level - 1] + rho[level]) * (depth[level] - depth[level - 1]))
    return press


def last_level(values):
    return -((values[0] + values[1]) + values[2])


def turn(value, shift):
    shift = shift % LANES
    return value if shift == 0 else pltpu.roll(value, shift, 1)


def transposed(parts, lane):
    low = lane < 2 * QUARTER
    even = (lane // QUARTER) % 2 == 0
    halves = [None] * 4
    for i in range(2):
        first, second = parts[i], parts[i + 2]
        halves[i] = jnp.where(low, first, turn(second, 64))
        halves[i + 2] = jnp.where(low, turn(first, 64), second)
    out = [None] * 4
    for i in (0, 2):
        first, second = halves[i], halves[i + 1]
        out[i] = jnp.where(even, first, turn(second, QUARTER))
        out[i + 1] = jnp.where(even, turn(first, -QUARTER), second)
    return out


def shared(parts, lane, sign):
    block = lane // QUARTER
    out = []
    for i in range(4):
        total = parts[i]
        for b in range(1, 4):
            total = jnp.where(block == b, parts[(i + sign * b) % 4], total)
        out.append(total)
    return out


def block_transposed(value, lane):
    value = pltpu.roll(value, 0, 1, stride=HOURS, stride_axis=0)
    total = value
    for block in range(1, 8):
        total = jnp.where(lane // HOURS == block, pltpu.roll(value, 8 - block, 0), total)
    return pltpu.roll(total, 0, 1, stride=HOURS, stride_axis=0)


def summary_kernel(
    levels_hbm, u_hbm, v_hbm, rho_hbm, mask_hbm, start_hbm, out_ref, kept_ref, levels_ref, u_ref, v_ref, rho_ref, mask_ref, start_ref, sums_ref, sems
):
    summary, scale = plan()["summary"], float(plan()["scale"])
    copies = [
        pltpu.make_async_copy(source, target, sems.at[index])
        for index, (source, target) in enumerate(
            (
                (mask_hbm, mask_ref),
                (start_hbm, start_ref),
                (levels_hbm, levels_ref),
                (u_hbm, u_ref),
                (rho_hbm, rho_ref),
                (v_hbm, v_ref),
            )
        )
    ]
    for copy in copies:
        copy.start()
    for copy in copies[:3]:
        copy.wait()
    live = live_hours(mask_ref[...], start_ref[...], scale)
    depth = depths(levels_ref)
    lane = lanes_of()
    zeros = jnp.zeros((ROWS, LANES), jnp.float32)
    west, east = zeros, zeros
    for which, ref in enumerate((u_ref, rho_ref, v_ref)):
        copies[3 + which].wait()
        sums = [[None] * 8 for _ in range(3)]
        for hour in range(HOURS):
            field = [ref[level, hour] for level in range(4)]
            if which == 1:
                field = pressures(field, depth)
            values = anomalies(field, live[hour])
            for level, value in enumerate(values):
                kept_ref[which * 3 + level, hour] = value
                for k in range(8):
                    term = float(summary[k, hour]) * value
                    sums[level][k] = term if hour == 0 else sums[level][k] + term
                if which < 2:
                    position = (8 - which * 4 - level) % 8 * HOURS + hour
                    turned = turn(value, position)
                    west = jnp.where(lane == position, turned, west)
                    east = jnp.where(lane == (position - 1) % LANES, turned, east)
        for level in range(3):
            for k in range(8):
                sums_ref[(which * 3 + level) * 8 + k] = sums[level][k]
        if which == 1:
            edges = finished_edges(west, east, lane)
            for index, quarter in enumerate(QUARTERS):
                out_ref[pl.ds(index * SLOT + 18, ROWS, stride=4 * SLOT), :] = edges.get(quarter, zeros)
            lay_out(sums_ref, list(range(4)), out_ref, 0, lane)
    lay_out(sums_ref, list(range(4, 8)), out_ref, 8, lane)
    for v in range(2):
        lay_out_rows([sums_ref[64 + 4 * v + a] for a in range(4)], out_ref, 16 + v, lane)


def finished_edges(west, east, lane):
    block = lane // HOURS
    out = []
    for ends in (west, turn(east, 1)):
        three = -((turn(ends, -HOURS) + turn(ends, -2 * HOURS)) + turn(ends, -3 * HOURS))
        out.append(jnp.where((block == 5) | (block == 1), three, ends))
    return {0: out[0], 3: out[1]}


def lay_out(sums_ref, series, out_ref, first, lane):
    for k in range(8):
        parts = shared([sums_ref[s * 8 + k] for s in series], lane, 1)
        for index in range(4):
            out_ref[pl.ds(index * SLOT + first + k, ROWS, stride=4 * SLOT), :] = parts[index]


def lay_out_rows(values, out_ref, row, lane):
    parts = transposed(values, lane)
    for index, quarter in enumerate(QUARTERS):
        out_ref[pl.ds(index * SLOT + row, ROWS, stride=4 * SLOT), :] = parts[quarter]


def blocks_of(in_ref, tile):
    return jnp.concatenate(
        [
            jnp.concatenate([in_ref[pl.ds((2 * j + tile) * SLOT + v * 8, 8), :] for j in range(GROUP)], axis=0)
            for v in range(2)
        ],
        axis=1,
    )


def ninth_of(in_ref):
    first = lanes_of((GROUP, LANES)) < QUARTER
    parts = []
    for half in range(2):
        tiles = [in_ref[pl.ds(tile * SLOT + 16 + half, GROUP, stride=2 * SLOT), :] for tile in range(2)]
        for a in range(4):
            parts.append(jnp.where(first, turn(tiles[0], -QUARTER * a), turn(tiles[1], QUARTER - QUARTER * a)))
    return jnp.concatenate(parts, axis=0)


def edge_hours(in_ref, tile):
    lane = lanes_of()
    rows = in_ref[pl.ds(tile * SLOT + 18, GROUP, stride=2 * SLOT), :]
    return jnp.concatenate([block_transposed(rows[half * 8 : half * 8 + 8], lane) for half in range(2)], axis=1)


def dot(lhs, rhs):
    return jnp.dot(lhs, rhs, precision=HIGH, preferred_element_type=jnp.float32)


def run_kernel(in_ref, send_ref, send_ninth_ref, edge_sum_ref, out_ref):
    run, tile, side = place()
    blocks = jnp.concatenate([blocks_of(in_ref, 0), blocks_of(in_ref, 1)], axis=0)
    totals = dot(send_ref[run], blocks)
    ninth = dot(send_ninth_ref[run], ninth_of(in_ref))
    near = edge_hours(in_ref, 1 - tile)
    far = edge_hours(in_ref, tile)
    sums = dot(jnp.concatenate([near, far], axis=0), edge_sum_ref[...])
    first = lanes_of() < 2 * QUARTER
    for other in range(RUNS):
        for v in range(3):
            lanes = slice(v * LANES, (v + 1) * LANES)
            if v == 2:
                mine = jnp.where(first, jnp.where(other > run, ninth[0:8], ninth[8:16]), sums[0:8])
                across = sums[8:16]
            else:
                mine = jnp.where(other > run, totals[0:8, lanes], totals[8:16, lanes])
                across = far[:, lanes]
            for slot_side in range(2):
                out_ref[2 * other + slot_side, pl.ds(v * 8, 8), :] = jnp.where(side == slot_side, mine, across)


def split(value):
    high = value.astype(jnp.bfloat16)
    rest = value - high.astype(jnp.float32)
    middle = rest.astype(jnp.bfloat16)
    return high, middle, (rest - middle.astype(jnp.float32)).astype(jnp.bfloat16)


def six_below(value, height):
    high, middle, low = split(value)
    parts = [high, middle, high, middle, low, high]
    rest = height - 6 * value.shape[0]
    if rest:
        parts.append(jnp.zeros((rest, value.shape[1]), jnp.bfloat16))
    return jnp.concatenate(parts, axis=0)


def product(lhs, rhs):
    return jnp.dot(lhs, rhs, preferred_element_type=jnp.float32)


def mapped(first, second, value):
    high, middle, low = split(value)
    upper = product(first, jnp.concatenate([high, middle], axis=0))
    lower = product(second, jnp.concatenate([low, high], axis=0))
    rows = 2 * GROUP * 8
    half = GROUP * 8
    spread = (upper[:half] + upper[half:rows]) + lower[:half]
    local = (upper[rows : rows + 16] + upper[rows + 16 :]) + lower[half:]
    return spread, local


def edge_flux(in_ref, runs_ref, run, tile, side, edge_gather, response_ref, edge_inject):
    lane = lanes_of()
    own = [runs_ref[2 * other + side, pl.ds(16, 8), :] for other in range(RUNS)]
    across = [runs_ref[2 * other + 1 - side, pl.ds(16, 8), :] for other in range(RUNS)]
    sums = []
    for parts in (own, across):
        total = jnp.zeros((ROWS, LANES), jnp.float32)
        for other in range(RUNS):
            total = jnp.where(lane // 8 == other, turn(parts[other], other * 8 - 2 * QUARTER), total)
        sums.append(total)
    high, middle, low = (part.astype(jnp.float32) for part in split(jnp.concatenate(sums, axis=0)))
    first = (high + turn(middle, 32)) + (turn(high, 64) + turn(middle, 96))
    sums = jnp.concatenate([first, low + turn(high, 32)], axis=1)
    states = product(sums.astype(jnp.bfloat16), edge_gather)
    high, middle, low = (part.astype(jnp.float32) for part in split(states))
    states = (high + turn(middle, 8)) + (turn(high, 16) + turn(middle, 24)) + (turn(low, 32) + turn(high, 40))
    near = edge_hours(in_ref, 1 - tile)
    far = jnp.concatenate([runs_ref[2 * run + 1 - side, pl.ds(v * 8, 8), :] for v in range(2)], axis=1)
    high, middle, low = split(jnp.concatenate([near, far], axis=0))
    one = product(jnp.concatenate([high, middle, low], axis=0), response_ref[0])
    two = product(jnp.concatenate([high, middle], axis=0), response_ref[1])
    three = product(high, response_ref[2])
    banded = (one[0:16] + one[16:32]) + (one[32:48] + two[0:16]) + (two[16:32] + three)
    banded = banded + product(states.astype(jnp.bfloat16), edge_inject)
    row = lax.broadcasted_iota(jnp.int32, (ROWS, SPAN), 0)
    products = [part * pltpu.roll(part, 4, 0) for part in (banded[0:8], banded[8:16])]
    flux = jnp.where(row < 4, products[0], products[1])
    return jnp.concatenate(
        [block_transposed(flux[:, half * LANES : (half + 1) * LANES], lane) for half in range(2)], axis=0
    )


def border_kernel(
    in_ref,
    runs_ref,
    gather_ref,
    local_first_ref,
    local_second_ref,
    spread_first_ref,
    spread_second_ref,
    inject_ref,
    local_ninth_first_ref,
    local_ninth_second_ref,
    ninth_first_ref,
    ninth_second_ref,
    inject_ninth_ref,
    edge_gather_ref,
    edge_response_ref,
    edge_inject_ref,
    out_ref,
):
    run, tile, side = place()
    flux = edge_flux(in_ref, runs_ref, run, tile, side, edge_gather_ref[run], edge_response_ref, edge_inject_ref[...])
    runs = [
        jnp.concatenate([runs_ref[2 * other + side, pl.ds(v * 8, 8), :] for other in range(RUNS)], axis=0)
        for v in range(3)
    ]
    states = product(gather_ref[run], six_below(jnp.concatenate(runs, axis=1), 256))
    bases, locals_ = [], []
    for which in range(2):
        base, local = mapped(
            jnp.concatenate([spread_first_ref[...], local_first_ref[run, which]], axis=0),
            jnp.concatenate([spread_second_ref[...], local_second_ref[run, which]], axis=0),
            blocks_of(in_ref, which),
        )
        bases.append(base)
        locals_.append(local)
    ninth, local = mapped(
        jnp.concatenate([ninth_first_ref[...], local_ninth_first_ref[run]], axis=0),
        jnp.concatenate([ninth_second_ref[...], local_ninth_second_ref[run]], axis=0),
        ninth_of(in_ref),
    )
    states = six_below(states + jnp.concatenate([locals_[0] + locals_[1], local], axis=1), LANES)
    added = product(inject_ref[...], states[:, : 2 * LANES])
    ninth = ninth + product(inject_ninth_ref[...], states[:, 2 * LANES :])
    for which in range(2):
        for j in range(GROUP):
            row = which * GROUP * 8 + j * 8
            borders = bases[which][j * 8 : j * 8 + 8] + added[row : row + 8]
            for v in range(2):
                out_ref[pl.ds((2 * j + which) * SLOT + v * 8, 8), :] = borders[:, v * LANES : (v + 1) * LANES]
        out_ref[pl.ds(which * SLOT + 18, GROUP, stride=2 * SLOT), :] = flux
    block = lanes_of((GROUP, LANES)) // QUARTER
    for which in range(2):
        for half in range(2):
            total = jnp.zeros((GROUP, LANES), jnp.float32)
            for a in range(4):
                row = (half * 4 + a) * GROUP
                total = jnp.where(block == a, turn(ninth[row : row + GROUP], QUARTER * (a - which)), total)
            out_ref[pl.ds(which * SLOT + 16 + half, GROUP, stride=2 * SLOT), :] = total


def filter_steps(state, samples):
    _, one, two, three, four = (float(value) for value in plan()["denom"])
    first, second, third, fourth = state
    out = []
    for sample in samples:
        value = sample + first
        out.append(value)
        first = second - one * value
        second = (third - (sample + sample)) - two * value
        third = fourth - three * value
        fourth = sample - four * value
    return out


def band_kernel(
    kept_ref, mask_ref, borders_ref, press_hbm, flux_hbm, press_ref, flux_ref, east_ref, north_ref, states_ref, sems
):
    _, tile, _ = place()
    column = lax.axis_index("col")
    lane = lanes_of()
    for v in range(2):
        for k in range(8):
            parts = [borders_ref[pl.ds(index * SLOT + v * 8 + k, ROWS, stride=4 * SLOT), :] for index in range(4)]
            for a, part in enumerate(shared(parts, lane, -1)):
                states_ref[(4 * v + a) * 8 + k] = part
        for index, quarter in enumerate(QUARTERS):
            parts[quarter] = borders_ref[pl.ds(index * SLOT + 16 + v, ROWS, stride=4 * SLOT), :]
        for a, part in enumerate(transposed(parts, lane)):
            states_ref[64 + 4 * v + a] = part
    copies = []

    def send(source, target):
        copies.append(pltpu.make_async_copy(source, target, sems.at[len(copies)]))
        copies[-1].start()

    row = lax.broadcasted_iota(jnp.int32, (ROWS, LANES), 0)
    half = 0.5 * mask_ref[...].astype(jnp.float32)
    last = lane == LANES - 1
    halos = borders_ref[pl.ds(tile * SLOT + 18, ROWS, stride=4 * SLOT), :]
    halos = jnp.where(tile == 0, turn(halos, 64), halos)
    outside = ((column == 0) & (lane < 64)) | ((column == 2 * len(PAIRS) - 1) & (lane >= 64))
    halos = jnp.where(outside, 0.0, halos)
    for level in range(4):
        if level < 3:
            for which, target in ((1, press_ref), (0, east_ref), (2, north_ref)):
                s = which * 3 + level
                states = [states_ref[s * 8 + k] for k in range(8)]
                samples = filter_steps(states[:4], [kept_ref[s, hour] for hour in range(HOURS)])
                samples = filter_steps(states[4:], samples[::-1])[::-1]
                for hour in range(HOURS):
                    target[level, hour] = samples[hour]
        else:
            for hour in range(HOURS):
                press_ref[3, hour] = last_level([press_ref[lower, hour] for lower in range(3)])
        send(press_ref.at[level], press_hbm.at[level])
        for hour in range(HOURS):
            press = press_ref[level, hour]
            if level < 3:
                u_here, v_here = east_ref[level, hour], north_ref[level, hour]
            else:
                u_here = last_level([east_ref[lower, hour] for lower in range(3)])
                v_here = last_level([north_ref[lower, hour] for lower in range(3)])
            fx = u_here * press
            fy = v_here * press
            position = level * HOURS + hour
            next_x = jnp.where(last, turn(halos, LANES - 1 - 64 - position), turn(fx, -1))
            prev_x = jnp.where(lane == 0, turn(halos, -position), turn(fx, 1))
            next_y = jnp.where(row == ROWS - 1, 0.0, pltpu.roll(fy, ROWS - 1, 0))
            prev_y = jnp.where(row == 0, 0.0, pltpu.roll(fy, 1, 0))
            flux_ref[level, hour] = half * ((next_x - prev_x) + (next_y - prev_y))
        send(flux_ref.at[level], flux_hbm.at[level])
    for copy in copies:
        copy.wait()


def swap(array, devices, columns):
    groups = [[tm * 8 + col for tm in some for col in pair] for some in devices for pair in columns]
    return lax.all_to_all(array, ("tm", "col"), 0, 0, tiled=True, axis_index_groups=groups)


VMEM = pl.BlockSpec(memory_space=pltpu.VMEM)
HBM = pl.BlockSpec(memory_space=pltpu.HBM)


def call(kernel, shapes, in_specs, scratch=(), out_spec=VMEM):
    return pl.pallas_call(
        kernel,
        out_shape=[
            jax.ShapeDtypeStruct(shape, jnp.float32) if out_spec is HBM else pltpu.VMEM(shape, jnp.float32)
            for shape in shapes
        ],
        in_specs=in_specs,
        out_specs=[out_spec] * len(shapes),
        scratch_shapes=scratch,
        compiler_params=pltpu.CompilerParams(vmem_limit_bytes=32 * 1024 * 1024),
    )


def on_device(u_vel, v_vel, density, land_mask, start_hour, levels):
    tables = plan()
    whole = (4, HOURS, ROWS, LANES)
    part = (3, HOURS, ROWS, LANES)
    flat = (OWNERS * SLOT, LANES)
    slots = (OWNERS, 1, SLOT * LANES)
    runs = [[z * GROUP + j for j in range(GROUP)] for z in range(RUNS)]
    across = [[z * GROUP + j for z in range(RUNS)] for j in range(GROUP)]
    state_scratch = pltpu.VMEM((SERIES * 8, ROWS, LANES), jnp.float32)
    arguments = (levels, u_vel, v_vel, density, land_mask, start_hour)
    own, kept = call(
        summary_kernel,
        [flat, (SERIES, HOURS, ROWS, LANES)],
        [HBM] * 6,
        [
            pltpu.SMEM((4,), jnp.int32),
            pltpu.VMEM(whole, jnp.float32),
            pltpu.VMEM(whole, jnp.float32),
            pltpu.VMEM(whole, jnp.float32),
            pltpu.VMEM((ROWS, LANES), jnp.int32),
            pltpu.VMEM((ROWS, LANES), jnp.int32),
            state_scratch,
            pltpu.SemaphoreType.DMA((6,)),
        ],
    )(*[pltpu.with_memory_space_constraint(array, pltpu.HBM) for array in arguments])
    blocks = swap(own.reshape(slots), runs, PAIRS).reshape(flat)
    (totals,) = call(run_kernel, [(2 * RUNS, 24, LANES)], [VMEM] * 4)(
        blocks, tables["send"], tables["send_ninth"], tables["edge_sum"]
    )
    totals = swap(totals, across, FAR)
    names = (
        "gather",
        "local_first",
        "local_second",
        "spread_first",
        "spread_second",
        "inject",
        "local_ninth_first",
        "local_ninth_second",
        "ninth_first",
        "ninth_second",
        "inject_ninth",
        "edge_gather",
        "edge_response",
        "edge_inject",
    )
    (borders,) = call(border_kernel, [flat], [VMEM] * (2 + len(names)))(
        blocks, totals, *[tables[name] for name in names]
    )
    borders = swap(borders.reshape(slots), runs, PAIRS).reshape(flat)
    pressure, flux = call(
        band_kernel,
        [whole, whole],
        [VMEM] * 3,
        [
            pltpu.VMEM(whole, jnp.float32),
            pltpu.VMEM(whole, jnp.float32),
            pltpu.VMEM(part, jnp.float32),
            pltpu.VMEM(part, jnp.float32),
            state_scratch,
            pltpu.SemaphoreType.DMA((8,)),
        ],
        out_spec=HBM,
    )(kept, land_mask, borders)
    return (pressure, flux)


def solution(mesh):
    return jax.shard_map(
        on_device,
        mesh=mesh,
        in_specs=(
            P(None, "tm", None, "col"),
            P(None, "tm", None, "col"),
            P(None, "tm", None, "col"),
            P(None, "col"),
            P(None, "col"),
            P(),
        ),
        out_specs=(P(None, "tm", None, "col"), P(None, "tm", None, "col")),
        check_vma=False,
    )
```

```python
import functools
import math

import jax
import jax.numpy as jnp
import ml_dtypes
import numpy as np
from jax import lax
from jax.experimental import pallas as pl
from jax.experimental.pallas import tpu as pltpu
from jax.sharding import PartitionSpec as P

HOURS = 16
GROUP = 16
RUNS = 4
OWNERS = 2 * GROUP
SERIES = 9
ROWS = 8
LANES = 128
QUARTER = 32
SLOT = 19
SPAN = GROUP * HOURS
QUARTERS = (0, 3, 1, 2)
PAIRS = ((0, 1), (2, 3), (4, 5), (6, 7))
FAR = ((1, 2), (3, 4), (5, 6), (7, 0))
HIGH = lax.Precision.HIGHEST


def expand_roots(roots):
    coefficients = [complex(1.0, 0.0)]
    for root in roots:
        widened = coefficients + [complex(0.0, 0.0)]
        for position in range(1, len(widened)):
            widened[position] = widened[position] - root * coefficients[position - 1]
        coefficients = widened
    return [coefficient.real for coefficient in coefficients]


def horner_value(coefficients, point):
    running = complex(0.0, 0.0)
    for coefficient in coefficients:
        running = running * point + coefficient
    return running


def derive_coeffs(coefficients):
    degree = len(coefficients) - 1
    return [coefficients[position] * (degree - position) for position in range(degree)]


def filter_design():
    low_edge = 1.0 / 12.9
    high_edge = 1.0 / 12.0
    warped_low = 2.0 * math.tan(math.pi * low_edge)
    warped_high = 2.0 * math.tan(math.pi * high_edge)
    centre = math.sqrt(warped_low * warped_high)
    spread = warped_high - warped_low
    digital = []
    for octant in (3, 5):
        proto = complex(math.cos(octant * math.pi / 4.0), math.sin(octant * math.pi / 4.0)) * spread
        radical = (proto * proto - 4.0 * centre * centre) ** 0.5
        for analog in ((proto + radical) / 2.0, (proto - radical) / 2.0):
            digital.append((2.0 + analog) / (2.0 - analog))
    denom = expand_roots(digital)
    numer = [1.0, 0.0, -2.0, 0.0, 1.0]
    omega = 2.0 * math.atan(centre / 2.0)
    zcentre = complex(math.cos(omega), math.sin(omega))
    respond = horner_value(numer, zcentre) / horner_value(denom, zcentre)
    numer = [coefficient / abs(respond) for coefficient in numer]
    remain = [numer[position] - numer[0] * denom[position] for position in range(1, 5)]
    slope = derive_coeffs(denom)
    amat = np.zeros((4, 4))
    bvec = np.zeros(4)
    cvec = np.zeros(4)
    upper = [pole for pole in digital if pole.imag > 0]
    for index, pole in enumerate(upper):
        resid = horner_value(remain, pole) / horner_value(slope, pole)
        first = 2 * index
        amat[first, first] = pole.real
        amat[first, first + 1] = -pole.imag
        amat[first + 1, first] = pole.imag
        amat[first + 1, first + 1] = pole.real
        bvec[first] = 1.0
        cvec[first] = 2.0 * resid.real
        cvec[first + 1] = -2.0 * resid.imag
    return (amat, bvec, cvec, float(numer[0]))


def power(matrix, exponent):
    return np.linalg.matrix_power(matrix, exponent)


def power(matrix, exponent):
    return np.linalg.matrix_power(matrix, exponent)


def block_maps(hours):
    amat, bvec, cvec, direct = filter_design()
    impulse = [direct] + [float(cvec @ power(amat, step - 1) @ bvec) for step in range(1, hours)]
    toeplitz = np.zeros((hours, hours))
    for row in range(hours):
        for column in range(row + 1):
            toeplitz[row, column] = impulse[row - column]
    powers = [np.eye(4)]
    for hour in range(hours):
        powers.append(powers[-1] @ amat)
    left = np.stack([powers[hours - 1 - hour] @ bvec for hour in range(hours)], axis=1)
    entering = np.stack([cvec @ powers[hour] for hour in range(hours)], axis=0)
    back = np.stack([powers[hour] @ bvec for hour in range(hours)], axis=1)
    summary = np.concatenate([left, back @ toeplitz], axis=0)
    response = toeplitz.T @ toeplitz
    injected = np.concatenate([toeplitz.T @ entering, entering[::-1]], axis=1)
    return summary, back @ entering, powers[hours], response, injected


def direct_form():
    amat, _, cvec, _ = filter_design()
    denom = np.poly(amat)
    outputs = [cvec @ power(amat, hour) for hour in range(4)]
    rows = [sum(denom[lag] * outputs[row - lag] for lag in range(row + 1)) for row in range(4)]
    return denom, np.stack(rows)


def thirds(table):
    rest = table.astype(np.float32)
    out = []
    for _ in range(3):
        part = rest.astype(ml_dtypes.bfloat16)
        out.append(part)
        rest = rest - part.astype(np.float32)
    return out


def along_rows(table):
    high, middle, low = thirds(table)
    first = np.concatenate([np.concatenate([high, high], axis=-1), np.concatenate([middle, middle], axis=-1)], axis=-2)
    return first, np.concatenate([high, low], axis=-1)


def along_depth(table, height):
    high, middle, low = thirds(table)
    parts = np.concatenate([high, high, middle, middle, high, low], axis=-1)
    pad = [(0, 0)] * (parts.ndim - 1) + [(0, height - parts.shape[-1])]
    return np.pad(parts, pad)


@functools.lru_cache(maxsize=None)
def plan():
    gain = filter_design()[3]
    scale = gain * gain
    denom, to_direct = direct_form()
    summary, coupling, step, _, _ = block_maps(HOURS)
    own = GROUP * 8
    forward = np.zeros((GROUP + 1, 4, own + 8))
    forward[0][:, own : own + 4] = np.eye(4)
    for j in range(GROUP):
        forward[j + 1] = step @ forward[j]
        forward[j + 1][:, j * 8 : j * 8 + 4] += np.eye(4)
    backward = np.zeros((GROUP + 1, 4, own + 8))
    backward[GROUP][:, own + 4 :] = np.eye(4)
    for j in reversed(range(GROUP)):
        backward[j] = step @ backward[j + 1] + coupling @ forward[j]
        backward[j][:, j * 8 + 4 : j * 8 + 8] += np.eye(4)
    inner = np.zeros((own, own + 8))
    for j in range(GROUP):
        inner[j * 8 : j * 8 + 4] = gain * to_direct @ forward[j]
        inner[j * 8 + 4 : j * 8 + 8] = to_direct @ backward[j + 1]
    run_left = forward[GROUP][:, :own]
    run_right = backward[0][:, :own]
    run_summary, run_coupling, run_step, response, injected = block_maps(SPAN)
    swapped = [j * 8 + k for k in range(8) for j in range(GROUP)]
    suffix = [np.zeros((4, 4))]
    for m in range(RUNS):
        suffix.append(suffix[-1] + power(run_step, m) @ run_coupling @ power(run_step, m))
    send = np.zeros((RUNS, 16, 2 * own))
    local = np.zeros((RUNS, 16, 2 * own))
    gather = np.zeros((RUNS, 16, RUNS * 8))
    send_ninth = np.zeros((RUNS, 16, own))
    gather_ninth = np.zeros((RUNS, 16, 4 * RUNS))
    local_ninth = np.zeros((RUNS, 16, own))
    edge_gather = np.zeros((RUNS, QUARTER, LANES))
    for z in range(RUNS):
        after = suffix[RUNS - 1 - z]
        right = run_right + run_step @ after @ run_left
        send_ninth[z, 0:4] = run_left[[0, 2, 1, 3]][:, swapped]
        send_ninth[z, 8:12] = right[[0, 2, 1, 3]][:, swapped]
        local_ninth[z, 8:12] = (after @ run_left)[:, swapped]
        for tile in range(2):
            columns = slice(tile * own, (tile + 1) * own)
            ahead = slice(4 * tile, 4 * tile + 4)
            behind = slice(8 + 4 * tile, 12 + 4 * tile)
            send[z, ahead, columns] = run_left
            send[z, behind, columns] = right
            local[z, behind, columns] = after @ run_left
            for other in range(RUNS):
                here = slice(other * 8 + 4 * tile, other * 8 + 4 * tile + 4)
                if other < z:
                    came = power(run_step, z - 1 - other)
                    gather[z, ahead, here] = came
                    gather[z, behind, here] = after @ run_step @ came
                if other > z:
                    gather[z, behind, here] = power(run_step, other - z - 1)
        gather_ninth[z] = gather[z].reshape(16, RUNS, 8)[:, :, :4].swapaxes(1, 2).reshape(16, 4 * RUNS)
        for other in range(RUNS):
            from_left = slice(other * 8, other * 8 + 4)
            from_right = slice(other * 8 + 4, other * 8 + 8)
            if other < z:
                came = power(run_step, z - 1 - other)
                edge_gather[z, from_left, 0:4] = came.T
                edge_gather[z, from_left, 4:8] = (after @ run_step @ came).T
            if other == z:
                edge_gather[z, from_left, 4:8] = after.T
            if other > z:
                came = power(run_step, other - z - 1)
                edge_gather[z, from_right, 4:8] = came.T
                edge_gather[z, from_left, 4:8] = (came @ run_step @ suffix[RUNS - 1 - other]).T
    spread = inner[:, :own]
    inject = np.zeros((2, own, 16))
    for tile in range(2):
        inject[tile, :, 4 * tile : 4 * tile + 4] = inner[:, own : own + 4]
        inject[tile, :, 8 + 4 * tile : 12 + 4 * tile] = inner[:, own + 4 :]
    edge_sum = np.tile(run_summary.T / scale, (1, LANES // 8))
    order = [(j // 8) * 8 + (8 - j % 8) % 8 for j in range(GROUP)]
    places = [order[j] * HOURS + hour for j in range(GROUP) for hour in range(HOURS)]
    edge_response = np.zeros((SPAN, SPAN))
    edge_response[:, places] = response.T / scale
    edge_inject = np.zeros((8, SPAN))
    edge_inject[:, places] = injected.T
    spread_first, spread_second = along_rows(spread)
    local_tiles = [along_rows(local[:, :, tile * own : (tile + 1) * own]) for tile in range(2)]
    ninth_first, ninth_second = along_rows(spread[swapped][:, swapped])
    local_ninth_first, local_ninth_second = along_rows(local_ninth)
    tables = dict(
        send=send.astype(np.float32),
        send_ninth=send_ninth.astype(np.float32),
        edge_sum=edge_sum.astype(np.float32),
        gather=along_depth(gather, 256),
        gather_ninth=along_depth(gather_ninth, LANES),
        local_first=np.stack([tile[0] for tile in local_tiles], axis=1),
        local_second=np.stack([tile[1] for tile in local_tiles], axis=1),
        spread_first=spread_first,
        spread_second=spread_second,
        inject=along_depth(np.concatenate([inject[0], inject[1]]), LANES),
        local_ninth_first=local_ninth_first,
        local_ninth_second=local_ninth_second,
        ninth_first=ninth_first,
        ninth_second=ninth_second,
        inject_ninth=along_depth(inject[0][swapped], LANES),
        edge_gather=along_depth(np.swapaxes(edge_gather, 1, 2), 256).swapaxes(1, 2),
        edge_response=np.stack(thirds(edge_response)),
        edge_inject=along_depth(edge_inject.T, LANES).T,
    )
    return dict(tables, denom=denom, scale=scale, summary=summary / scale)


def place():
    tile = lax.axis_index("col") % 2
    return lax.axis_index("tm") // GROUP, tile, 1 - tile


def lanes_of(shape=(ROWS, LANES)):
    return lax.broadcasted_iota(jnp.int32, shape, 1)


def live_hours(mask, start, scale):
    first = lax.axis_index("tm") * HOURS
    ocean = mask == 1
    return [jnp.where(ocean & (start <= first + hour), scale, 0.0) for hour in range(HOURS)]


def depths(levels_ref):
    out = []
    for level in range(4):
        number = jnp.full((ROWS, LANES), levels_ref[level], jnp.int32).astype(jnp.float32)
        out.append((number + number * number / 90.0) / 90.0)
    return out


def anomalies(field, live):
    mean = 0.25 * ((field[0] + field[1]) + (field[2] + field[3]))
    return [(field[level] - mean) * live for level in range(3)]


def pressures(rho, depth):
    press = [rho[0] * depth[0]]
    for level in range(1, 4):
        press.append(press[-1] + 0.5 * (rho[level - 1] + rho[level]) * (depth[level] - depth[level - 1]))
    return press


def last_level(values):
    return -((values[0] + values[1]) + values[2])


def turn(value, shift):
    shift = shift % LANES
    return value if shift == 0 else pltpu.roll(value, shift, 1)


def transposed(parts, lane):
    low = lane < 2 * QUARTER
    even = (lane // QUARTER) % 2 == 0
    halves = [None] * 4
    for i in range(2):
        first, second = parts[i], parts[i + 2]
        halves[i] = jnp.where(low, first, turn(second, 64))
        halves[i + 2] = jnp.where(low, turn(first, 64), second)
    out = [None] * 4
    for i in (0, 2):
        first, second = halves[i], halves[i + 1]
        out[i] = jnp.where(even, first, turn(second, QUARTER))
        out[i + 1] = jnp.where(even, turn(first, -QUARTER), second)
    return out


def shared(parts, lane, sign):
    block = lane // QUARTER
    out = []
    for i in range(4):
        total = parts[i]
        for b in range(1, 4):
            total = jnp.where(block == b, parts[(i + sign * b) % 4], total)
        out.append(total)
    return out


def block_transposed(value, lane):
    value = pltpu.roll(value, 0, 1, stride=HOURS, stride_axis=0)
    total = value
    for block in range(1, 8):
        total = jnp.where(lane // HOURS == block, pltpu.roll(value, 8 - block, 0), total)
    return pltpu.roll(total, 0, 1, stride=HOURS, stride_axis=0)


def summary_kernel(
    levels_hbm, u_hbm, v_hbm, rho_hbm, mask_hbm, start_hbm, out_ref, kept_ref, levels_ref, u_ref, v_ref, rho_ref, mask_ref, start_ref, sums_ref, sems
):
    summary, scale = plan()["summary"], float(plan()["scale"])
    copies = [
        pltpu.make_async_copy(source, target, sems.at[index])
        for index, (source, target) in enumerate(
            (
                (mask_hbm, mask_ref),
                (start_hbm, start_ref),
                (levels_hbm, levels_ref),
                (u_hbm, u_ref),
                (rho_hbm, rho_ref),
                (v_hbm, v_ref),
            )
        )
    ]
    for copy in copies:
        copy.start()
    for copy in copies[:3]:
        copy.wait()
    live = live_hours(mask_ref[...], start_ref[...], scale)
    depth = depths(levels_ref)
    lane = lanes_of()
    zeros = jnp.zeros((ROWS, LANES), jnp.float32)
    west, east = zeros, zeros
    for which, ref in enumerate((u_ref, rho_ref, v_ref)):
        copies[3 + which].wait()
        sums = [[None] * 8 for _ in range(3)]
        for hour in range(HOURS):
            field = [ref[level, hour] for level in range(4)]
            if which == 1:
                field = pressures(field, depth)
            values = anomalies(field, live[hour])
            for level, value in enumerate(values):
                kept_ref[which * 3 + level, hour] = value
                for k in range(8):
                    term = float(summary[k, hour]) * value
                    sums[level][k] = term if hour == 0 else sums[level][k] + term
                if which < 2:
                    position = (8 - which * 4 - level) % 8 * HOURS + hour
                    turned = turn(value, position)
                    west = jnp.where(lane == position, turned, west)
                    east = jnp.where(lane == (position - 1) % LANES, turned, east)
        for level in range(3):
            for k in range(8):
                sums_ref[(which * 3 + level) * 8 + k] = sums[level][k]
        if which == 1:
            edges = finished_edges(west, east, lane)
            for index, quarter in enumerate(QUARTERS):
                out_ref[pl.ds(index * SLOT + 18, ROWS, stride=4 * SLOT), :] = edges.get(quarter, zeros)
            lay_out(sums_ref, list(range(4)), out_ref, 0, lane)
    lay_out(sums_ref, list(range(4, 8)), out_ref, 8, lane)
    for v in range(2):
        lay_out_rows([sums_ref[64 + 4 * v + a] for a in range(4)], out_ref, 16 + v, lane)


def finished_edges(west, east, lane):
    block = lane // HOURS
    out = []
    for ends in (west, turn(east, 1)):
        three = -((turn(ends, -HOURS) + turn(ends, -2 * HOURS)) + turn(ends, -3 * HOURS))
        out.append(jnp.where((block == 5) | (block == 1), three, ends))
    return {0: out[0], 3: out[1]}


def lay_out(sums_ref, series, out_ref, first, lane):
    for k in range(8):
        parts = shared([sums_ref[s * 8 + k] for s in series], lane, 1)
        for index in range(4):
            out_ref[pl.ds(index * SLOT + first + k, ROWS, stride=4 * SLOT), :] = parts[index]


def lay_out_rows(values, out_ref, row, lane):
    parts = transposed(values, lane)
    for index, quarter in enumerate(QUARTERS):
        out_ref[pl.ds(index * SLOT + row, ROWS, stride=4 * SLOT), :] = parts[quarter]


def blocks_of(in_ref, tile):
    return jnp.concatenate(
        [
            jnp.concatenate([in_ref[pl.ds((2 * j + tile) * SLOT + v * 8, 8), :] for j in range(GROUP)], axis=0)
            for v in range(2)
        ],
        axis=1,
    )


def ninth_of(in_ref):
    first = lanes_of((GROUP, LANES)) < QUARTER
    parts = []
    for half in range(2):
        tiles = [in_ref[pl.ds(tile * SLOT + 16 + half, GROUP, stride=2 * SLOT), :] for tile in range(2)]
        for a in range(4):
            parts.append(jnp.where(first, turn(tiles[0], -QUARTER * a), turn(tiles[1], QUARTER - QUARTER * a)))
    return jnp.concatenate(parts, axis=0)


def edge_hours(in_ref, tile):
    lane = lanes_of()
    rows = in_ref[pl.ds(tile * SLOT + 18, GROUP, stride=2 * SLOT), :]
    return jnp.concatenate([block_transposed(rows[half * 8 : half * 8 + 8], lane) for half in range(2)], axis=1)


def dot(lhs, rhs):
    return jnp.dot(lhs, rhs, precision=HIGH, preferred_element_type=jnp.float32)


def run_kernel(in_ref, send_ref, send_ninth_ref, edge_sum_ref, out_ref):
    run, tile, side = place()
    blocks = jnp.concatenate([blocks_of(in_ref, 0), blocks_of(in_ref, 1)], axis=0)
    totals = dot(send_ref[run], blocks)
    ninth = dot(send_ninth_ref[run], ninth_of(in_ref))
    near = edge_hours(in_ref, 1 - tile)
    far = edge_hours(in_ref, tile)
    sums = dot(jnp.concatenate([near, far], axis=0), edge_sum_ref[...])
    lane = lanes_of()
    row = lax.broadcasted_iota(jnp.int32, (ROWS, LANES), 0)

    def packed(value):
        return jnp.where(lane < 64, value, turn(pltpu.roll(value, 6, 0), 64))

    def in_row(value):
        value = jnp.where(lane // 8 == 15 - row, value, 0.0)
        for shift in (4, 2, 1):
            value = value + pltpu.roll(value, shift, 0)
        return value

    left, right = packed(ninth[0:8]), packed(ninth[8:16])
    near_row, far_row = in_row(sums[0:8]), in_row(sums[8:16])
    for other in range(RUNS):
        later = other > run
        rest = jnp.where(row == 2, near_row, jnp.where(later, left, right))
        for slot_side in range(2):
            base = (2 * other + slot_side) * SLOT
            mine = side == slot_side
            for v in range(2):
                lanes = slice(v * LANES, (v + 1) * LANES)
                main = jnp.where(later, totals[0:8, lanes], totals[8:16, lanes])
                out_ref[pl.ds(base + v * 8, 8), :] = jnp.where(mine, main, far[:, lanes])
            out_ref[pl.ds(base + 16, 3), :] = jnp.where(mine, rest, far_row)[0:3]


def split(value):
    high = value.astype(jnp.bfloat16)
    rest = value - high.astype(jnp.float32)
    middle = rest.astype(jnp.bfloat16)
    return high, middle, (rest - middle.astype(jnp.float32)).astype(jnp.bfloat16)


def six_below(value, height):
    high, middle, low = split(value)
    parts = [high, middle, high, middle, low, high]
    rest = height - 6 * value.shape[0]
    if rest:
        parts.append(jnp.zeros((rest, value.shape[1]), jnp.bfloat16))
    return jnp.concatenate(parts, axis=0)


def product(lhs, rhs):
    return jnp.dot(lhs, rhs, preferred_element_type=jnp.float32)


def mapped(first, second, value):
    high, middle, low = split(value)
    upper = product(first, jnp.concatenate([high, middle], axis=0))
    lower = product(second, jnp.concatenate([low, high], axis=0))
    rows = 2 * GROUP * 8
    half = GROUP * 8
    spread = (upper[:half] + upper[half:rows]) + lower[:half]
    local = (upper[rows : rows + 16] + upper[rows + 16 :]) + lower[half:]
    return spread, local


def edge_flux(in_ref, runs_ref, run, tile, side, edge_gather, response_ref, edge_inject):
    lane = lanes_of()
    sums = []
    for which in (side, 1 - side):
        rows = runs_ref[pl.ds(which * SLOT + 18, RUNS, stride=2 * SLOT), :]
        total = jnp.zeros((ROWS, LANES), jnp.float32)
        for other in range(RUNS):
            value = jnp.broadcast_to(rows[other : other + 1], (ROWS, LANES))
            value = pltpu.roll(value, 8 * other + 8, 1, stride=8, stride_axis=0)
            total = jnp.where(lane // 8 == other, value, total)
        sums.append(total)
    high, middle, low = (part.astype(jnp.float32) for part in split(jnp.concatenate(sums, axis=0)))
    first = (high + turn(middle, 32)) + (turn(high, 64) + turn(middle, 96))
    sums = jnp.concatenate([first, low + turn(high, 32)], axis=1)
    states = product(sums.astype(jnp.bfloat16), edge_gather)
    high, middle, low = (part.astype(jnp.float32) for part in split(states))
    states = (high + turn(middle, 8)) + (turn(high, 16) + turn(middle, 24)) + (turn(low, 32) + turn(high, 40))
    near = edge_hours(in_ref, 1 - tile)
    far = jnp.zeros((ROWS, SPAN), jnp.float32)
    for slot in range(2 * RUNS):
        value = jnp.concatenate([runs_ref[pl.ds(slot * SLOT + v * 8, 8), :] for v in range(2)], axis=1)
        far = jnp.where(2 * run + 1 - side == slot, value, far)
    high, middle, low = split(jnp.concatenate([near, far], axis=0))
    one = product(jnp.concatenate([high, middle, low], axis=0), response_ref[0])
    two = product(jnp.concatenate([high, middle], axis=0), response_ref[1])
    three = product(high, response_ref[2])
    banded = (one[0:16] + one[16:32]) + (one[32:48] + two[0:16]) + (two[16:32] + three)
    banded = banded + product(states.astype(jnp.bfloat16), edge_inject)
    row = lax.broadcasted_iota(jnp.int32, (ROWS, SPAN), 0)
    products = [part * pltpu.roll(part, 4, 0) for part in (banded[0:8], banded[8:16])]
    flux = jnp.where(row < 4, products[0], products[1])
    return jnp.concatenate(
        [block_transposed(flux[:, half * LANES : (half + 1) * LANES], lane) for half in range(2)], axis=0
    )


def border_kernel(
    in_ref,
    runs_ref,
    gather_ref,
    gather_ninth_ref,
    local_first_ref,
    local_second_ref,
    spread_first_ref,
    spread_second_ref,
    inject_ref,
    local_ninth_first_ref,
    local_ninth_second_ref,
    ninth_first_ref,
    ninth_second_ref,
    inject_ninth_ref,
    edge_gather_ref,
    edge_response_ref,
    edge_inject_ref,
    out_ref,
):
    run, tile, side = place()
    flux = edge_flux(in_ref, runs_ref, run, tile, side, edge_gather_ref[run], edge_response_ref, edge_inject_ref[...])
    runs = []
    for v in range(2):
        parts = []
        for other in range(RUNS):
            slots = [runs_ref[pl.ds((2 * other + i) * SLOT + v * 8, 8), :] for i in range(2)]
            parts.append(jnp.where(side == 0, slots[0], slots[1]))
        runs.append(jnp.concatenate(parts, axis=0))
    states = product(gather_ref[run], six_below(jnp.concatenate(runs, axis=1), 256))
    pairs = [runs_ref[pl.ds(side * SLOT + 16 + i, RUNS, stride=2 * SLOT), :] for i in range(2)]
    runs = jnp.concatenate([turn(pair, shift) for pair in pairs for shift in (0, 64)], axis=0)
    states_ninth = product(gather_ninth_ref[run], six_below(runs, LANES))
    bases, locals_ = [], []
    for which in range(2):
        base, local = mapped(
            jnp.concatenate([spread_first_ref[...], local_first_ref[run, which]], axis=0),
            jnp.concatenate([spread_second_ref[...], local_second_ref[run, which]], axis=0),
            blocks_of(in_ref, which),
        )
        bases.append(base)
        locals_.append(local)
    ninth, local = mapped(
        jnp.concatenate([ninth_first_ref[...], local_ninth_first_ref[run]], axis=0),
        jnp.concatenate([ninth_second_ref[...], local_ninth_second_ref[run]], axis=0),
        ninth_of(in_ref),
    )
    states = jnp.concatenate([states + (locals_[0] + locals_[1]), states_ninth + local], axis=1)
    states = six_below(states, LANES)
    added = product(inject_ref[...], states[:, : 2 * LANES])
    ninth = ninth + product(inject_ninth_ref[...], states[:, 2 * LANES :])
    for which in range(2):
        for j in range(GROUP):
            row = which * GROUP * 8 + j * 8
            borders = bases[which][j * 8 : j * 8 + 8] + added[row : row + 8]
            for v in range(2):
                out_ref[pl.ds((2 * j + which) * SLOT + v * 8, 8), :] = borders[:, v * LANES : (v + 1) * LANES]
        out_ref[pl.ds(which * SLOT + 18, GROUP, stride=2 * SLOT), :] = flux
    block = lanes_of((GROUP, LANES)) // QUARTER
    for which in range(2):
        for half in range(2):
            total = jnp.zeros((GROUP, LANES), jnp.float32)
            for a in range(4):
                row = (half * 4 + a) * GROUP
                total = jnp.where(block == a, turn(ninth[row : row + GROUP], QUARTER * (a - which)), total)
            out_ref[pl.ds(which * SLOT + 16 + half, GROUP, stride=2 * SLOT), :] = total


def filter_steps(state, samples):
    _, one, two, three, four = (float(value) for value in plan()["denom"])
    first, second, third, fourth = state
    out = []
    for sample in samples:
        value = sample + first
        out.append(value)
        first = second - one * value
        second = (third - (sample + sample)) - two * value
        third = fourth - three * value
        fourth = sample - four * value
    return out


def band_kernel(
    kept_ref, mask_ref, borders_ref, press_hbm, flux_hbm, press_ref, flux_ref, east_ref, north_ref, states_ref, sems
):
    _, tile, _ = place()
    column = lax.axis_index("col")
    lane = lanes_of()
    for v in range(2):
        for k in range(8):
            parts = [borders_ref[pl.ds(index * SLOT + v * 8 + k, ROWS, stride=4 * SLOT), :] for index in range(4)]
            for a, part in enumerate(shared(parts, lane, -1)):
                states_ref[(4 * v + a) * 8 + k] = part
        for index, quarter in enumerate(QUARTERS):
            parts[quarter] = borders_ref[pl.ds(index * SLOT + 16 + v, ROWS, stride=4 * SLOT), :]
        for a, part in enumerate(transposed(parts, lane)):
            states_ref[64 + 4 * v + a] = part
    copies = []

    def send(source, target):
        copies.append(pltpu.make_async_copy(source, target, sems.at[len(copies)]))
        copies[-1].start()

    row = lax.broadcasted_iota(jnp.int32, (ROWS, LANES), 0)
    half = 0.5 * mask_ref[...].astype(jnp.float32)
    last = lane == LANES - 1
    halos = borders_ref[pl.ds(tile * SLOT + 18, ROWS, stride=4 * SLOT), :]
    halos = jnp.where(lane < 64, halos, pltpu.roll(halos, 4, 0))
    halos = jnp.where(tile == 0, turn(halos, 64), halos)
    outside = ((column == 0) & (lane < 64)) | ((column == 2 * len(PAIRS) - 1) & (lane >= 64))
    halos = jnp.where(outside, 0.0, halos)
    for level in range(4):
        if level < 3:
            for which, target in ((1, press_ref), (0, east_ref), (2, north_ref)):
                s = which * 3 + level
                states = [states_ref[s * 8 + k] for k in range(8)]
                samples = filter_steps(states[:4], [kept_ref[s, hour] for hour in range(HOURS)])
                samples = filter_steps(states[4:], samples[::-1])[::-1]
                for hour in range(HOURS):
                    target[level, hour] = samples[hour]
        else:
            for hour in range(HOURS):
                press_ref[3, hour] = last_level([press_ref[lower, hour] for lower in range(3)])
        send(press_ref.at[level], press_hbm.at[level])
        for hour in range(HOURS):
            press = press_ref[level, hour]
            if level < 3:
                u_here, v_here = east_ref[level, hour], north_ref[level, hour]
            else:
                u_here = last_level([east_ref[lower, hour] for lower in range(3)])
                v_here = last_level([north_ref[lower, hour] for lower in range(3)])
            fx = u_here * press
            fy = v_here * press
            position = level * HOURS + hour
            next_x = jnp.where(last, turn(halos, LANES - 1 - 64 - position), turn(fx, -1))
            prev_x = jnp.where(lane == 0, turn(halos, -position), turn(fx, 1))
            next_y = jnp.where(row == ROWS - 1, 0.0, pltpu.roll(fy, ROWS - 1, 0))
            prev_y = jnp.where(row == 0, 0.0, pltpu.roll(fy, 1, 0))
            flux_ref[level, hour] = half * ((next_x - prev_x) + (next_y - prev_y))
        send(flux_ref.at[level], flux_hbm.at[level])
    for copy in copies:
        copy.wait()


def swap(array, groups):
    return lax.all_to_all(array, ("tm", "col"), 0, 0, tiled=True, axis_index_groups=groups)


VMEM = pl.BlockSpec(memory_space=pltpu.VMEM)
HBM = pl.BlockSpec(memory_space=pltpu.HBM)


def call(kernel, shapes, in_specs, scratch=(), out_spec=VMEM):
    return pl.pallas_call(
        kernel,
        out_shape=[
            jax.ShapeDtypeStruct(shape, jnp.float32) if out_spec is HBM else pltpu.VMEM(shape, jnp.float32)
            for shape in shapes
        ],
        in_specs=in_specs,
        out_specs=[out_spec] * len(shapes),
        scratch_shapes=scratch,
        compiler_params=pltpu.CompilerParams(vmem_limit_bytes=32 * 1024 * 1024),
    )


def on_device(u_vel, v_vel, density, land_mask, start_hour, levels):
    tables = plan()
    whole = (4, HOURS, ROWS, LANES)
    part = (3, HOURS, ROWS, LANES)
    flat = (OWNERS * SLOT, LANES)
    slots = (OWNERS, 1, SLOT * LANES)
    runs = [
        [(z * GROUP + j) * 8 + col for j in range(GROUP) for col in pair] for z in range(RUNS) for pair in PAIRS
    ]
    across = [
        [(z * GROUP + mine) * 8 + col for z in range(RUNS) for mine, col in zip((j, j ^ 8), pair)]
        for j in range(GROUP)
        for pair in FAR
    ]
    state_scratch = pltpu.VMEM((SERIES * 8, ROWS, LANES), jnp.float32)
    arguments = (levels, u_vel, v_vel, density, land_mask, start_hour)
    own, kept = call(
        summary_kernel,
        [flat, (SERIES, HOURS, ROWS, LANES)],
        [HBM] * 6,
        [
            pltpu.SMEM((4,), jnp.int32),
            pltpu.VMEM(whole, jnp.float32),
            pltpu.VMEM(whole, jnp.float32),
            pltpu.VMEM(whole, jnp.float32),
            pltpu.VMEM((ROWS, LANES), jnp.int32),
            pltpu.VMEM((ROWS, LANES), jnp.int32),
            state_scratch,
            pltpu.SemaphoreType.DMA((6,)),
        ],
    )(*[pltpu.with_memory_space_constraint(array, pltpu.HBM) for array in arguments])
    blocks = swap(own.reshape(slots), runs).reshape(flat)
    (totals,) = call(run_kernel, [(2 * RUNS * SLOT, LANES)], [VMEM] * 4)(
        blocks, tables["send"], tables["send_ninth"], tables["edge_sum"]
    )
    totals = swap(totals.reshape(2 * RUNS, 1, SLOT * LANES), across).reshape(2 * RUNS * SLOT, LANES)
    names = (
        "gather",
        "gather_ninth",
        "local_first",
        "local_second",
        "spread_first",
        "spread_second",
        "inject",
        "local_ninth_first",
        "local_ninth_second",
        "ninth_first",
        "ninth_second",
        "inject_ninth",
        "edge_gather",
        "edge_response",
        "edge_inject",
    )
    (borders,) = call(border_kernel, [flat], [VMEM] * (2 + len(names)))(
        blocks, totals, *[tables[name] for name in names]
    )
    borders = swap(borders.reshape(slots), runs).reshape(flat)
    pressure, flux = call(
        band_kernel,
        [whole, whole],
        [VMEM] * 3,
        [
            pltpu.VMEM(whole, jnp.float32),
            pltpu.VMEM(whole, jnp.float32),
            pltpu.VMEM(part, jnp.float32),
            pltpu.VMEM(part, jnp.float32),
            state_scratch,
            pltpu.SemaphoreType.DMA((8,)),
        ],
        out_spec=HBM,
    )(kept, land_mask, borders)
    return (pressure, flux)


def solution(mesh):
    return jax.shard_map(
        on_device,
        mesh=mesh,
        in_specs=(
            P(None, "tm", None, "col"),
            P(None, "tm", None, "col"),
            P(None, "tm", None, "col"),
            P(None, "col"),
            P(None, "col"),
            P(),
        ),
        out_specs=(P(None, "tm", None, "col"), P(None, "tm", None, "col")),
        check_vma=False,
    )
```

```python
import functools
import math

import jax
import jax.numpy as jnp
import ml_dtypes
import numpy as np
from jax import lax
from jax.experimental import pallas as pl
from jax.experimental.pallas import tpu as pltpu
from jax.sharding import PartitionSpec as P

HOURS = 16
GROUP = 16
RUNS = 4
OWNERS = 2 * GROUP
SERIES = 9
ROWS = 8
LANES = 128
QUARTER = 32
SLOT = 19
SPAN = GROUP * HOURS
QUARTERS = (0, 3, 1, 2)
PAIRS = ((0, 1), (2, 3), (4, 5), (6, 7))
MEETINGS = (
    ((1, 2, 0), (5, 6, 0), (0, 4, 8), (3, 7, 8)),
    ((2, 5, 8), (1, 6, 8), (0, 4, 8), (3, 7, 8)),
)
SECOND = tuple(sum(1 << meeting[1] for meeting in meetings) for meetings in MEETINGS)
HIGH = lax.Precision.HIGHEST


def expand_roots(roots):
    coefficients = [complex(1.0, 0.0)]
    for root in roots:
        widened = coefficients + [complex(0.0, 0.0)]
        for position in range(1, len(widened)):
            widened[position] = widened[position] - root * coefficients[position - 1]
        coefficients = widened
    return [coefficient.real for coefficient in coefficients]


def horner_value(coefficients, point):
    running = complex(0.0, 0.0)
    for coefficient in coefficients:
        running = running * point + coefficient
    return running


def derive_coeffs(coefficients):
    degree = len(coefficients) - 1
    return [coefficients[position] * (degree - position) for position in range(degree)]


def filter_design():
    low_edge = 1.0 / 12.9
    high_edge = 1.0 / 12.0
    warped_low = 2.0 * math.tan(math.pi * low_edge)
    warped_high = 2.0 * math.tan(math.pi * high_edge)
    centre = math.sqrt(warped_low * warped_high)
    spread = warped_high - warped_low
    digital = []
    for octant in (3, 5):
        proto = complex(math.cos(octant * math.pi / 4.0), math.sin(octant * math.pi / 4.0)) * spread
        radical = (proto * proto - 4.0 * centre * centre) ** 0.5
        for analog in ((proto + radical) / 2.0, (proto - radical) / 2.0):
            digital.append((2.0 + analog) / (2.0 - analog))
    denom = expand_roots(digital)
    numer = [1.0, 0.0, -2.0, 0.0, 1.0]
    omega = 2.0 * math.atan(centre / 2.0)
    zcentre = complex(math.cos(omega), math.sin(omega))
    respond = horner_value(numer, zcentre) / horner_value(denom, zcentre)
    numer = [coefficient / abs(respond) for coefficient in numer]
    remain = [numer[position] - numer[0] * denom[position] for position in range(1, 5)]
    slope = derive_coeffs(denom)
    amat = np.zeros((4, 4))
    bvec = np.zeros(4)
    cvec = np.zeros(4)
    upper = [pole for pole in digital if pole.imag > 0]
    for index, pole in enumerate(upper):
        resid = horner_value(remain, pole) / horner_value(slope, pole)
        first = 2 * index
        amat[first, first] = pole.real
        amat[first, first + 1] = -pole.imag
        amat[first + 1, first] = pole.imag
        amat[first + 1, first + 1] = pole.real
        bvec[first] = 1.0
        cvec[first] = 2.0 * resid.real
        cvec[first + 1] = -2.0 * resid.imag
    return (amat, bvec, cvec, float(numer[0]))


def power(matrix, exponent):
    return np.linalg.matrix_power(matrix, exponent)


def power(matrix, exponent):
    return np.linalg.matrix_power(matrix, exponent)


def block_maps(hours):
    amat, bvec, cvec, direct = filter_design()
    impulse = [direct] + [float(cvec @ power(amat, step - 1) @ bvec) for step in range(1, hours)]
    toeplitz = np.zeros((hours, hours))
    for row in range(hours):
        for column in range(row + 1):
            toeplitz[row, column] = impulse[row - column]
    powers = [np.eye(4)]
    for hour in range(hours):
        powers.append(powers[-1] @ amat)
    left = np.stack([powers[hours - 1 - hour] @ bvec for hour in range(hours)], axis=1)
    entering = np.stack([cvec @ powers[hour] for hour in range(hours)], axis=0)
    back = np.stack([powers[hour] @ bvec for hour in range(hours)], axis=1)
    summary = np.concatenate([left, back @ toeplitz], axis=0)
    response = toeplitz.T @ toeplitz
    injected = np.concatenate([toeplitz.T @ entering, entering[::-1]], axis=1)
    return summary, back @ entering, powers[hours], response, injected


def direct_form():
    amat, _, cvec, _ = filter_design()
    denom = np.poly(amat)
    outputs = [cvec @ power(amat, hour) for hour in range(4)]
    rows = [sum(denom[lag] * outputs[row - lag] for lag in range(row + 1)) for row in range(4)]
    return denom, np.stack(rows)


def thirds(table):
    rest = table.astype(np.float32)
    out = []
    for _ in range(3):
        part = rest.astype(ml_dtypes.bfloat16)
        out.append(part)
        rest = rest - part.astype(np.float32)
    return out


def along_rows(table):
    high, middle, low = thirds(table)
    first = np.concatenate([np.concatenate([high, high], axis=-1), np.concatenate([middle, middle], axis=-1)], axis=-2)
    return first, np.concatenate([high, low], axis=-1)


def along_depth(table, height):
    high, middle, low = thirds(table)
    parts = np.concatenate([high, high, middle, middle, high, low], axis=-1)
    pad = [(0, 0)] * (parts.ndim - 1) + [(0, height - parts.shape[-1])]
    return np.pad(parts, pad)


@functools.lru_cache(maxsize=None)
def plan():
    gain = filter_design()[3]
    scale = gain * gain
    denom, to_direct = direct_form()
    summary, coupling, step, _, _ = block_maps(HOURS)
    own = GROUP * 8
    forward = np.zeros((GROUP + 1, 4, own + 8))
    forward[0][:, own : own + 4] = np.eye(4)
    for j in range(GROUP):
        forward[j + 1] = step @ forward[j]
        forward[j + 1][:, j * 8 : j * 8 + 4] += np.eye(4)
    backward = np.zeros((GROUP + 1, 4, own + 8))
    backward[GROUP][:, own + 4 :] = np.eye(4)
    for j in reversed(range(GROUP)):
        backward[j] = step @ backward[j + 1] + coupling @ forward[j]
        backward[j][:, j * 8 + 4 : j * 8 + 8] += np.eye(4)
    inner = np.zeros((own, own + 8))
    for j in range(GROUP):
        inner[j * 8 : j * 8 + 4] = gain * to_direct @ forward[j]
        inner[j * 8 + 4 : j * 8 + 8] = to_direct @ backward[j + 1]
    run_left = forward[GROUP][:, :own]
    run_right = backward[0][:, :own]
    run_summary, run_coupling, run_step, response, injected = block_maps(SPAN)
    swapped = [j * 8 + k for k in range(8) for j in range(GROUP)]
    suffix = [np.zeros((4, 4))]
    for m in range(RUNS):
        suffix.append(suffix[-1] + power(run_step, m) @ run_coupling @ power(run_step, m))
    send = np.zeros((RUNS, 16, 2 * own))
    local = np.zeros((RUNS, 16, 2 * own))
    gather = np.zeros((RUNS, 16, RUNS * 8))
    send_ninth = np.zeros((RUNS, 16, own))
    gather_ninth = np.zeros((RUNS, 16, 4 * RUNS))
    local_ninth = np.zeros((RUNS, 16, own))
    edge_gather = np.zeros((RUNS, QUARTER, LANES))
    for z in range(RUNS):
        after = suffix[RUNS - 1 - z]
        right = run_right + run_step @ after @ run_left
        send_ninth[z, 0:4] = run_left[[0, 2, 1, 3]][:, swapped]
        send_ninth[z, 8:12] = right[[0, 2, 1, 3]][:, swapped]
        local_ninth[z, 8:12] = (after @ run_left)[:, swapped]
        for tile in range(2):
            columns = slice(tile * own, (tile + 1) * own)
            ahead = slice(4 * tile, 4 * tile + 4)
            behind = slice(8 + 4 * tile, 12 + 4 * tile)
            send[z, ahead, columns] = run_left
            send[z, behind, columns] = right
            local[z, behind, columns] = after @ run_left
            for other in range(RUNS):
                here = slice(other * 8 + 4 * tile, other * 8 + 4 * tile + 4)
                if other < z:
                    came = power(run_step, z - 1 - other)
                    gather[z, ahead, here] = came
                    gather[z, behind, here] = after @ run_step @ came
                if other > z:
                    gather[z, behind, here] = power(run_step, other - z - 1)
        gather_ninth[z] = gather[z].reshape(16, RUNS, 8)[:, :, :4].swapaxes(1, 2).reshape(16, 4 * RUNS)
        for other in range(RUNS):
            from_left = slice(other * 8, other * 8 + 4)
            from_right = slice(other * 8 + 4, other * 8 + 8)
            if other < z:
                came = power(run_step, z - 1 - other)
                edge_gather[z, from_left, 0:4] = came.T
                edge_gather[z, from_left, 4:8] = (after @ run_step @ came).T
            if other == z:
                edge_gather[z, from_left, 4:8] = after.T
            if other > z:
                came = power(run_step, other - z - 1)
                edge_gather[z, from_right, 4:8] = came.T
                edge_gather[z, from_left, 4:8] = (came @ run_step @ suffix[RUNS - 1 - other]).T
    spread = inner[:, :own]
    inject = np.zeros((2, own, 16))
    for tile in range(2):
        inject[tile, :, 4 * tile : 4 * tile + 4] = inner[:, own : own + 4]
        inject[tile, :, 8 + 4 * tile : 12 + 4 * tile] = inner[:, own + 4 :]
    edge_sum = np.tile(run_summary.T / scale, (1, LANES // 8))
    order = [(j // 8) * 8 + (8 - j % 8) % 8 for j in range(GROUP)]
    places = [order[j] * HOURS + hour for j in range(GROUP) for hour in range(HOURS)]
    edge_response = np.zeros((SPAN, SPAN))
    edge_response[:, places] = response.T / scale
    edge_inject = np.zeros((8, SPAN))
    edge_inject[:, places] = injected.T
    spread_first, spread_second = along_rows(spread)
    local_tiles = [along_rows(local[:, :, tile * own : (tile + 1) * own]) for tile in range(2)]
    ninth_first, ninth_second = along_rows(spread[swapped][:, swapped])
    local_ninth_first, local_ninth_second = along_rows(local_ninth)
    tables = dict(
        send=send.astype(np.float32),
        send_ninth=send_ninth.astype(np.float32),
        edge_sum=edge_sum.astype(np.float32),
        gather=along_depth(gather, 256),
        gather_ninth=along_depth(gather_ninth, LANES),
        local_first=np.stack([tile[0] for tile in local_tiles], axis=1),
        local_second=np.stack([tile[1] for tile in local_tiles], axis=1),
        spread_first=spread_first,
        spread_second=spread_second,
        inject=along_depth(np.concatenate([inject[0], inject[1]]), LANES),
        local_ninth_first=local_ninth_first,
        local_ninth_second=local_ninth_second,
        ninth_first=ninth_first,
        ninth_second=ninth_second,
        inject_ninth=along_depth(inject[0][swapped], LANES),
        edge_gather=along_depth(np.swapaxes(edge_gather, 1, 2), 256).swapaxes(1, 2),
        edge_response=np.stack(thirds(edge_response)),
        edge_inject=along_depth(edge_inject.T, LANES).T,
    )
    return dict(tables, denom=denom, scale=scale, summary=summary / scale)


def place():
    device, column = lax.axis_index("tm"), lax.axis_index("col")
    odd = device % 2
    second = jnp.where(odd == 0, SECOND[0], SECOND[1])
    return device // GROUP, (column + odd) % 2, lax.shift_right_logical(second, column) & 1


def lanes_of(shape=(ROWS, LANES)):
    return lax.broadcasted_iota(jnp.int32, shape, 1)


def live_hours(mask, start, scale):
    first = lax.axis_index("tm") * HOURS
    ocean = mask == 1
    return [jnp.where(ocean & (start <= first + hour), scale, 0.0) for hour in range(HOURS)]


def depths(levels_ref):
    out = []
    for level in range(4):
        number = jnp.full((ROWS, LANES), levels_ref[level], jnp.int32).astype(jnp.float32)
        out.append((number + number * number / 90.0) / 90.0)
    return out


def anomalies(field, live):
    mean = 0.25 * ((field[0] + field[1]) + (field[2] + field[3]))
    return [(field[level] - mean) * live for level in range(3)]


def pressures(rho, depth):
    press = [rho[0] * depth[0]]
    for level in range(1, 4):
        press.append(press[-1] + 0.5 * (rho[level - 1] + rho[level]) * (depth[level] - depth[level - 1]))
    return press


def last_level(values):
    return -((values[0] + values[1]) + values[2])


def turn(value, shift):
    shift = shift % LANES
    return value if shift == 0 else pltpu.roll(value, shift, 1)


def transposed(parts, lane):
    low = lane < 2 * QUARTER
    even = (lane // QUARTER) % 2 == 0
    halves = [None] * 4
    for i in range(2):
        first, second = parts[i], parts[i + 2]
        halves[i] = jnp.where(low, first, turn(second, 64))
        halves[i + 2] = jnp.where(low, turn(first, 64), second)
    out = [None] * 4
    for i in (0, 2):
        first, second = halves[i], halves[i + 1]
        out[i] = jnp.where(even, first, turn(second, QUARTER))
        out[i + 1] = jnp.where(even, turn(first, -QUARTER), second)
    return out


def shared(parts, lane, sign):
    block = lane // QUARTER
    out = []
    for i in range(4):
        total = parts[i]
        for b in range(1, 4):
            total = jnp.where(block == b, parts[(i + sign * b) % 4], total)
        out.append(total)
    return out


def block_transposed(value, lane):
    value = pltpu.roll(value, 0, 1, stride=HOURS, stride_axis=0)
    total = value
    for block in range(1, 8):
        total = jnp.where(lane // HOURS == block, pltpu.roll(value, 8 - block, 0), total)
    return pltpu.roll(total, 0, 1, stride=HOURS, stride_axis=0)


def summary_kernel(
    levels_hbm, u_hbm, v_hbm, rho_hbm, mask_hbm, start_hbm, out_ref, kept_ref, levels_ref, u_ref, v_ref, rho_ref, mask_ref, start_ref, sums_ref, sems
):
    summary, scale = plan()["summary"], float(plan()["scale"])
    copies = [
        pltpu.make_async_copy(source, target, sems.at[index])
        for index, (source, target) in enumerate(
            (
                (mask_hbm, mask_ref),
                (start_hbm, start_ref),
                (levels_hbm, levels_ref),
                (u_hbm, u_ref),
                (rho_hbm, rho_ref),
                (v_hbm, v_ref),
            )
        )
    ]
    for copy in copies:
        copy.start()
    for copy in copies[:3]:
        copy.wait()
    live = live_hours(mask_ref[...], start_ref[...], scale)
    depth = depths(levels_ref)
    lane = lanes_of()
    zeros = jnp.zeros((ROWS, LANES), jnp.float32)
    west, east = zeros, zeros
    for which, ref in enumerate((u_ref, rho_ref, v_ref)):
        copies[3 + which].wait()
        sums = [[None] * 8 for _ in range(3)]
        for hour in range(HOURS):
            field = [ref[level, hour] for level in range(4)]
            if which == 1:
                field = pressures(field, depth)
            values = anomalies(field, live[hour])
            for level, value in enumerate(values):
                kept_ref[which * 3 + level, hour] = value
                for k in range(8):
                    term = float(summary[k, hour]) * value
                    sums[level][k] = term if hour == 0 else sums[level][k] + term
                if which < 2:
                    position = (8 - which * 4 - level) % 8 * HOURS + hour
                    turned = turn(value, position)
                    west = jnp.where(lane == position, turned, west)
                    east = jnp.where(lane == (position - 1) % LANES, turned, east)
        for level in range(3):
            for k in range(8):
                sums_ref[(which * 3 + level) * 8 + k] = sums[level][k]
        if which == 1:
            edges = finished_edges(west, east, lane)
            for index in range(4):
                out_ref[pl.ds(index * SLOT + 18, ROWS, stride=4 * SLOT), :] = edges[(0, 1, 1, 0)[index]]
            lay_out(sums_ref, list(range(4)), out_ref, 0, lane)
    lay_out(sums_ref, list(range(4, 8)), out_ref, 8, lane)
    for v in range(2):
        lay_out_rows([sums_ref[64 + 4 * v + a] for a in range(4)], out_ref, 16 + v, lane)


def finished_edges(west, east, lane):
    block = lane // HOURS
    out = []
    for ends in (west, turn(east, 1)):
        three = -((turn(ends, -HOURS) + turn(ends, -2 * HOURS)) + turn(ends, -3 * HOURS))
        out.append(jnp.where((block == 5) | (block == 1), three, ends))
    return out


def lay_out(sums_ref, series, out_ref, first, lane):
    for k in range(8):
        parts = shared([sums_ref[s * 8 + k] for s in series], lane, 1)
        for index in range(4):
            out_ref[pl.ds(index * SLOT + first + k, ROWS, stride=4 * SLOT), :] = parts[index]


def lay_out_rows(values, out_ref, row, lane):
    parts = transposed(values, lane)
    for index, quarter in enumerate(QUARTERS):
        out_ref[pl.ds(index * SLOT + row, ROWS, stride=4 * SLOT), :] = parts[quarter]


def blocks_of(in_ref, tile):
    return jnp.concatenate(
        [
            jnp.concatenate([in_ref[pl.ds((2 * j + tile) * SLOT + v * 8, 8), :] for j in range(GROUP)], axis=0)
            for v in range(2)
        ],
        axis=1,
    )


def ninth_of(in_ref):
    first = lanes_of((GROUP, LANES)) < QUARTER
    parts = []
    for half in range(2):
        tiles = [in_ref[pl.ds(tile * SLOT + 16 + half, GROUP, stride=2 * SLOT), :] for tile in range(2)]
        for a in range(4):
            parts.append(jnp.where(first, turn(tiles[0], -QUARTER * a), turn(tiles[1], QUARTER - QUARTER * a)))
    return jnp.concatenate(parts, axis=0)


def edge_hours(in_ref, tile):
    lane = lanes_of()
    rows = in_ref[pl.ds(tile * SLOT + 18, GROUP, stride=2 * SLOT), :]
    return jnp.concatenate([block_transposed(rows[half * 8 : half * 8 + 8], lane) for half in range(2)], axis=1)


def dot(lhs, rhs):
    return jnp.dot(lhs, rhs, precision=HIGH, preferred_element_type=jnp.float32)


def run_kernel(in_ref, send_ref, send_ninth_ref, edge_sum_ref, out_ref):
    run, tile, side = place()
    blocks = jnp.concatenate([blocks_of(in_ref, 0), blocks_of(in_ref, 1)], axis=0)
    totals = dot(send_ref[run], blocks)
    ninth = dot(send_ninth_ref[run], ninth_of(in_ref))
    near = edge_hours(in_ref, 1 - tile)
    far = edge_hours(in_ref, tile)
    sums = dot(jnp.concatenate([near, far], axis=0), edge_sum_ref[...])
    lane = lanes_of()
    row = lax.broadcasted_iota(jnp.int32, (ROWS, LANES), 0)

    def packed(value):
        return jnp.where(lane < 64, value, turn(pltpu.roll(value, 6, 0), 64))

    def in_row(value):
        value = jnp.where(lane // 8 == 15 - row, value, 0.0)
        for shift in (4, 2, 1):
            value = value + pltpu.roll(value, shift, 0)
        return value

    left, right = packed(ninth[0:8]), packed(ninth[8:16])
    near_row, far_row = in_row(sums[0:8]), in_row(sums[8:16])
    for other in range(RUNS):
        later = other > run
        rest = jnp.where(row == 2, near_row, jnp.where(later, left, right))
        for slot_side in range(2):
            base = (2 * other + slot_side) * SLOT
            mine = side == slot_side
            for v in range(2):
                lanes = slice(v * LANES, (v + 1) * LANES)
                main = jnp.where(later, totals[0:8, lanes], totals[8:16, lanes])
                out_ref[pl.ds(base + v * 8, 8), :] = jnp.where(mine, main, far[:, lanes])
            out_ref[pl.ds(base + 16, 3), :] = jnp.where(mine, rest, far_row)[0:3]


def split(value):
    high = value.astype(jnp.bfloat16)
    rest = value - high.astype(jnp.float32)
    middle = rest.astype(jnp.bfloat16)
    return high, middle, (rest - middle.astype(jnp.float32)).astype(jnp.bfloat16)


def six_below(value, height):
    high, middle, low = split(value)
    parts = [high, middle, high, middle, low, high]
    rest = height - 6 * value.shape[0]
    if rest:
        parts.append(jnp.zeros((rest, value.shape[1]), jnp.bfloat16))
    return jnp.concatenate(parts, axis=0)


def product(lhs, rhs):
    return jnp.dot(lhs, rhs, preferred_element_type=jnp.float32)


def mapped(first, second, value):
    high, middle, low = split(value)
    upper = product(first, jnp.concatenate([high, middle], axis=0))
    lower = product(second, jnp.concatenate([low, high], axis=0))
    rows = 2 * GROUP * 8
    half = GROUP * 8
    spread = (upper[:half] + upper[half:rows]) + lower[:half]
    local = (upper[rows : rows + 16] + upper[rows + 16 :]) + lower[half:]
    return spread, local


def edge_flux(in_ref, runs_ref, run, tile, side, edge_gather, response_ref, edge_inject):
    lane = lanes_of()
    sums = []
    for which in (side, 1 - side):
        rows = runs_ref[pl.ds(which * SLOT + 18, RUNS, stride=2 * SLOT), :]
        total = jnp.zeros((ROWS, LANES), jnp.float32)
        for other in range(RUNS):
            value = jnp.broadcast_to(rows[other : other + 1], (ROWS, LANES))
            value = pltpu.roll(value, 8 * other + 8, 1, stride=8, stride_axis=0)
            total = jnp.where(lane // 8 == other, value, total)
        sums.append(total)
    high, middle, low = (part.astype(jnp.float32) for part in split(jnp.concatenate(sums, axis=0)))
    first = (high + turn(middle, 32)) + (turn(high, 64) + turn(middle, 96))
    sums = jnp.concatenate([first, low + turn(high, 32)], axis=1)
    states = product(sums.astype(jnp.bfloat16), edge_gather)
    high, middle, low = (part.astype(jnp.float32) for part in split(states))
    states = (high + turn(middle, 8)) + (turn(high, 16) + turn(middle, 24)) + (turn(low, 32) + turn(high, 40))
    near = edge_hours(in_ref, 1 - tile)
    far = jnp.zeros((ROWS, SPAN), jnp.float32)
    for slot in range(2 * RUNS):
        value = jnp.concatenate([runs_ref[pl.ds(slot * SLOT + v * 8, 8), :] for v in range(2)], axis=1)
        far = jnp.where(2 * run + 1 - side == slot, value, far)
    high, middle, low = split(jnp.concatenate([near, far], axis=0))
    one = product(jnp.concatenate([high, middle, low], axis=0), response_ref[0])
    two = product(jnp.concatenate([high, middle], axis=0), response_ref[1])
    three = product(high, response_ref[2])
    banded = (one[0:16] + one[16:32]) + (one[32:48] + two[0:16]) + (two[16:32] + three)
    banded = banded + product(states.astype(jnp.bfloat16), edge_inject)
    row = lax.broadcasted_iota(jnp.int32, (ROWS, SPAN), 0)
    products = [part * pltpu.roll(part, 4, 0) for part in (banded[0:8], banded[8:16])]
    flux = jnp.where(row < 4, products[0], products[1])
    return jnp.concatenate(
        [block_transposed(flux[:, half * LANES : (half + 1) * LANES], lane) for half in range(2)], axis=0
    )


def border_kernel(
    in_ref,
    runs_ref,
    gather_ref,
    gather_ninth_ref,
    local_first_ref,
    local_second_ref,
    spread_first_ref,
    spread_second_ref,
    inject_ref,
    local_ninth_first_ref,
    local_ninth_second_ref,
    ninth_first_ref,
    ninth_second_ref,
    inject_ninth_ref,
    edge_gather_ref,
    edge_response_ref,
    edge_inject_ref,
    out_ref,
):
    run, tile, side = place()
    flux = edge_flux(in_ref, runs_ref, run, tile, side, edge_gather_ref[run], edge_response_ref, edge_inject_ref[...])
    runs = []
    for v in range(2):
        parts = []
        for other in range(RUNS):
            slots = [runs_ref[pl.ds((2 * other + i) * SLOT + v * 8, 8), :] for i in range(2)]
            parts.append(jnp.where(side == 0, slots[0], slots[1]))
        runs.append(jnp.concatenate(parts, axis=0))
    states = product(gather_ref[run], six_below(jnp.concatenate(runs, axis=1), 256))
    pairs = [runs_ref[pl.ds(side * SLOT + 16 + i, RUNS, stride=2 * SLOT), :] for i in range(2)]
    runs = jnp.concatenate([turn(pair, shift) for pair in pairs for shift in (0, 64)], axis=0)
    states_ninth = product(gather_ninth_ref[run], six_below(runs, LANES))
    bases, locals_ = [], []
    for which in range(2):
        base, local = mapped(
            jnp.concatenate([spread_first_ref[...], local_first_ref[run, which]], axis=0),
            jnp.concatenate([spread_second_ref[...], local_second_ref[run, which]], axis=0),
            blocks_of(in_ref, which),
        )
        bases.append(base)
        locals_.append(local)
    ninth, local = mapped(
        jnp.concatenate([ninth_first_ref[...], local_ninth_first_ref[run]], axis=0),
        jnp.concatenate([ninth_second_ref[...], local_ninth_second_ref[run]], axis=0),
        ninth_of(in_ref),
    )
    states = jnp.concatenate([states + (locals_[0] + locals_[1]), states_ninth + local], axis=1)
    states = six_below(states, LANES)
    added = product(inject_ref[...], states[:, : 2 * LANES])
    ninth = ninth + product(inject_ninth_ref[...], states[:, 2 * LANES :])
    for which in range(2):
        for j in range(GROUP):
            row = which * GROUP * 8 + j * 8
            borders = bases[which][j * 8 : j * 8 + 8] + added[row : row + 8]
            for v in range(2):
                out_ref[pl.ds((2 * j + which) * SLOT + v * 8, 8), :] = borders[:, v * LANES : (v + 1) * LANES]
        out_ref[pl.ds(which * SLOT + 18, GROUP, stride=2 * SLOT), :] = flux
    block = lanes_of((GROUP, LANES)) // QUARTER
    for which in range(2):
        for half in range(2):
            total = jnp.zeros((GROUP, LANES), jnp.float32)
            for a in range(4):
                row = (half * 4 + a) * GROUP
                total = jnp.where(block == a, turn(ninth[row : row + GROUP], QUARTER * (a - which)), total)
            out_ref[pl.ds(which * SLOT + 16 + half, GROUP, stride=2 * SLOT), :] = total


def filter_steps(state, samples):
    _, one, two, three, four = (float(value) for value in plan()["denom"])
    first, second, third, fourth = state
    out = []
    for sample in samples:
        value = sample + first
        out.append(value)
        first = second - one * value
        second = (third - (sample + sample)) - two * value
        third = fourth - three * value
        fourth = sample - four * value
    return out


def band_kernel(
    kept_ref, mask_ref, borders_ref, press_hbm, flux_hbm, press_ref, flux_ref, east_ref, north_ref, states_ref, sems
):
    column = lax.axis_index("col")
    tile = column % 2
    lane = lanes_of()
    for v in range(2):
        for k in range(8):
            parts = [borders_ref[pl.ds(index * SLOT + v * 8 + k, ROWS, stride=4 * SLOT), :] for index in range(4)]
            for a, part in enumerate(shared(parts, lane, -1)):
                states_ref[(4 * v + a) * 8 + k] = part
        for index, quarter in enumerate(QUARTERS):
            parts[quarter] = borders_ref[pl.ds(index * SLOT + 16 + v, ROWS, stride=4 * SLOT), :]
        for a, part in enumerate(transposed(parts, lane)):
            states_ref[64 + 4 * v + a] = part
    copies = []

    def send(source, target):
        copies.append(pltpu.make_async_copy(source, target, sems.at[len(copies)]))
        copies[-1].start()

    row = lax.broadcasted_iota(jnp.int32, (ROWS, LANES), 0)
    half = 0.5 * mask_ref[...].astype(jnp.float32)
    last = lane == LANES - 1
    halos = borders_ref[pl.ds(tile * SLOT + 18, ROWS, stride=4 * SLOT), :]
    other = borders_ref[pl.ds((3 - tile) * SLOT + 18, ROWS, stride=4 * SLOT), :]
    half_way = (column == 3) | (column == 4)
    halos = jnp.where(half_way & (lane >= 64), pltpu.roll(other, 4, 0), halos)
    halos = jnp.where(tile == 0, turn(halos, 64), halos)
    outside = ((column == 0) & (lane < 64)) | ((column == 2 * len(PAIRS) - 1) & (lane >= 64))
    halos = jnp.where(outside, 0.0, halos)
    for level in range(4):
        if level < 3:
            for which, target in ((1, press_ref), (0, east_ref), (2, north_ref)):
                s = which * 3 + level
                states = [states_ref[s * 8 + k] for k in range(8)]
                samples = filter_steps(states[:4], [kept_ref[s, hour] for hour in range(HOURS)])
                samples = filter_steps(states[4:], samples[::-1])[::-1]
                for hour in range(HOURS):
                    target[level, hour] = samples[hour]
        else:
            for hour in range(HOURS):
                press_ref[3, hour] = last_level([press_ref[lower, hour] for lower in range(3)])
        send(press_ref.at[level], press_hbm.at[level])
        for hour in range(HOURS):
            press = press_ref[level, hour]
            if level < 3:
                u_here, v_here = east_ref[level, hour], north_ref[level, hour]
            else:
                u_here = last_level([east_ref[lower, hour] for lower in range(3)])
                v_here = last_level([north_ref[lower, hour] for lower in range(3)])
            fx = u_here * press
            fy = v_here * press
            position = level * HOURS + hour
            next_x = jnp.where(last, turn(halos, LANES - 1 - 64 - position), turn(fx, -1))
            prev_x = jnp.where(lane == 0, turn(halos, -position), turn(fx, 1))
            next_y = jnp.where(row == ROWS - 1, 0.0, pltpu.roll(fy, ROWS - 1, 0))
            prev_y = jnp.where(row == 0, 0.0, pltpu.roll(fy, 1, 0))
            flux_ref[level, hour] = half * ((next_x - prev_x) + (next_y - prev_y))
        send(flux_ref.at[level], flux_hbm.at[level])
    for copy in copies:
        copy.wait()


def swap(array, groups):
    return lax.all_to_all(array, ("tm", "col"), 0, 0, tiled=True, axis_index_groups=groups)


VMEM = pl.BlockSpec(memory_space=pltpu.VMEM)
HBM = pl.BlockSpec(memory_space=pltpu.HBM)


def call(kernel, shapes, in_specs, scratch=(), out_spec=VMEM):
    return pl.pallas_call(
        kernel,
        out_shape=[
            jax.ShapeDtypeStruct(shape, jnp.float32) if out_spec is HBM else pltpu.VMEM(shape, jnp.float32)
            for shape in shapes
        ],
        in_specs=in_specs,
        out_specs=[out_spec] * len(shapes),
        scratch_shapes=scratch,
        compiler_params=pltpu.CompilerParams(vmem_limit_bytes=32 * 1024 * 1024),
    )


def on_device(u_vel, v_vel, density, land_mask, start_hour, levels):
    tables = plan()
    whole = (4, HOURS, ROWS, LANES)
    part = (3, HOURS, ROWS, LANES)
    flat = (OWNERS * SLOT, LANES)
    slots = (OWNERS, 1, SLOT * LANES)
    runs = [
        [(z * GROUP + j) * 8 + col for j in range(GROUP) for col in pair] for z in range(RUNS) for pair in PAIRS
    ]
    across = [
        [(z * GROUP + mine) * 8 + col for z in range(RUNS) for mine, col in ((j, first), (j ^ flip, second))]
        for j in range(GROUP)
        for first, second, flip in MEETINGS[j % 2]
    ]
    state_scratch = pltpu.VMEM((SERIES * 8, ROWS, LANES), jnp.float32)
    arguments = (levels, u_vel, v_vel, density, land_mask, start_hour)
    own, kept = call(
        summary_kernel,
        [flat, (SERIES, HOURS, ROWS, LANES)],
        [HBM] * 6,
        [
            pltpu.SMEM((4,), jnp.int32),
            pltpu.VMEM(whole, jnp.float32),
            pltpu.VMEM(whole, jnp.float32),
            pltpu.VMEM(whole, jnp.float32),
            pltpu.VMEM((ROWS, LANES), jnp.int32),
            pltpu.VMEM((ROWS, LANES), jnp.int32),
            state_scratch,
            pltpu.SemaphoreType.DMA((6,)),
        ],
    )(*[pltpu.with_memory_space_constraint(array, pltpu.HBM) for array in arguments])
    blocks = swap(own.reshape(slots), runs).reshape(flat)
    (totals,) = call(run_kernel, [(2 * RUNS * SLOT, LANES)], [VMEM] * 4)(
        blocks, tables["send"], tables["send_ninth"], tables["edge_sum"]
    )
    totals = swap(totals.reshape(2 * RUNS, 1, SLOT * LANES), across).reshape(2 * RUNS * SLOT, LANES)
    names = (
        "gather",
        "gather_ninth",
        "local_first",
        "local_second",
        "spread_first",
        "spread_second",
        "inject",
        "local_ninth_first",
        "local_ninth_second",
        "ninth_first",
        "ninth_second",
        "inject_ninth",
        "edge_gather",
        "edge_response",
        "edge_inject",
    )
    (borders,) = call(border_kernel, [flat], [VMEM] * (2 + len(names)))(
        blocks, totals, *[tables[name] for name in names]
    )
    borders = swap(borders.reshape(slots), runs).reshape(flat)
    pressure, flux = call(
        band_kernel,
        [whole, whole],
        [VMEM] * 3,
        [
            pltpu.VMEM(whole, jnp.float32),
            pltpu.VMEM(whole, jnp.float32),
            pltpu.VMEM(part, jnp.float32),
            pltpu.VMEM(part, jnp.float32),
            state_scratch,
            pltpu.SemaphoreType.DMA((8,)),
        ],
        out_spec=HBM,
    )(kept, land_mask, borders)
    return (pressure, flux)


def solution(mesh):
    return jax.shard_map(
        on_device,
        mesh=mesh,
        in_specs=(
            P(None, "tm", None, "col"),
            P(None, "tm", None, "col"),
            P(None, "tm", None, "col"),
            P(None, "col"),
            P(None, "col"),
            P(),
        ),
        out_specs=(P(None, "tm", None, "col"), P(None, "tm", None, "col")),
        check_vma=False,
    )
```

```python
import functools
import math

import jax
import jax.numpy as jnp
import ml_dtypes
import numpy as np
from jax import lax
from jax.experimental import pallas as pl
from jax.experimental.pallas import tpu as pltpu
from jax.sharding import PartitionSpec as P

HOURS = 16
GROUP = 16
RUNS = 4
OWNERS = 2 * GROUP
SERIES = 9
ROWS = 8
LANES = 128
QUARTER = 32
SLOT = 19
SPAN = GROUP * HOURS
QUARTERS = (0, 3, 1, 2)
PAIRS = ((0, 1), (2, 3), (4, 5), (6, 7))
MEETINGS = (
    ((1, 2, 0), (5, 6, 0), (0, 3, 0), (4, 7, 0)),
    ((2, 5, 8), (3, 7, 8), (0, 1, 0), (4, 6, 0)),
)
SECOND = tuple(sum(1 << meeting[1] for meeting in meetings) for meetings in MEETINGS)
HIGH = lax.Precision.HIGHEST


def expand_roots(roots):
    coefficients = [complex(1.0, 0.0)]
    for root in roots:
        widened = coefficients + [complex(0.0, 0.0)]
        for position in range(1, len(widened)):
            widened[position] = widened[position] - root * coefficients[position - 1]
        coefficients = widened
    return [coefficient.real for coefficient in coefficients]


def horner_value(coefficients, point):
    running = complex(0.0, 0.0)
    for coefficient in coefficients:
        running = running * point + coefficient
    return running


def derive_coeffs(coefficients):
    degree = len(coefficients) - 1
    return [coefficients[position] * (degree - position) for position in range(degree)]


def filter_design():
    low_edge = 1.0 / 12.9
    high_edge = 1.0 / 12.0
    warped_low = 2.0 * math.tan(math.pi * low_edge)
    warped_high = 2.0 * math.tan(math.pi * high_edge)
    centre = math.sqrt(warped_low * warped_high)
    spread = warped_high - warped_low
    digital = []
    for octant in (3, 5):
        proto = complex(math.cos(octant * math.pi / 4.0), math.sin(octant * math.pi / 4.0)) * spread
        radical = (proto * proto - 4.0 * centre * centre) ** 0.5
        for analog in ((proto + radical) / 2.0, (proto - radical) / 2.0):
            digital.append((2.0 + analog) / (2.0 - analog))
    denom = expand_roots(digital)
    numer = [1.0, 0.0, -2.0, 0.0, 1.0]
    omega = 2.0 * math.atan(centre / 2.0)
    zcentre = complex(math.cos(omega), math.sin(omega))
    respond = horner_value(numer, zcentre) / horner_value(denom, zcentre)
    numer = [coefficient / abs(respond) for coefficient in numer]
    remain = [numer[position] - numer[0] * denom[position] for position in range(1, 5)]
    slope = derive_coeffs(denom)
    amat = np.zeros((4, 4))
    bvec = np.zeros(4)
    cvec = np.zeros(4)
    upper = [pole for pole in digital if pole.imag > 0]
    for index, pole in enumerate(upper):
        resid = horner_value(remain, pole) / horner_value(slope, pole)
        first = 2 * index
        amat[first, first] = pole.real
        amat[first, first + 1] = -pole.imag
        amat[first + 1, first] = pole.imag
        amat[first + 1, first + 1] = pole.real
        bvec[first] = 1.0
        cvec[first] = 2.0 * resid.real
        cvec[first + 1] = -2.0 * resid.imag
    return (amat, bvec, cvec, float(numer[0]))


def power(matrix, exponent):
    return np.linalg.matrix_power(matrix, exponent)


def power(matrix, exponent):
    return np.linalg.matrix_power(matrix, exponent)


def block_maps(hours):
    amat, bvec, cvec, direct = filter_design()
    impulse = [direct] + [float(cvec @ power(amat, step - 1) @ bvec) for step in range(1, hours)]
    toeplitz = np.zeros((hours, hours))
    for row in range(hours):
        for column in range(row + 1):
            toeplitz[row, column] = impulse[row - column]
    powers = [np.eye(4)]
    for hour in range(hours):
        powers.append(powers[-1] @ amat)
    left = np.stack([powers[hours - 1 - hour] @ bvec for hour in range(hours)], axis=1)
    entering = np.stack([cvec @ powers[hour] for hour in range(hours)], axis=0)
    back = np.stack([powers[hour] @ bvec for hour in range(hours)], axis=1)
    summary = np.concatenate([left, back @ toeplitz], axis=0)
    response = toeplitz.T @ toeplitz
    injected = np.concatenate([toeplitz.T @ entering, entering[::-1]], axis=1)
    return summary, back @ entering, powers[hours], response, injected


def direct_form():
    amat, _, cvec, _ = filter_design()
    denom = np.poly(amat)
    outputs = [cvec @ power(amat, hour) for hour in range(4)]
    rows = [sum(denom[lag] * outputs[row - lag] for lag in range(row + 1)) for row in range(4)]
    return denom, np.stack(rows)


def thirds(table):
    rest = table.astype(np.float32)
    out = []
    for _ in range(3):
        part = rest.astype(ml_dtypes.bfloat16)
        out.append(part)
        rest = rest - part.astype(np.float32)
    return out


def along_rows(table):
    high, middle, low = thirds(table)
    first = np.concatenate([np.concatenate([high, high], axis=-1), np.concatenate([middle, middle], axis=-1)], axis=-2)
    return first, np.concatenate([high, low], axis=-1)


def along_depth(table, height):
    high, middle, low = thirds(table)
    parts = np.concatenate([high, high, middle, middle, high, low], axis=-1)
    pad = [(0, 0)] * (parts.ndim - 1) + [(0, height - parts.shape[-1])]
    return np.pad(parts, pad)


@functools.lru_cache(maxsize=None)
def plan():
    gain = filter_design()[3]
    scale = gain * gain
    denom, to_direct = direct_form()
    summary, coupling, step, _, _ = block_maps(HOURS)
    own = GROUP * 8
    forward = np.zeros((GROUP + 1, 4, own + 8))
    forward[0][:, own : own + 4] = np.eye(4)
    for j in range(GROUP):
        forward[j + 1] = step @ forward[j]
        forward[j + 1][:, j * 8 : j * 8 + 4] += np.eye(4)
    backward = np.zeros((GROUP + 1, 4, own + 8))
    backward[GROUP][:, own + 4 :] = np.eye(4)
    for j in reversed(range(GROUP)):
        backward[j] = step @ backward[j + 1] + coupling @ forward[j]
        backward[j][:, j * 8 + 4 : j * 8 + 8] += np.eye(4)
    inner = np.zeros((own, own + 8))
    for j in range(GROUP):
        inner[j * 8 : j * 8 + 4] = gain * to_direct @ forward[j]
        inner[j * 8 + 4 : j * 8 + 8] = to_direct @ backward[j + 1]
    run_left = forward[GROUP][:, :own]
    run_right = backward[0][:, :own]
    run_summary, run_coupling, run_step, response, injected = block_maps(SPAN)
    swapped = [j * 8 + k for k in range(8) for j in range(GROUP)]
    suffix = [np.zeros((4, 4))]
    for m in range(RUNS):
        suffix.append(suffix[-1] + power(run_step, m) @ run_coupling @ power(run_step, m))
    send = np.zeros((RUNS, 16, 2 * own))
    local = np.zeros((RUNS, 16, 2 * own))
    gather = np.zeros((RUNS, 16, RUNS * 8))
    send_ninth = np.zeros((RUNS, 16, own))
    gather_ninth = np.zeros((RUNS, 16, 4 * RUNS))
    local_ninth = np.zeros((RUNS, 16, own))
    edge_gather = np.zeros((RUNS, QUARTER, LANES))
    for z in range(RUNS):
        after = suffix[RUNS - 1 - z]
        right = run_right + run_step @ after @ run_left
        send_ninth[z, 0:4] = run_left[[0, 2, 1, 3]][:, swapped]
        send_ninth[z, 8:12] = right[[0, 2, 1, 3]][:, swapped]
        local_ninth[z, 8:12] = (after @ run_left)[:, swapped]
        for tile in range(2):
            columns = slice(tile * own, (tile + 1) * own)
            ahead = slice(4 * tile, 4 * tile + 4)
            behind = slice(8 + 4 * tile, 12 + 4 * tile)
            send[z, ahead, columns] = run_left
            send[z, behind, columns] = right
            local[z, behind, columns] = after @ run_left
            for other in range(RUNS):
                here = slice(other * 8 + 4 * tile, other * 8 + 4 * tile + 4)
                if other < z:
                    came = power(run_step, z - 1 - other)
                    gather[z, ahead, here] = came
                    gather[z, behind, here] = after @ run_step @ came
                if other > z:
                    gather[z, behind, here] = power(run_step, other - z - 1)
        gather_ninth[z] = gather[z].reshape(16, RUNS, 8)[:, :, :4].swapaxes(1, 2).reshape(16, 4 * RUNS)
        for other in range(RUNS):
            from_left = slice(other * 8, other * 8 + 4)
            from_right = slice(other * 8 + 4, other * 8 + 8)
            if other < z:
                came = power(run_step, z - 1 - other)
                edge_gather[z, from_left, 0:4] = came.T
                edge_gather[z, from_left, 4:8] = (after @ run_step @ came).T
            if other == z:
                edge_gather[z, from_left, 4:8] = after.T
            if other > z:
                came = power(run_step, other - z - 1)
                edge_gather[z, from_right, 4:8] = came.T
                edge_gather[z, from_left, 4:8] = (came @ run_step @ suffix[RUNS - 1 - other]).T
    spread = inner[:, :own]
    inject = np.zeros((2, own, 16))
    for tile in range(2):
        inject[tile, :, 4 * tile : 4 * tile + 4] = inner[:, own : own + 4]
        inject[tile, :, 8 + 4 * tile : 12 + 4 * tile] = inner[:, own + 4 :]
    edge_sum = np.tile(run_summary.T / scale, (1, LANES // 8))
    order = [(j // 8) * 8 + (8 - j % 8) % 8 for j in range(GROUP)]
    places = [order[j] * HOURS + hour for j in range(GROUP) for hour in range(HOURS)]
    edge_response = np.zeros((SPAN, SPAN))
    edge_response[:, places] = response.T / scale
    edge_inject = np.zeros((8, SPAN))
    edge_inject[:, places] = injected.T
    spread_first, spread_second = along_rows(spread)
    local_tiles = [along_rows(local[:, :, tile * own : (tile + 1) * own]) for tile in range(2)]
    ninth_first, ninth_second = along_rows(spread[swapped][:, swapped])
    local_ninth_first, local_ninth_second = along_rows(local_ninth)
    tables = dict(
        send=send.astype(np.float32),
        send_ninth=send_ninth.astype(np.float32),
        edge_sum=edge_sum.astype(np.float32),
        gather=along_depth(gather, 256),
        gather_ninth=along_depth(gather_ninth, LANES),
        local_first=np.stack([tile[0] for tile in local_tiles], axis=1),
        local_second=np.stack([tile[1] for tile in local_tiles], axis=1),
        spread_first=spread_first,
        spread_second=spread_second,
        inject=along_depth(np.concatenate([inject[0], inject[1]]), LANES),
        local_ninth_first=local_ninth_first,
        local_ninth_second=local_ninth_second,
        ninth_first=ninth_first,
        ninth_second=ninth_second,
        inject_ninth=along_depth(inject[0][swapped], LANES),
        edge_gather=along_depth(np.swapaxes(edge_gather, 1, 2), 256).swapaxes(1, 2),
        edge_response=np.stack(thirds(edge_response)),
        edge_inject=along_depth(edge_inject.T, LANES).T,
    )
    return dict(tables, denom=denom, scale=scale, summary=summary / scale)


def place():
    device, column = lax.axis_index("tm"), lax.axis_index("col")
    odd = device % 2
    second = jnp.where(odd == 0, SECOND[0], SECOND[1])
    return device // GROUP, (column + odd) % 2, lax.shift_right_logical(second, column) & 1


def lanes_of(shape=(ROWS, LANES)):
    return lax.broadcasted_iota(jnp.int32, shape, 1)


def live_hours(mask, start, scale):
    first = lax.axis_index("tm") * HOURS
    ocean = mask == 1
    return [jnp.where(ocean & (start <= first + hour), scale, 0.0) for hour in range(HOURS)]


def depths(levels_ref):
    out = []
    for level in range(4):
        number = jnp.full((ROWS, LANES), levels_ref[level], jnp.int32).astype(jnp.float32)
        out.append((number + number * number / 90.0) / 90.0)
    return out


def anomalies(field, live):
    mean = 0.25 * ((field[0] + field[1]) + (field[2] + field[3]))
    return [(field[level] - mean) * live for level in range(3)]


def pressures(rho, depth):
    press = [rho[0] * depth[0]]
    for level in range(1, 4):
        press.append(press[-1] + 0.5 * (rho[level - 1] + rho[level]) * (depth[level] - depth[level - 1]))
    return press


def last_level(values):
    return -((values[0] + values[1]) + values[2])


def turn(value, shift):
    shift = shift % LANES
    return value if shift == 0 else pltpu.roll(value, shift, 1)


def transposed(parts, lane):
    low = lane < 2 * QUARTER
    even = (lane // QUARTER) % 2 == 0
    halves = [None] * 4
    for i in range(2):
        first, second = parts[i], parts[i + 2]
        halves[i] = jnp.where(low, first, turn(second, 64))
        halves[i + 2] = jnp.where(low, turn(first, 64), second)
    out = [None] * 4
    for i in (0, 2):
        first, second = halves[i], halves[i + 1]
        out[i] = jnp.where(even, first, turn(second, QUARTER))
        out[i + 1] = jnp.where(even, turn(first, -QUARTER), second)
    return out


def shared(parts, lane, sign):
    block = lane // QUARTER
    out = []
    for i in range(4):
        total = parts[i]
        for b in range(1, 4):
            total = jnp.where(block == b, parts[(i + sign * b) % 4], total)
        out.append(total)
    return out


def block_transposed(value, lane):
    value = pltpu.roll(value, 0, 1, stride=HOURS, stride_axis=0)
    total = value
    for block in range(1, 8):
        total = jnp.where(lane // HOURS == block, pltpu.roll(value, 8 - block, 0), total)
    return pltpu.roll(total, 0, 1, stride=HOURS, stride_axis=0)


def summary_kernel(
    levels_hbm, u_hbm, v_hbm, rho_hbm, mask_hbm, start_hbm, out_ref, kept_ref, levels_ref, u_ref, v_ref, rho_ref, mask_ref, start_ref, sums_ref, sems
):
    summary, scale = plan()["summary"], float(plan()["scale"])
    copies = [
        pltpu.make_async_copy(source, target, sems.at[index])
        for index, (source, target) in enumerate(
            (
                (mask_hbm, mask_ref),
                (start_hbm, start_ref),
                (levels_hbm, levels_ref),
                (u_hbm, u_ref),
                (rho_hbm, rho_ref),
                (v_hbm, v_ref),
            )
        )
    ]
    for copy in copies:
        copy.start()
    for copy in copies[:3]:
        copy.wait()
    live = live_hours(mask_ref[...], start_ref[...], scale)
    depth = depths(levels_ref)
    lane = lanes_of()
    zeros = jnp.zeros((ROWS, LANES), jnp.float32)
    west, east = zeros, zeros
    for which, ref in enumerate((u_ref, rho_ref, v_ref)):
        copies[3 + which].wait()
        sums = [[None] * 8 for _ in range(3)]
        for hour in range(HOURS):
            field = [ref[level, hour] for level in range(4)]
            if which == 1:
                field = pressures(field, depth)
            values = anomalies(field, live[hour])
            for level, value in enumerate(values):
                kept_ref[which * 3 + level, hour] = value
                for k in range(8):
                    term = float(summary[k, hour]) * value
                    sums[level][k] = term if hour == 0 else sums[level][k] + term
                if which < 2:
                    position = (8 - which * 4 - level) % 8 * HOURS + hour
                    turned = turn(value, position)
                    west = jnp.where(lane == position, turned, west)
                    east = jnp.where(lane == (position - 1) % LANES, turned, east)
        for level in range(3):
            for k in range(8):
                sums_ref[(which * 3 + level) * 8 + k] = sums[level][k]
        if which == 1:
            edges = finished_edges(west, east, lane)
            for index in range(4):
                out_ref[pl.ds(index * SLOT + 18, ROWS, stride=4 * SLOT), :] = edges[(0, 1, 1, 0)[index]]
            lay_out(sums_ref, list(range(4)), out_ref, 0, lane)
    lay_out(sums_ref, list(range(4, 8)), out_ref, 8, lane)
    for v in range(2):
        lay_out_rows([sums_ref[64 + 4 * v + a] for a in range(4)], out_ref, 16 + v, lane)


def finished_edges(west, east, lane):
    block = lane // HOURS
    out = []
    for ends in (west, turn(east, 1)):
        three = -((turn(ends, -HOURS) + turn(ends, -2 * HOURS)) + turn(ends, -3 * HOURS))
        out.append(jnp.where((block == 5) | (block == 1), three, ends))
    return out


def lay_out(sums_ref, series, out_ref, first, lane):
    for k in range(8):
        parts = shared([sums_ref[s * 8 + k] for s in series], lane, 1)
        for index in range(4):
            out_ref[pl.ds(index * SLOT + first + k, ROWS, stride=4 * SLOT), :] = parts[index]


def lay_out_rows(values, out_ref, row, lane):
    parts = transposed(values, lane)
    for index, quarter in enumerate(QUARTERS):
        out_ref[pl.ds(index * SLOT + row, ROWS, stride=4 * SLOT), :] = parts[quarter]


def blocks_of(in_ref, tile):
    return jnp.concatenate(
        [
            jnp.concatenate([in_ref[pl.ds((2 * j + tile) * SLOT + v * 8, 8), :] for j in range(GROUP)], axis=0)
            for v in range(2)
        ],
        axis=1,
    )


def ninth_of(in_ref):
    first = lanes_of((GROUP, LANES)) < QUARTER
    parts = []
    for half in range(2):
        tiles = [in_ref[pl.ds(tile * SLOT + 16 + half, GROUP, stride=2 * SLOT), :] for tile in range(2)]
        for a in range(4):
            parts.append(jnp.where(first, turn(tiles[0], -QUARTER * a), turn(tiles[1], QUARTER - QUARTER * a)))
    return jnp.concatenate(parts, axis=0)


def edge_hours(in_ref, tile):
    lane = lanes_of()
    rows = in_ref[pl.ds(tile * SLOT + 18, GROUP, stride=2 * SLOT), :]
    return jnp.concatenate([block_transposed(rows[half * 8 : half * 8 + 8], lane) for half in range(2)], axis=1)


def dot(lhs, rhs):
    return jnp.dot(lhs, rhs, precision=HIGH, preferred_element_type=jnp.float32)


def run_kernel(in_ref, send_ref, send_ninth_ref, edge_sum_ref, out_ref):
    run, tile, side = place()
    blocks = jnp.concatenate([blocks_of(in_ref, 0), blocks_of(in_ref, 1)], axis=0)
    totals = dot(send_ref[run], blocks)
    ninth = dot(send_ninth_ref[run], ninth_of(in_ref))
    near = edge_hours(in_ref, 1 - tile)
    far = edge_hours(in_ref, tile)
    sums = dot(jnp.concatenate([near, far], axis=0), edge_sum_ref[...])
    lane = lanes_of()
    row = lax.broadcasted_iota(jnp.int32, (ROWS, LANES), 0)

    def packed(value):
        return jnp.where(lane < 64, value, turn(pltpu.roll(value, 6, 0), 64))

    def in_row(value):
        value = jnp.where(lane // 8 == 15 - row, value, 0.0)
        for shift in (4, 2, 1):
            value = value + pltpu.roll(value, shift, 0)
        return value

    left, right = packed(ninth[0:8]), packed(ninth[8:16])
    near_row, far_row = in_row(sums[0:8]), in_row(sums[8:16])
    for other in range(RUNS):
        later = other > run
        rest = jnp.where(row == 2, near_row, jnp.where(later, left, right))
        for slot_side in range(2):
            base = (2 * other + slot_side) * SLOT
            mine = side == slot_side
            for v in range(2):
                lanes = slice(v * LANES, (v + 1) * LANES)
                main = jnp.where(later, totals[0:8, lanes], totals[8:16, lanes])
                out_ref[pl.ds(base + v * 8, 8), :] = jnp.where(mine, main, far[:, lanes])
            out_ref[pl.ds(base + 16, 3), :] = jnp.where(mine, rest, far_row)[0:3]


def split(value):
    high = value.astype(jnp.bfloat16)
    rest = value - high.astype(jnp.float32)
    middle = rest.astype(jnp.bfloat16)
    return high, middle, (rest - middle.astype(jnp.float32)).astype(jnp.bfloat16)


def six_below(value, height):
    high, middle, low = split(value)
    parts = [high, middle, high, middle, low, high]
    rest = height - 6 * value.shape[0]
    if rest:
        parts.append(jnp.zeros((rest, value.shape[1]), jnp.bfloat16))
    return jnp.concatenate(parts, axis=0)


def product(lhs, rhs):
    return jnp.dot(lhs, rhs, preferred_element_type=jnp.float32)


def mapped(first, second, value):
    high, middle, low = split(value)
    upper = product(first, jnp.concatenate([high, middle], axis=0))
    lower = product(second, jnp.concatenate([low, high], axis=0))
    rows = 2 * GROUP * 8
    half = GROUP * 8
    spread = (upper[:half] + upper[half:rows]) + lower[:half]
    local = (upper[rows : rows + 16] + upper[rows + 16 :]) + lower[half:]
    return spread, local


def edge_flux(in_ref, runs_ref, run, tile, side, edge_gather, response_ref, edge_inject):
    lane = lanes_of()
    sums = []
    for which in (side, 1 - side):
        rows = runs_ref[pl.ds(which * SLOT + 18, RUNS, stride=2 * SLOT), :]
        total = jnp.zeros((ROWS, LANES), jnp.float32)
        for other in range(RUNS):
            value = jnp.broadcast_to(rows[other : other + 1], (ROWS, LANES))
            value = pltpu.roll(value, 8 * other + 8, 1, stride=8, stride_axis=0)
            total = jnp.where(lane // 8 == other, value, total)
        sums.append(total)
    high, middle, low = (part.astype(jnp.float32) for part in split(jnp.concatenate(sums, axis=0)))
    first = (high + turn(middle, 32)) + (turn(high, 64) + turn(middle, 96))
    sums = jnp.concatenate([first, low + turn(high, 32)], axis=1)
    states = product(sums.astype(jnp.bfloat16), edge_gather)
    high, middle, low = (part.astype(jnp.float32) for part in split(states))
    states = (high + turn(middle, 8)) + (turn(high, 16) + turn(middle, 24)) + (turn(low, 32) + turn(high, 40))
    near = edge_hours(in_ref, 1 - tile)
    far = jnp.zeros((ROWS, SPAN), jnp.float32)
    for slot in range(2 * RUNS):
        value = jnp.concatenate([runs_ref[pl.ds(slot * SLOT + v * 8, 8), :] for v in range(2)], axis=1)
        far = jnp.where(2 * run + 1 - side == slot, value, far)
    high, middle, low = split(jnp.concatenate([near, far], axis=0))
    one = product(jnp.concatenate([high, middle, low], axis=0), response_ref[0])
    two = product(jnp.concatenate([high, middle], axis=0), response_ref[1])
    three = product(high, response_ref[2])
    banded = (one[0:16] + one[16:32]) + (one[32:48] + two[0:16]) + (two[16:32] + three)
    banded = banded + product(states.astype(jnp.bfloat16), edge_inject)
    row = lax.broadcasted_iota(jnp.int32, (ROWS, SPAN), 0)
    products = [part * pltpu.roll(part, 4, 0) for part in (banded[0:8], banded[8:16])]
    flux = jnp.where(row < 4, products[0], products[1])
    return jnp.concatenate(
        [block_transposed(flux[:, half * LANES : (half + 1) * LANES], lane) for half in range(2)], axis=0
    )


def border_kernel(
    in_ref,
    runs_ref,
    gather_ref,
    gather_ninth_ref,
    local_first_ref,
    local_second_ref,
    spread_first_ref,
    spread_second_ref,
    inject_ref,
    local_ninth_first_ref,
    local_ninth_second_ref,
    ninth_first_ref,
    ninth_second_ref,
    inject_ninth_ref,
    edge_gather_ref,
    edge_response_ref,
    edge_inject_ref,
    out_ref,
):
    run, tile, side = place()
    flux = edge_flux(in_ref, runs_ref, run, tile, side, edge_gather_ref[run], edge_response_ref, edge_inject_ref[...])
    runs = []
    for v in range(2):
        parts = []
        for other in range(RUNS):
            slots = [runs_ref[pl.ds((2 * other + i) * SLOT + v * 8, 8), :] for i in range(2)]
            parts.append(jnp.where(side == 0, slots[0], slots[1]))
        runs.append(jnp.concatenate(parts, axis=0))
    states = product(gather_ref[run], six_below(jnp.concatenate(runs, axis=1), 256))
    pairs = [runs_ref[pl.ds(side * SLOT + 16 + i, RUNS, stride=2 * SLOT), :] for i in range(2)]
    runs = jnp.concatenate([turn(pair, shift) for pair in pairs for shift in (0, 64)], axis=0)
    states_ninth = product(gather_ninth_ref[run], six_below(runs, LANES))
    bases, locals_ = [], []
    for which in range(2):
        base, local = mapped(
            jnp.concatenate([spread_first_ref[...], local_first_ref[run, which]], axis=0),
            jnp.concatenate([spread_second_ref[...], local_second_ref[run, which]], axis=0),
            blocks_of(in_ref, which),
        )
        bases.append(base)
        locals_.append(local)
    ninth, local = mapped(
        jnp.concatenate([ninth_first_ref[...], local_ninth_first_ref[run]], axis=0),
        jnp.concatenate([ninth_second_ref[...], local_ninth_second_ref[run]], axis=0),
        ninth_of(in_ref),
    )
    states = jnp.concatenate([states + (locals_[0] + locals_[1]), states_ninth + local], axis=1)
    states = six_below(states, LANES)
    added = product(inject_ref[...], states[:, : 2 * LANES])
    ninth = ninth + product(inject_ninth_ref[...], states[:, 2 * LANES :])
    for which in range(2):
        for j in range(GROUP):
            row = which * GROUP * 8 + j * 8
            borders = bases[which][j * 8 : j * 8 + 8] + added[row : row + 8]
            for v in range(2):
                out_ref[pl.ds((2 * j + which) * SLOT + v * 8, 8), :] = borders[:, v * LANES : (v + 1) * LANES]
        out_ref[pl.ds(which * SLOT + 18, GROUP, stride=2 * SLOT), :] = flux
    block = lanes_of((GROUP, LANES)) // QUARTER
    for which in range(2):
        for half in range(2):
            total = jnp.zeros((GROUP, LANES), jnp.float32)
            for a in range(4):
                row = (half * 4 + a) * GROUP
                total = jnp.where(block == a, turn(ninth[row : row + GROUP], QUARTER * (a - which)), total)
            out_ref[pl.ds(which * SLOT + 16 + half, GROUP, stride=2 * SLOT), :] = total


def filter_steps(state, samples):
    _, one, two, three, four = (float(value) for value in plan()["denom"])
    first, second, third, fourth = state
    out = []
    for sample in samples:
        value = sample + first
        out.append(value)
        first = second - one * value
        second = (third - (sample + sample)) - two * value
        third = fourth - three * value
        fourth = sample - four * value
    return out


def band_kernel(
    kept_ref, mask_ref, borders_ref, press_hbm, flux_hbm, press_ref, flux_ref, east_ref, north_ref, states_ref, sems
):
    column = lax.axis_index("col")
    tile = column % 2
    lane = lanes_of()
    for v in range(2):
        for k in range(8):
            parts = [borders_ref[pl.ds(index * SLOT + v * 8 + k, ROWS, stride=4 * SLOT), :] for index in range(4)]
            for a, part in enumerate(shared(parts, lane, -1)):
                states_ref[(4 * v + a) * 8 + k] = part
        for index, quarter in enumerate(QUARTERS):
            parts[quarter] = borders_ref[pl.ds(index * SLOT + 16 + v, ROWS, stride=4 * SLOT), :]
        for a, part in enumerate(transposed(parts, lane)):
            states_ref[64 + 4 * v + a] = part
    copies = []

    def send(source, target):
        copies.append(pltpu.make_async_copy(source, target, sems.at[len(copies)]))
        copies[-1].start()

    row = lax.broadcasted_iota(jnp.int32, (ROWS, LANES), 0)
    half = 0.5 * mask_ref[...].astype(jnp.float32)
    last = lane == LANES - 1
    halos = borders_ref[pl.ds(tile * SLOT + 18, ROWS, stride=4 * SLOT), :]
    other = borders_ref[pl.ds((3 - tile) * SLOT + 18, ROWS, stride=4 * SLOT), :]
    half_way = (column == 3) | (column == 4)
    halos = jnp.where(half_way & (lane >= 64), pltpu.roll(other, 4, 0), halos)
    halos = jnp.where(tile == 0, turn(halos, 64), halos)
    outside = ((column == 0) & (lane < 64)) | ((column == 2 * len(PAIRS) - 1) & (lane >= 64))
    halos = jnp.where(outside, 0.0, halos)
    for level in range(4):
        if level < 3:
            for which, target in ((1, press_ref), (0, east_ref), (2, north_ref)):
                s = which * 3 + level
                states = [states_ref[s * 8 + k] for k in range(8)]
                samples = filter_steps(states[:4], [kept_ref[s, hour] for hour in range(HOURS)])
                samples = filter_steps(states[4:], samples[::-1])[::-1]
                for hour in range(HOURS):
                    target[level, hour] = samples[hour]
        else:
            for hour in range(HOURS):
                press_ref[3, hour] = last_level([press_ref[lower, hour] for lower in range(3)])
        send(press_ref.at[level], press_hbm.at[level])
        for hour in range(HOURS):
            press = press_ref[level, hour]
            if level < 3:
                u_here, v_here = east_ref[level, hour], north_ref[level, hour]
            else:
                u_here = last_level([east_ref[lower, hour] for lower in range(3)])
                v_here = last_level([north_ref[lower, hour] for lower in range(3)])
            fx = u_here * press
            fy = v_here * press
            position = level * HOURS + hour
            next_x = jnp.where(last, turn(halos, LANES - 1 - 64 - position), turn(fx, -1))
            prev_x = jnp.where(lane == 0, turn(halos, -position), turn(fx, 1))
            next_y = jnp.where(row == ROWS - 1, 0.0, pltpu.roll(fy, ROWS - 1, 0))
            prev_y = jnp.where(row == 0, 0.0, pltpu.roll(fy, 1, 0))
            flux_ref[level, hour] = half * ((next_x - prev_x) + (next_y - prev_y))
        send(flux_ref.at[level], flux_hbm.at[level])
    for copy in copies:
        copy.wait()


def swap(array, groups):
    return lax.all_to_all(array, ("tm", "col"), 0, 0, tiled=True, axis_index_groups=groups)


VMEM = pl.BlockSpec(memory_space=pltpu.VMEM)
HBM = pl.BlockSpec(memory_space=pltpu.HBM)


def call(kernel, shapes, in_specs, scratch=(), out_spec=VMEM):
    return pl.pallas_call(
        kernel,
        out_shape=[
            jax.ShapeDtypeStruct(shape, jnp.float32) if out_spec is HBM else pltpu.VMEM(shape, jnp.float32)
            for shape in shapes
        ],
        in_specs=in_specs,
        out_specs=[out_spec] * len(shapes),
        scratch_shapes=scratch,
        compiler_params=pltpu.CompilerParams(vmem_limit_bytes=32 * 1024 * 1024),
    )


def on_device(u_vel, v_vel, density, land_mask, start_hour, levels):
    tables = plan()
    whole = (4, HOURS, ROWS, LANES)
    part = (3, HOURS, ROWS, LANES)
    flat = (OWNERS * SLOT, LANES)
    slots = (OWNERS, 1, SLOT * LANES)
    runs = [
        [(z * GROUP + j) * 8 + col for j in range(GROUP) for col in pair] for z in range(RUNS) for pair in PAIRS
    ]
    across = [
        [(z * GROUP + mine) * 8 + col for z in range(RUNS) for mine, col in ((j, first), (j ^ flip, second))]
        for j in range(GROUP)
        for first, second, flip in MEETINGS[j % 2]
    ]
    state_scratch = pltpu.VMEM((SERIES * 8, ROWS, LANES), jnp.float32)
    arguments = (levels, u_vel, v_vel, density, land_mask, start_hour)
    own, kept = call(
        summary_kernel,
        [flat, (SERIES, HOURS, ROWS, LANES)],
        [HBM] * 6,
        [
            pltpu.SMEM((4,), jnp.int32),
            pltpu.VMEM(whole, jnp.float32),
            pltpu.VMEM(whole, jnp.float32),
            pltpu.VMEM(whole, jnp.float32),
            pltpu.VMEM((ROWS, LANES), jnp.int32),
            pltpu.VMEM((ROWS, LANES), jnp.int32),
            state_scratch,
            pltpu.SemaphoreType.DMA((6,)),
        ],
    )(*[pltpu.with_memory_space_constraint(array, pltpu.HBM) for array in arguments])
    blocks = swap(own.reshape(slots), runs).reshape(flat)
    (totals,) = call(run_kernel, [(2 * RUNS * SLOT, LANES)], [VMEM] * 4)(
        blocks, tables["send"], tables["send_ninth"], tables["edge_sum"]
    )
    totals = swap(totals.reshape(2 * RUNS, 1, SLOT * LANES), across).reshape(2 * RUNS * SLOT, LANES)
    names = (
        "gather",
        "gather_ninth",
        "local_first",
        "local_second",
        "spread_first",
        "spread_second",
        "inject",
        "local_ninth_first",
        "local_ninth_second",
        "ninth_first",
        "ninth_second",
        "inject_ninth",
        "edge_gather",
        "edge_response",
        "edge_inject",
    )
    (borders,) = call(border_kernel, [flat], [VMEM] * (2 + len(names)))(
        blocks, totals, *[tables[name] for name in names]
    )
    borders = swap(borders.reshape(slots), runs).reshape(flat)
    pressure, flux = call(
        band_kernel,
        [whole, whole],
        [VMEM] * 3,
        [
            pltpu.VMEM(whole, jnp.float32),
            pltpu.VMEM(whole, jnp.float32),
            pltpu.VMEM(part, jnp.float32),
            pltpu.VMEM(part, jnp.float32),
            state_scratch,
            pltpu.SemaphoreType.DMA((8,)),
        ],
        out_spec=HBM,
    )(kept, land_mask, borders)
    return (pressure, flux)


def solution(mesh):
    return jax.shard_map(
        on_device,
        mesh=mesh,
        in_specs=(
            P(None, "tm", None, "col"),
            P(None, "tm", None, "col"),
            P(None, "tm", None, "col"),
            P(None, "col"),
            P(None, "col"),
            P(),
        ),
        out_specs=(P(None, "tm", None, "col"), P(None, "tm", None, "col")),
        check_vma=False,
    )
```

```python
import functools
import math

import jax
import jax.numpy as jnp
import ml_dtypes
import numpy as np
from jax import lax
from jax.experimental import pallas as pl
from jax.experimental.pallas import tpu as pltpu
from jax.sharding import PartitionSpec as P

HOURS = 16
GROUP = 16
RUNS = 4
OWNERS = 2 * GROUP
SERIES = 9
ROWS = 8
LANES = 128
QUARTER = 32
SLOT = 19
SPAN = GROUP * HOURS
QUARTERS = (0, 3, 1, 2)
PAIRS = ((0, 1), (2, 3), (4, 5), (6, 7))
MEETINGS = (((1, 2, 0), (5, 6, 0)), ((2, 5, 8),))
SECOND = tuple(sum(1 << meeting[1] for meeting in meetings) for meetings in MEETINGS)
ALONE = tuple(255 - sum((1 << meeting[0]) + (1 << meeting[1]) for meeting in meetings) for meetings in MEETINGS)
HIGH = lax.Precision.HIGHEST


def expand_roots(roots):
    coefficients = [complex(1.0, 0.0)]
    for root in roots:
        widened = coefficients + [complex(0.0, 0.0)]
        for position in range(1, len(widened)):
            widened[position] = widened[position] - root * coefficients[position - 1]
        coefficients = widened
    return [coefficient.real for coefficient in coefficients]


def horner_value(coefficients, point):
    running = complex(0.0, 0.0)
    for coefficient in coefficients:
        running = running * point + coefficient
    return running


def derive_coeffs(coefficients):
    degree = len(coefficients) - 1
    return [coefficients[position] * (degree - position) for position in range(degree)]


def filter_design():
    low_edge = 1.0 / 12.9
    high_edge = 1.0 / 12.0
    warped_low = 2.0 * math.tan(math.pi * low_edge)
    warped_high = 2.0 * math.tan(math.pi * high_edge)
    centre = math.sqrt(warped_low * warped_high)
    spread = warped_high - warped_low
    digital = []
    for octant in (3, 5):
        proto = complex(math.cos(octant * math.pi / 4.0), math.sin(octant * math.pi / 4.0)) * spread
        radical = (proto * proto - 4.0 * centre * centre) ** 0.5
        for analog in ((proto + radical) / 2.0, (proto - radical) / 2.0):
            digital.append((2.0 + analog) / (2.0 - analog))
    denom = expand_roots(digital)
    numer = [1.0, 0.0, -2.0, 0.0, 1.0]
    omega = 2.0 * math.atan(centre / 2.0)
    zcentre = complex(math.cos(omega), math.sin(omega))
    respond = horner_value(numer, zcentre) / horner_value(denom, zcentre)
    numer = [coefficient / abs(respond) for coefficient in numer]
    remain = [numer[position] - numer[0] * denom[position] for position in range(1, 5)]
    slope = derive_coeffs(denom)
    amat = np.zeros((4, 4))
    bvec = np.zeros(4)
    cvec = np.zeros(4)
    upper = [pole for pole in digital if pole.imag > 0]
    for index, pole in enumerate(upper):
        resid = horner_value(remain, pole) / horner_value(slope, pole)
        first = 2 * index
        amat[first, first] = pole.real
        amat[first, first + 1] = -pole.imag
        amat[first + 1, first] = pole.imag
        amat[first + 1, first + 1] = pole.real
        bvec[first] = 1.0
        cvec[first] = 2.0 * resid.real
        cvec[first + 1] = -2.0 * resid.imag
    return (amat, bvec, cvec, float(numer[0]))


def power(matrix, exponent):
    return np.linalg.matrix_power(matrix, exponent)


def power(matrix, exponent):
    return np.linalg.matrix_power(matrix, exponent)


def block_maps(hours):
    amat, bvec, cvec, direct = filter_design()
    impulse = [direct] + [float(cvec @ power(amat, step - 1) @ bvec) for step in range(1, hours)]
    toeplitz = np.zeros((hours, hours))
    for row in range(hours):
        for column in range(row + 1):
            toeplitz[row, column] = impulse[row - column]
    powers = [np.eye(4)]
    for hour in range(hours):
        powers.append(powers[-1] @ amat)
    left = np.stack([powers[hours - 1 - hour] @ bvec for hour in range(hours)], axis=1)
    entering = np.stack([cvec @ powers[hour] for hour in range(hours)], axis=0)
    back = np.stack([powers[hour] @ bvec for hour in range(hours)], axis=1)
    summary = np.concatenate([left, back @ toeplitz], axis=0)
    response = toeplitz.T @ toeplitz
    injected = np.concatenate([toeplitz.T @ entering, entering[::-1]], axis=1)
    return summary, back @ entering, powers[hours], response, injected


def direct_form():
    amat, _, cvec, _ = filter_design()
    denom = np.poly(amat)
    outputs = [cvec @ power(amat, hour) for hour in range(4)]
    rows = [sum(denom[lag] * outputs[row - lag] for lag in range(row + 1)) for row in range(4)]
    return denom, np.stack(rows)


def thirds(table):
    rest = table.astype(np.float32)
    out = []
    for _ in range(3):
        part = rest.astype(ml_dtypes.bfloat16)
        out.append(part)
        rest = rest - part.astype(np.float32)
    return out


def along_rows(table):
    high, middle, low = thirds(table)
    first = np.concatenate([np.concatenate([high, high], axis=-1), np.concatenate([middle, middle], axis=-1)], axis=-2)
    return first, np.concatenate([high, low], axis=-1)


def along_depth(table, height):
    high, middle, low = thirds(table)
    parts = np.concatenate([high, high, middle, middle, high, low], axis=-1)
    pad = [(0, 0)] * (parts.ndim - 1) + [(0, height - parts.shape[-1])]
    return np.pad(parts, pad)


@functools.lru_cache(maxsize=None)
def plan():
    gain = filter_design()[3]
    scale = gain * gain
    denom, to_direct = direct_form()
    summary, coupling, step, _, _ = block_maps(HOURS)
    own = GROUP * 8
    forward = np.zeros((GROUP + 1, 4, own + 8))
    forward[0][:, own : own + 4] = np.eye(4)
    for j in range(GROUP):
        forward[j + 1] = step @ forward[j]
        forward[j + 1][:, j * 8 : j * 8 + 4] += np.eye(4)
    backward = np.zeros((GROUP + 1, 4, own + 8))
    backward[GROUP][:, own + 4 :] = np.eye(4)
    for j in reversed(range(GROUP)):
        backward[j] = step @ backward[j + 1] + coupling @ forward[j]
        backward[j][:, j * 8 + 4 : j * 8 + 8] += np.eye(4)
    inner = np.zeros((own, own + 8))
    for j in range(GROUP):
        inner[j * 8 : j * 8 + 4] = gain * to_direct @ forward[j]
        inner[j * 8 + 4 : j * 8 + 8] = to_direct @ backward[j + 1]
    run_left = forward[GROUP][:, :own]
    run_right = backward[0][:, :own]
    run_summary, run_coupling, run_step, response, injected = block_maps(SPAN)
    swapped = [j * 8 + k for k in range(8) for j in range(GROUP)]
    suffix = [np.zeros((4, 4))]
    for m in range(RUNS):
        suffix.append(suffix[-1] + power(run_step, m) @ run_coupling @ power(run_step, m))
    send = np.zeros((RUNS, 16, 2 * own))
    local = np.zeros((RUNS, 16, 2 * own))
    gather = np.zeros((RUNS, 16, RUNS * 8))
    send_ninth = np.zeros((RUNS, 16, own))
    gather_ninth = np.zeros((RUNS, 16, 4 * RUNS))
    local_ninth = np.zeros((RUNS, 16, own))
    edge_gather = np.zeros((RUNS, QUARTER, LANES))
    for z in range(RUNS):
        after = suffix[RUNS - 1 - z]
        right = run_right + run_step @ after @ run_left
        send_ninth[z, 0:4] = run_left[[0, 2, 1, 3]][:, swapped]
        send_ninth[z, 8:12] = right[[0, 2, 1, 3]][:, swapped]
        local_ninth[z, 8:12] = (after @ run_left)[:, swapped]
        for tile in range(2):
            columns = slice(tile * own, (tile + 1) * own)
            ahead = slice(4 * tile, 4 * tile + 4)
            behind = slice(8 + 4 * tile, 12 + 4 * tile)
            send[z, ahead, columns] = run_left
            send[z, behind, columns] = right
            local[z, behind, columns] = after @ run_left
            for other in range(RUNS):
                here = slice(other * 8 + 4 * tile, other * 8 + 4 * tile + 4)
                if other < z:
                    came = power(run_step, z - 1 - other)
                    gather[z, ahead, here] = came
                    gather[z, behind, here] = after @ run_step @ came
                if other > z:
                    gather[z, behind, here] = power(run_step, other - z - 1)
        gather_ninth[z] = gather[z].reshape(16, RUNS, 8)[:, :, :4].swapaxes(1, 2).reshape(16, 4 * RUNS)
        for other in range(RUNS):
            from_left = slice(other * 8, other * 8 + 4)
            from_right = slice(other * 8 + 4, other * 8 + 8)
            if other < z:
                came = power(run_step, z - 1 - other)
                edge_gather[z, from_left, 0:4] = came.T
                edge_gather[z, from_left, 4:8] = (after @ run_step @ came).T
            if other == z:
                edge_gather[z, from_left, 4:8] = after.T
            if other > z:
                came = power(run_step, other - z - 1)
                edge_gather[z, from_right, 4:8] = came.T
                edge_gather[z, from_left, 4:8] = (came @ run_step @ suffix[RUNS - 1 - other]).T
    spread = inner[:, :own]
    inject = np.zeros((2, own, 16))
    for tile in range(2):
        inject[tile, :, 4 * tile : 4 * tile + 4] = inner[:, own : own + 4]
        inject[tile, :, 8 + 4 * tile : 12 + 4 * tile] = inner[:, own + 4 :]
    edge_sum = np.tile(run_summary.T / scale, (1, LANES // 8))
    order = [(j // 8) * 8 + (8 - j % 8) % 8 for j in range(GROUP)]
    places = [order[j] * HOURS + hour for j in range(GROUP) for hour in range(HOURS)]
    edge_response = np.zeros((SPAN, SPAN))
    edge_response[:, places] = response.T / scale
    edge_inject = np.zeros((8, SPAN))
    edge_inject[:, places] = injected.T
    spread_first, spread_second = along_rows(spread)
    local_tiles = [along_rows(local[:, :, tile * own : (tile + 1) * own]) for tile in range(2)]
    ninth_first, ninth_second = along_rows(spread[swapped][:, swapped])
    local_ninth_first, local_ninth_second = along_rows(local_ninth)
    tables = dict(
        send=send.astype(np.float32),
        send_ninth=send_ninth.astype(np.float32),
        edge_sum=edge_sum.astype(np.float32),
        gather=along_depth(gather, 256),
        gather_ninth=along_depth(gather_ninth, LANES),
        local_first=np.stack([tile[0] for tile in local_tiles], axis=1),
        local_second=np.stack([tile[1] for tile in local_tiles], axis=1),
        spread_first=spread_first,
        spread_second=spread_second,
        inject=along_depth(np.concatenate([inject[0], inject[1]]), LANES),
        local_ninth_first=local_ninth_first,
        local_ninth_second=local_ninth_second,
        ninth_first=ninth_first,
        ninth_second=ninth_second,
        inject_ninth=along_depth(inject[0][swapped], LANES),
        edge_gather=along_depth(np.swapaxes(edge_gather, 1, 2), 256).swapaxes(1, 2),
        edge_response=np.stack(thirds(edge_response)),
        edge_inject=along_depth(edge_inject.T, LANES).T,
    )
    return dict(tables, denom=denom, scale=scale, summary=summary / scale)


def place():
    device, column = lax.axis_index("tm"), lax.axis_index("col")
    odd = device % 2
    second = jnp.where(odd == 0, SECOND[0], SECOND[1])
    alone = jnp.where(odd == 0, ALONE[0], ALONE[1])
    second = lax.shift_right_logical(second, column) & 1
    alone = lax.shift_right_logical(alone, column) & 1
    side = jnp.where(alone == 1, (device // 2) % 2, second)
    return device // GROUP, (column + odd) % 2, side


def lanes_of(shape=(ROWS, LANES)):
    return lax.broadcasted_iota(jnp.int32, shape, 1)


def live_hours(mask, start, scale):
    first = lax.axis_index("tm") * HOURS
    ocean = mask == 1
    return [jnp.where(ocean & (start <= first + hour), scale, 0.0) for hour in range(HOURS)]


def depths(levels_ref):
    out = []
    for level in range(4):
        number = jnp.full((ROWS, LANES), levels_ref[level], jnp.int32).astype(jnp.float32)
        out.append((number + number * number / 90.0) / 90.0)
    return out


def anomalies(field, live):
    mean = 0.25 * ((field[0] + field[1]) + (field[2] + field[3]))
    return [(field[level] - mean) * live for level in range(3)]


def pressures(rho, depth):
    press = [rho[0] * depth[0]]
    for level in range(1, 4):
        press.append(press[-1] + 0.5 * (rho[level - 1] + rho[level]) * (depth[level] - depth[level - 1]))
    return press


def last_level(values):
    return -((values[0] + values[1]) + values[2])


def turn(value, shift):
    shift = shift % LANES
    return value if shift == 0 else pltpu.roll(value, shift, 1)


def transposed(parts, lane):
    low = lane < 2 * QUARTER
    even = (lane // QUARTER) % 2 == 0
    halves = [None] * 4
    for i in range(2):
        first, second = parts[i], parts[i + 2]
        halves[i] = jnp.where(low, first, turn(second, 64))
        halves[i + 2] = jnp.where(low, turn(first, 64), second)
    out = [None] * 4
    for i in (0, 2):
        first, second = halves[i], halves[i + 1]
        out[i] = jnp.where(even, first, turn(second, QUARTER))
        out[i + 1] = jnp.where(even, turn(first, -QUARTER), second)
    return out


def shared(parts, lane, sign):
    block = lane // QUARTER
    out = []
    for i in range(4):
        total = parts[i]
        for b in range(1, 4):
            total = jnp.where(block == b, parts[(i + sign * b) % 4], total)
        out.append(total)
    return out


def block_transposed(value, lane):
    value = pltpu.roll(value, 0, 1, stride=HOURS, stride_axis=0)
    total = value
    for block in range(1, 8):
        total = jnp.where(lane // HOURS == block, pltpu.roll(value, 8 - block, 0), total)
    return pltpu.roll(total, 0, 1, stride=HOURS, stride_axis=0)


def summary_kernel(
    levels_hbm, u_hbm, v_hbm, rho_hbm, mask_hbm, start_hbm, out_ref, kept_ref, levels_ref, u_ref, v_ref, rho_ref, mask_ref, start_ref, sums_ref, sems
):
    summary, scale = plan()["summary"], float(plan()["scale"])
    copies = [
        pltpu.make_async_copy(source, target, sems.at[index])
        for index, (source, target) in enumerate(
            (
                (mask_hbm, mask_ref),
                (start_hbm, start_ref),
                (levels_hbm, levels_ref),
                (u_hbm, u_ref),
                (rho_hbm, rho_ref),
                (v_hbm, v_ref),
            )
        )
    ]
    for copy in copies:
        copy.start()
    for copy in copies[:3]:
        copy.wait()
    live = live_hours(mask_ref[...], start_ref[...], scale)
    depth = depths(levels_ref)
    lane = lanes_of()
    zeros = jnp.zeros((ROWS, LANES), jnp.float32)
    west, east = zeros, zeros
    for which, ref in enumerate((u_ref, rho_ref, v_ref)):
        copies[3 + which].wait()
        sums = [[None] * 8 for _ in range(3)]
        for hour in range(HOURS):
            field = [ref[level, hour] for level in range(4)]
            if which == 1:
                field = pressures(field, depth)
            values = anomalies(field, live[hour])
            for level, value in enumerate(values):
                kept_ref[which * 3 + level, hour] = value
                for k in range(8):
                    term = float(summary[k, hour]) * value
                    sums[level][k] = term if hour == 0 else sums[level][k] + term
                if which < 2:
                    position = (8 - which * 4 - level) % 8 * HOURS + hour
                    turned = turn(value, position)
                    west = jnp.where(lane == position, turned, west)
                    east = jnp.where(lane == (position - 1) % LANES, turned, east)
        for level in range(3):
            for k in range(8):
                sums_ref[(which * 3 + level) * 8 + k] = sums[level][k]
        if which == 1:
            edges = finished_edges(west, east, lane)
            for index in range(4):
                out_ref[pl.ds(index * SLOT + 18, ROWS, stride=4 * SLOT), :] = edges[(0, 1, 1, 0)[index]]
            lay_out(sums_ref, list(range(4)), out_ref, 0, lane)
    lay_out(sums_ref, list(range(4, 8)), out_ref, 8, lane)
    for v in range(2):
        lay_out_rows([sums_ref[64 + 4 * v + a] for a in range(4)], out_ref, 16 + v, lane)


def finished_edges(west, east, lane):
    block = lane // HOURS
    out = []
    for ends in (west, turn(east, 1)):
        three = -((turn(ends, -HOURS) + turn(ends, -2 * HOURS)) + turn(ends, -3 * HOURS))
        out.append(jnp.where((block == 5) | (block == 1), three, ends))
    return out


def lay_out(sums_ref, series, out_ref, first, lane):
    for k in range(8):
        parts = shared([sums_ref[s * 8 + k] for s in series], lane, 1)
        for index in range(4):
            out_ref[pl.ds(index * SLOT + first + k, ROWS, stride=4 * SLOT), :] = parts[index]


def lay_out_rows(values, out_ref, row, lane):
    parts = transposed(values, lane)
    for index, quarter in enumerate(QUARTERS):
        out_ref[pl.ds(index * SLOT + row, ROWS, stride=4 * SLOT), :] = parts[quarter]


def blocks_of(in_ref, tile):
    return jnp.concatenate(
        [
            jnp.concatenate([in_ref[pl.ds((2 * j + tile) * SLOT + v * 8, 8), :] for j in range(GROUP)], axis=0)
            for v in range(2)
        ],
        axis=1,
    )


def ninth_of(in_ref):
    first = lanes_of((GROUP, LANES)) < QUARTER
    parts = []
    for half in range(2):
        tiles = [in_ref[pl.ds(tile * SLOT + 16 + half, GROUP, stride=2 * SLOT), :] for tile in range(2)]
        for a in range(4):
            parts.append(jnp.where(first, turn(tiles[0], -QUARTER * a), turn(tiles[1], QUARTER - QUARTER * a)))
    return jnp.concatenate(parts, axis=0)


def edge_hours(in_ref, tile):
    lane = lanes_of()
    rows = in_ref[pl.ds(tile * SLOT + 18, GROUP, stride=2 * SLOT), :]
    return jnp.concatenate([block_transposed(rows[half * 8 : half * 8 + 8], lane) for half in range(2)], axis=1)


def dot(lhs, rhs):
    return jnp.dot(lhs, rhs, precision=HIGH, preferred_element_type=jnp.float32)


def run_kernel(in_ref, send_ref, send_ninth_ref, edge_sum_ref, out_ref):
    run, tile, side = place()
    blocks = jnp.concatenate([blocks_of(in_ref, 0), blocks_of(in_ref, 1)], axis=0)
    totals = dot(send_ref[run], blocks)
    ninth = dot(send_ninth_ref[run], ninth_of(in_ref))
    near = edge_hours(in_ref, 1 - tile)
    far = edge_hours(in_ref, tile)
    sums = dot(jnp.concatenate([near, far], axis=0), edge_sum_ref[...])
    lane = lanes_of()
    row = lax.broadcasted_iota(jnp.int32, (ROWS, LANES), 0)

    def packed(value):
        return jnp.where(lane < 64, value, turn(pltpu.roll(value, 6, 0), 64))

    def in_row(value):
        value = jnp.where(lane // 8 == 15 - row, value, 0.0)
        for shift in (4, 2, 1):
            value = value + pltpu.roll(value, shift, 0)
        return value

    left, right = packed(ninth[0:8]), packed(ninth[8:16])
    near_row, far_row = in_row(sums[0:8]), in_row(sums[8:16])
    for other in range(RUNS):
        later = other > run
        rest = jnp.where(row == 2, near_row, jnp.where(later, left, right))
        for slot_side in range(2):
            base = (2 * other + slot_side) * SLOT
            mine = side == slot_side
            for v in range(2):
                lanes = slice(v * LANES, (v + 1) * LANES)
                main = jnp.where(later, totals[0:8, lanes], totals[8:16, lanes])
                out_ref[pl.ds(base + v * 8, 8), :] = jnp.where(mine, main, far[:, lanes])
            out_ref[pl.ds(base + 16, 3), :] = jnp.where(mine, rest, far_row)[0:3]


def split(value):
    high = value.astype(jnp.bfloat16)
    rest = value - high.astype(jnp.float32)
    middle = rest.astype(jnp.bfloat16)
    return high, middle, (rest - middle.astype(jnp.float32)).astype(jnp.bfloat16)


def six_below(value, height):
    high, middle, low = split(value)
    parts = [high, middle, high, middle, low, high]
    rest = height - 6 * value.shape[0]
    if rest:
        parts.append(jnp.zeros((rest, value.shape[1]), jnp.bfloat16))
    return jnp.concatenate(parts, axis=0)


def product(lhs, rhs):
    return jnp.dot(lhs, rhs, preferred_element_type=jnp.float32)


def mapped(first, second, value):
    high, middle, low = split(value)
    upper = product(first, jnp.concatenate([high, middle], axis=0))
    lower = product(second, jnp.concatenate([low, high], axis=0))
    rows = 2 * GROUP * 8
    half = GROUP * 8
    spread = (upper[:half] + upper[half:rows]) + lower[:half]
    local = (upper[rows : rows + 16] + upper[rows + 16 :]) + lower[half:]
    return spread, local


def edge_flux(in_ref, runs_ref, run, tile, side, edge_gather, response_ref, edge_inject):
    lane = lanes_of()
    sums = []
    for which in (side, 1 - side):
        rows = runs_ref[pl.ds(which * SLOT + 18, RUNS, stride=2 * SLOT), :]
        total = jnp.zeros((ROWS, LANES), jnp.float32)
        for other in range(RUNS):
            value = jnp.broadcast_to(rows[other : other + 1], (ROWS, LANES))
            value = pltpu.roll(value, 8 * other + 8, 1, stride=8, stride_axis=0)
            total = jnp.where(lane // 8 == other, value, total)
        sums.append(total)
    high, middle, low = (part.astype(jnp.float32) for part in split(jnp.concatenate(sums, axis=0)))
    first = (high + turn(middle, 32)) + (turn(high, 64) + turn(middle, 96))
    sums = jnp.concatenate([first, low + turn(high, 32)], axis=1)
    states = product(sums.astype(jnp.bfloat16), edge_gather)
    high, middle, low = (part.astype(jnp.float32) for part in split(states))
    states = (high + turn(middle, 8)) + (turn(high, 16) + turn(middle, 24)) + (turn(low, 32) + turn(high, 40))
    near = edge_hours(in_ref, 1 - tile)
    far = jnp.zeros((ROWS, SPAN), jnp.float32)
    for slot in range(2 * RUNS):
        value = jnp.concatenate([runs_ref[pl.ds(slot * SLOT + v * 8, 8), :] for v in range(2)], axis=1)
        far = jnp.where(2 * run + 1 - side == slot, value, far)
    high, middle, low = split(jnp.concatenate([near, far], axis=0))
    one = product(jnp.concatenate([high, middle, low], axis=0), response_ref[0])
    two = product(jnp.concatenate([high, middle], axis=0), response_ref[1])
    three = product(high, response_ref[2])
    banded = (one[0:16] + one[16:32]) + (one[32:48] + two[0:16]) + (two[16:32] + three)
    banded = banded + product(states.astype(jnp.bfloat16), edge_inject)
    row = lax.broadcasted_iota(jnp.int32, (ROWS, SPAN), 0)
    products = [part * pltpu.roll(part, 4, 0) for part in (banded[0:8], banded[8:16])]
    flux = jnp.where(row < 4, products[0], products[1])
    return jnp.concatenate(
        [block_transposed(flux[:, half * LANES : (half + 1) * LANES], lane) for half in range(2)], axis=0
    )


def border_kernel(
    in_ref,
    runs_ref,
    gather_ref,
    gather_ninth_ref,
    local_first_ref,
    local_second_ref,
    spread_first_ref,
    spread_second_ref,
    inject_ref,
    local_ninth_first_ref,
    local_ninth_second_ref,
    ninth_first_ref,
    ninth_second_ref,
    inject_ninth_ref,
    edge_gather_ref,
    edge_response_ref,
    edge_inject_ref,
    out_ref,
):
    run, tile, side = place()
    flux = edge_flux(in_ref, runs_ref, run, tile, side, edge_gather_ref[run], edge_response_ref, edge_inject_ref[...])
    runs = []
    for v in range(2):
        parts = []
        for other in range(RUNS):
            slots = [runs_ref[pl.ds((2 * other + i) * SLOT + v * 8, 8), :] for i in range(2)]
            parts.append(jnp.where(side == 0, slots[0], slots[1]))
        runs.append(jnp.concatenate(parts, axis=0))
    states = product(gather_ref[run], six_below(jnp.concatenate(runs, axis=1), 256))
    pairs = [runs_ref[pl.ds(side * SLOT + 16 + i, RUNS, stride=2 * SLOT), :] for i in range(2)]
    runs = jnp.concatenate([turn(pair, shift) for pair in pairs for shift in (0, 64)], axis=0)
    states_ninth = product(gather_ninth_ref[run], six_below(runs, LANES))
    bases, locals_ = [], []
    for which in range(2):
        base, local = mapped(
            jnp.concatenate([spread_first_ref[...], local_first_ref[run, which]], axis=0),
            jnp.concatenate([spread_second_ref[...], local_second_ref[run, which]], axis=0),
            blocks_of(in_ref, which),
        )
        bases.append(base)
        locals_.append(local)
    ninth, local = mapped(
        jnp.concatenate([ninth_first_ref[...], local_ninth_first_ref[run]], axis=0),
        jnp.concatenate([ninth_second_ref[...], local_ninth_second_ref[run]], axis=0),
        ninth_of(in_ref),
    )
    states = jnp.concatenate([states + (locals_[0] + locals_[1]), states_ninth + local], axis=1)
    states = six_below(states, LANES)
    added = product(inject_ref[...], states[:, : 2 * LANES])
    ninth = ninth + product(inject_ninth_ref[...], states[:, 2 * LANES :])
    for which in range(2):
        for j in range(GROUP):
            row = which * GROUP * 8 + j * 8
            borders = bases[which][j * 8 : j * 8 + 8] + added[row : row + 8]
            for v in range(2):
                out_ref[pl.ds((2 * j + which) * SLOT + v * 8, 8), :] = borders[:, v * LANES : (v + 1) * LANES]
        out_ref[pl.ds(which * SLOT + 18, GROUP, stride=2 * SLOT), :] = flux
    block = lanes_of((GROUP, LANES)) // QUARTER
    for which in range(2):
        for half in range(2):
            total = jnp.zeros((GROUP, LANES), jnp.float32)
            for a in range(4):
                row = (half * 4 + a) * GROUP
                total = jnp.where(block == a, turn(ninth[row : row + GROUP], QUARTER * (a - which)), total)
            out_ref[pl.ds(which * SLOT + 16 + half, GROUP, stride=2 * SLOT), :] = total


def filter_steps(state, samples):
    _, one, two, three, four = (float(value) for value in plan()["denom"])
    first, second, third, fourth = state
    out = []
    for sample in samples:
        value = sample + first
        out.append(value)
        first = second - one * value
        second = (third - (sample + sample)) - two * value
        third = fourth - three * value
        fourth = sample - four * value
    return out


def band_kernel(
    kept_ref, mask_ref, borders_ref, press_hbm, flux_hbm, press_ref, flux_ref, east_ref, north_ref, states_ref, sems
):
    column = lax.axis_index("col")
    tile = column % 2
    lane = lanes_of()
    for v in range(2):
        for k in range(8):
            parts = [borders_ref[pl.ds(index * SLOT + v * 8 + k, ROWS, stride=4 * SLOT), :] for index in range(4)]
            for a, part in enumerate(shared(parts, lane, -1)):
                states_ref[(4 * v + a) * 8 + k] = part
        for index, quarter in enumerate(QUARTERS):
            parts[quarter] = borders_ref[pl.ds(index * SLOT + 16 + v, ROWS, stride=4 * SLOT), :]
        for a, part in enumerate(transposed(parts, lane)):
            states_ref[64 + 4 * v + a] = part
    copies = []

    def send(source, target):
        copies.append(pltpu.make_async_copy(source, target, sems.at[len(copies)]))
        copies[-1].start()

    row = lax.broadcasted_iota(jnp.int32, (ROWS, LANES), 0)
    half = 0.5 * mask_ref[...].astype(jnp.float32)
    last = lane == LANES - 1
    halos = borders_ref[pl.ds(tile * SLOT + 18, ROWS, stride=4 * SLOT), :]
    other = borders_ref[pl.ds((3 - tile) * SLOT + 18, ROWS, stride=4 * SLOT), :]
    half_way = (column == 3) | (column == 4)
    halos = jnp.where(half_way & (lane >= 64), pltpu.roll(other, 4, 0), halos)
    halos = jnp.where(tile == 0, turn(halos, 64), halos)
    outside = ((column == 0) & (lane < 64)) | ((column == 2 * len(PAIRS) - 1) & (lane >= 64))
    halos = jnp.where(outside, 0.0, halos)
    for level in range(4):
        if level < 3:
            for which, target in ((1, press_ref), (0, east_ref), (2, north_ref)):
                s = which * 3 + level
                states = [states_ref[s * 8 + k] for k in range(8)]
                samples = filter_steps(states[:4], [kept_ref[s, hour] for hour in range(HOURS)])
                samples = filter_steps(states[4:], samples[::-1])[::-1]
                for hour in range(HOURS):
                    target[level, hour] = samples[hour]
        else:
            for hour in range(HOURS):
                press_ref[3, hour] = last_level([press_ref[lower, hour] for lower in range(3)])
        send(press_ref.at[level], press_hbm.at[level])
        for hour in range(HOURS):
            press = press_ref[level, hour]
            if level < 3:
                u_here, v_here = east_ref[level, hour], north_ref[level, hour]
            else:
                u_here = last_level([east_ref[lower, hour] for lower in range(3)])
                v_here = last_level([north_ref[lower, hour] for lower in range(3)])
            fx = u_here * press
            fy = v_here * press
            position = level * HOURS + hour
            next_x = jnp.where(last, turn(halos, LANES - 1 - 64 - position), turn(fx, -1))
            prev_x = jnp.where(lane == 0, turn(halos, -position), turn(fx, 1))
            next_y = jnp.where(row == ROWS - 1, 0.0, pltpu.roll(fy, ROWS - 1, 0))
            prev_y = jnp.where(row == 0, 0.0, pltpu.roll(fy, 1, 0))
            flux_ref[level, hour] = half * ((next_x - prev_x) + (next_y - prev_y))
        send(flux_ref.at[level], flux_hbm.at[level])
    for copy in copies:
        copy.wait()


def swap(array, groups):
    return lax.all_to_all(array, ("tm", "col"), 0, 0, tiled=True, axis_index_groups=groups)


VMEM = pl.BlockSpec(memory_space=pltpu.VMEM)
HBM = pl.BlockSpec(memory_space=pltpu.HBM)


def call(kernel, shapes, in_specs, scratch=(), out_spec=VMEM):
    return pl.pallas_call(
        kernel,
        out_shape=[
            jax.ShapeDtypeStruct(shape, jnp.float32) if out_spec is HBM else pltpu.VMEM(shape, jnp.float32)
            for shape in shapes
        ],
        in_specs=in_specs,
        out_specs=[out_spec] * len(shapes),
        scratch_shapes=scratch,
        compiler_params=pltpu.CompilerParams(vmem_limit_bytes=32 * 1024 * 1024),
    )


def on_device(u_vel, v_vel, density, land_mask, start_hour, levels):
    tables = plan()
    whole = (4, HOURS, ROWS, LANES)
    part = (3, HOURS, ROWS, LANES)
    flat = (OWNERS * SLOT, LANES)
    slots = (OWNERS, 1, SLOT * LANES)
    runs = [
        [(z * GROUP + j) * 8 + col for j in range(GROUP) for col in pair] for z in range(RUNS) for pair in PAIRS
    ]
    across = [
        [(z * GROUP + mine) * 8 + col for z in range(RUNS) for mine, col in ((j, first), (j ^ flip, second))]
        for j in range(GROUP)
        for first, second, flip in MEETINGS[j % 2]
    ] + [
        [(z * GROUP + i) * 8 + col for z in range(RUNS) for i in (j, j ^ 2)]
        for j in range(GROUP)
        for col in range(8)
        if j & 2 == 0 and ALONE[j % 2] >> col & 1
    ]
    state_scratch = pltpu.VMEM((SERIES * 8, ROWS, LANES), jnp.float32)
    arguments = (levels, u_vel, v_vel, density, land_mask, start_hour)
    own, kept = call(
        summary_kernel,
        [flat, (SERIES, HOURS, ROWS, LANES)],
        [HBM] * 6,
        [
            pltpu.SMEM((4,), jnp.int32),
            pltpu.VMEM(whole, jnp.float32),
            pltpu.VMEM(whole, jnp.float32),
            pltpu.VMEM(whole, jnp.float32),
            pltpu.VMEM((ROWS, LANES), jnp.int32),
            pltpu.VMEM((ROWS, LANES), jnp.int32),
            state_scratch,
            pltpu.SemaphoreType.DMA((6,)),
        ],
    )(*[pltpu.with_memory_space_constraint(array, pltpu.HBM) for array in arguments])
    blocks = swap(own.reshape(slots), runs).reshape(flat)
    (totals,) = call(run_kernel, [(2 * RUNS * SLOT, LANES)], [VMEM] * 4)(
        blocks, tables["send"], tables["send_ninth"], tables["edge_sum"]
    )
    totals = swap(totals.reshape(2 * RUNS, 1, SLOT * LANES), across).reshape(2 * RUNS * SLOT, LANES)
    names = (
        "gather",
        "gather_ninth",
        "local_first",
        "local_second",
        "spread_first",
        "spread_second",
        "inject",
        "local_ninth_first",
        "local_ninth_second",
        "ninth_first",
        "ninth_second",
        "inject_ninth",
        "edge_gather",
        "edge_response",
        "edge_inject",
    )
    (borders,) = call(border_kernel, [flat], [VMEM] * (2 + len(names)))(
        blocks, totals, *[tables[name] for name in names]
    )
    borders = swap(borders.reshape(slots), runs).reshape(flat)
    pressure, flux = call(
        band_kernel,
        [whole, whole],
        [VMEM] * 3,
        [
            pltpu.VMEM(whole, jnp.float32),
            pltpu.VMEM(whole, jnp.float32),
            pltpu.VMEM(part, jnp.float32),
            pltpu.VMEM(part, jnp.float32),
            state_scratch,
            pltpu.SemaphoreType.DMA((8,)),
        ],
        out_spec=HBM,
    )(kept, land_mask, borders)
    return (pressure, flux)


def solution(mesh):
    return jax.shard_map(
        on_device,
        mesh=mesh,
        in_specs=(
            P(None, "tm", None, "col"),
            P(None, "tm", None, "col"),
            P(None, "tm", None, "col"),
            P(None, "col"),
            P(None, "col"),
            P(),
        ),
        out_specs=(P(None, "tm", None, "col"), P(None, "tm", None, "col")),
        check_vma=False,
    )
```
